32 devices in a mesh: dp: 8 (over z, y), tensor: 4 (over x, core).
Axes of the slice: x: 2, y: 2, z: 4, core: 2. Of those that a mesh axis runs over, the one named last changes fastest.
Arguments:
- tokens: bfloat16 [4096, 2048], P(('dp', 'tensor')), may hold values from -6 to 6
- norm_gain: bfloat16 [2048], P('dp'), may hold values from 0.5 to 1.5
- q_weight: bfloat16 [2048, 2048], P('dp', 'tensor'), may hold values from -0.5 to 0.5
- key_matrix: bfloat16 [2048, 512], P('dp', 'tensor'), may hold values from -0.5 to 0.5
- value_matrix: bfloat16 [2048, 512], P('dp', 'tensor'), may hold values from -0.125 to 0.125
- o_weight: bfloat16 [2048, 2048], P('tensor', 'dp'), may hold values from -3 to 3
- mlp_gain: bfloat16 [2048], P('dp'), may hold values from 0.5 to 1.5
- gate_weight: bfloat16 [2048, 8192], P('dp', 'tensor'), may hold values from -0.125 to 0.125
- up_weight: bfloat16 [2048, 8192], P('dp', 'tensor'), may hold values from -0.125 to 0.125
- down_weight: bfloat16 [8192, 2048], P('tensor', 'dp'), may hold values from -0.25 to 0.25
- parents: int32 [16], replicated, may hold values from 0 to 15, as said below
- out_grad: bfloat16 [4096, 2048], P(('dp', 'tensor')), may hold values from -6 to 6
Outputs:
- mixed: bfloat16 [4096, 2048], P(('dp', 'tensor'))
- grad_tokens: bfloat16 [4096, 2048], P(('dp', 'tensor'))
- grad_norm_gain: float32 [2048], P('dp')
- grad_q_weight: float32 [2048, 2048], P('dp', 'tensor')
- grad_k_weight: float32 [2048, 512], P('dp', 'tensor')
- grad_v_weight: float32 [2048, 512], P('dp', 'tensor')
- grad_o_weight: float32 [2048, 2048], P('tensor', 'dp')
- grad_mlp_gain: float32 [2048], P('dp')
- grad_gate_weight: float32 [2048, 8192], P('dp', 'tensor')
- grad_up_weight: float32 [2048, 8192], P('dp', 'tensor')
- grad_down_weight: float32 [8192, 2048], P('tensor', 'dp')
The draws below stay inside these ranges and needn't reach their ends.
Inputs may be any that keep to these rules, and one draw needn't show every extreme that they name: parents[s] is the segment that segment s continues; a root names itself. Segments of 256 tokens form trees: a chain of up to 8 trunk segments, up to 4 branch segments continuing the trunk's last, and up to 2 leaf segments on each branch; from any segment the root is reached in at most 9 steps. Trees are filled in that order and the last one may be cut.
All inputs are finite; a program needn't handle non-finite values.
Results may differ from the reference program's by a relative error of at most 0.025.
Values may be sent and summed in bfloat16 or wider, within the bound.
No kernel may reach another device: no remote copies, remote signals or barrier semaphores. Data moves between devices by JAX's collectives and lax.ppermute only.
A program may use at most 192 MiB of HBM per device.

```python
import jax
import jax.numpy as jnp
from jax import lax

MODEL_WIDTH = 2048
QUERY_HEAD_COUNT = 32
KEY_VALUE_HEADS = 8
HEAD_SIZE = 64
FF = 8192
SEG = 256
TOKENS = 4096
NSEG = 16


def tree_parents(seg_total):
    canonical = jnp.arange(seg_total, dtype=jnp.int32)
    tree_role = canonical % 20
    tree_start = canonical - tree_role
    trunk_end = tree_start + 7
    leaf_branch = tree_start + 8 + (tree_role - 12) // 2
    return jnp.where(tree_role == 0, canonical, jnp.where(tree_role < 8, canonical - 1, jnp.where(tree_role < 12, trunk_end, leaf_branch)))


def place_value(slot_of, where_index, wanted):
    holder = jnp.argmax(slot_of == wanted).astype(jnp.int32)
    current = slot_of[where_index]
    slot_of = jnp.where(jnp.arange(slot_of.shape[0], dtype=jnp.int32) == holder, current, slot_of)
    return slot_of.at[where_index].set(wanted)


def draw_parents(key, part):
    key = jax.random.fold_in(key, 7)
    perm_key, pick_key = jax.random.split(key)
    slot_of = jax.random.permutation(perm_key, NSEG).astype(jnp.int32)
    chosen = jax.random.randint(pick_key, (), 0, max(NSEG // 20, 1), dtype=jnp.int32) * 20
    slot_of = place_value(slot_of, chosen, NSEG - 1)
    slot_of = place_value(slot_of, chosen + 1, 0)
    canonical_parent = tree_parents(NSEG)
    return jnp.zeros((NSEG,), jnp.int32).at[slot_of].set(slot_of[canonical_parent])


def raised(values, stream_key, source, target, shards_of, factor):
    owner, partner = [(jnp.arange(values.shape[dim]) // (values.shape[dim] // shards_of)).reshape([-1 if axis == dim else 1 for axis in range(values.ndim)]) for dim in (source, target)]
    chosen = jax.random.permutation(stream_key, shards_of)[partner]
    strong = (owner == chosen) | (owner == (partner + shards_of // 2) % shards_of)
    return jnp.where(strong, factor * values, values)


def block_scale(stream_key, shape, pieces, smallest, top_value):
    level = 1.0
    for axis_at, blocks in pieces:
        heights = jax.random.uniform(jax.random.fold_in(jax.random.fold_in(stream_key, 6), axis_at), (blocks,), jnp.float32, smallest / len(pieces), top_value / len(pieces))
        level = level * jnp.repeat(jnp.exp(heights), shape[axis_at] // blocks).reshape((-1,) + (1,) * (len(shape) - 1 - axis_at))
    return level


def centred(rng, shape, width, limit, cuts=(), held_as=jnp.bfloat16):
    values = jax.random.normal(rng, shape, jnp.float32) * width
    if len(cuts) > 0:
        values = block_scale(rng, shape, cuts, -0.22, 0.18) * values
    return jnp.clip(values, min=-limit, max=limit).astype(held_as)


def noise_with(own_key, dims, width, bound, pieces, heavy, held_as=jnp.bfloat16):
    drawn = width * jax.random.normal(own_key, dims, jnp.float32)
    if pieces:
        drawn = drawn * block_scale(own_key, dims, pieces, -0.22, 0.18)
    return jnp.clip(raised(drawn, jax.random.fold_in(own_key, 3), *heavy), -bound, bound).astype(held_as)


def setup_inputs(seed: int = 0) -> dict:
    key_of = jax.random.split(jax.random.key(seed), 13)
    return {
        "tokens": centred(key_of[0], (TOKENS, MODEL_WIDTH), 1.0, 6.0, ((0, 32),)),
        "norm_gain": jnp.clip(1.0 + 0.1 * jax.random.normal(key_of[1], (MODEL_WIDTH,), jnp.float32), 0.5, 1.5).astype(jnp.bfloat16),
        "q_weight": centred(key_of[2], (MODEL_WIDTH, QUERY_HEAD_COUNT * HEAD_SIZE), (MODEL_WIDTH // 16) ** -0.5, 0.5, ((0, 8), (1, 4))),
        "key_matrix": centred(key_of[3], (MODEL_WIDTH, KEY_VALUE_HEADS * HEAD_SIZE), (MODEL_WIDTH // 16) ** -0.5, 0.5, ((0, 8), (1, 4))),
        "value_matrix": centred(key_of[4], (MODEL_WIDTH, KEY_VALUE_HEADS * HEAD_SIZE), MODEL_WIDTH ** -0.5, 0.125, ((0, 8), (1, 4))),
        "o_weight": centred(key_of[5], (QUERY_HEAD_COUNT * HEAD_SIZE, MODEL_WIDTH), (max(1, MODEL_WIDTH // 512)) ** -0.5, 3.0, ((0, 4), (1, 8))),
        "mlp_gain": jnp.clip(1.0 + 0.1 * jax.random.normal(key_of[6], (MODEL_WIDTH,), jnp.float32), 0.5, 1.5).astype(jnp.bfloat16),
        "gate_weight": centred(key_of[7], (MODEL_WIDTH, FF), MODEL_WIDTH ** -0.5, 0.125, ((0, 8), (1, 4))),
        "up_weight": centred(key_of[8], (MODEL_WIDTH, FF), MODEL_WIDTH ** -0.5, 0.125, ((0, 8), (1, 4))),
        "down_weight": centred(key_of[9], (FF, MODEL_WIDTH), (FF // 16) ** -0.5, 0.25, ((0, 4), (1, 8))),
        "parents": draw_parents(jax.random.fold_in(key_of[12], 71), 0),
        "out_grad": noise_with(key_of[11], (TOKENS, MODEL_WIDTH), 1.0, 6.0, ((0, 32),), (0, 1, 32, 2.75)),
    }


attn_scale = 0.015625
branch_scale = 0.22
norm_eps = 1e-05
rope_base = 10000000.0
masked_score = -1e+30

@jax.custom_vjp
def lower_precision(v):
    return lax.optimization_barrier(v.astype(jnp.bfloat16)).astype(jnp.float32)

@jax.custom_vjp
def low_back(v):
    return v

def low_keep(v):
    return (lower_precision(v), None)

def low_pass(kept, grad):
    return (grad,)

def back_keep(v):
    return (v, None)

def back_low(kept, grad):
    return (lower_precision(grad),)
lower_precision.defvjp(low_keep, low_pass)
low_back.defvjp(back_keep, back_low)

def matmul(left, right):
    return jnp.dot(left, right, precision=lax.Precision.HIGHEST, preferred_element_type=jnp.float32)

def ancestry(parents):
    seg_total = parents.shape[0]
    seg_ids = jnp.arange(seg_total, dtype=jnp.int32)
    current = seg_ids
    lineage = current[:, None] == seg_ids[None, :]
    for repeat in range(9):
        current = parents[current]
        lineage = lineage | (current[:, None] == seg_ids[None, :])
    depth = lax.optimization_barrier(jnp.sum(lineage.astype(jnp.int32), axis=1)) - 1
    return (lineage, depth)

def rope_tables(position, head_dim):
    half_dim = head_dim // 2
    exponent = jnp.arange(half_dim, dtype=jnp.float32) * (2.0 / head_dim)
    inverse = jnp.power(rope_base, -exponent)
    angles = position.astype(jnp.float32)[:, None] * inverse[None, :]
    return (jnp.cos(angles), jnp.sin(angles))

def rotary_apply(value_rows, cosine_table, sine_table, direction):
    half_dim = value_rows.shape[-1] // 2
    first_half = value_rows[..., :half_dim]
    second = value_rows[..., half_dim:]
    cos_part = cosine_table[:, None, :]
    sin_part = sine_table[:, None, :] * direction
    return jnp.concatenate([first_half * cos_part - second * sin_part, second * cos_part + first_half * sin_part], axis=-1)

def attention(query_rows, key_rows, value_rows, lineage):
    grand_total = query_rows.shape[0]
    row_block = min(grand_total, 256)
    block_count = grand_total // row_block
    grouped_queries = query_rows.reshape(grand_total, KEY_VALUE_HEADS, QUERY_HEAD_COUNT // KEY_VALUE_HEADS, HEAD_SIZE)
    key_head_rows = key_rows.reshape(grand_total, KEY_VALUE_HEADS, HEAD_SIZE)
    value_head_rows = value_rows.reshape(grand_total, KEY_VALUE_HEADS, HEAD_SIZE)
    key_index = jnp.arange(grand_total, dtype=jnp.int32)
    seg_key = key_index // SEG

    def one_block(block_id):
        first_row = block_id * row_block
        query_part = lax.dynamic_slice_in_dim(grouped_queries, first_row, row_block, 0)
        query_index = first_row + jnp.arange(row_block, dtype=jnp.int32)
        seg_query = query_index // SEG
        allowed = lineage[seg_query][:, seg_key] & ((seg_query[:, None] != seg_key[None, :]) | (key_index[None, :] <= query_index[:, None]))
        raw_scores = low_back(jnp.einsum('qhgd,khd->hgqk', query_part, key_head_rows, precision=lax.Precision.HIGHEST))
        scores = jnp.where(allowed[None, None], raw_scores * attn_scale, masked_score)
        weights = lower_precision(jax.nn.softmax(scores, axis=-1))
        return jnp.einsum('hgqk,khd->qhgd', weights, value_head_rows, precision=lax.Precision.HIGHEST)
    outputs = lax.map(jax.checkpoint(one_block), jnp.arange(block_count, dtype=jnp.int32))
    return outputs.reshape(grand_total, QUERY_HEAD_COUNT * HEAD_SIZE)

def reference(tokens, norm_gain, q_weight, key_matrix, value_matrix, o_weight, mlp_gain, gate_weight, up_weight, down_weight, parents, out_grad):
    lineage, depth = ancestry(parents)
    grand_total = tokens.shape[0]
    token_index = jnp.arange(grand_total, dtype=jnp.int32)
    position = depth[token_index // SEG] * SEG + token_index % SEG
    cosine_table, sine_table = rope_tables(position, HEAD_SIZE)

    def layer_forward(inputs, norm_gain, q_weight, key_matrix, value_matrix, o_weight, mlp_gain, gate_weight, up_weight, down_weight):
        inv_one = lax.rsqrt(lax.optimization_barrier(jnp.mean(inputs * inputs, axis=-1, keepdims=True)) + norm_eps)
        hidden_one = lower_precision(inputs * inv_one * norm_gain)
        query_proj = low_back(matmul(hidden_one, q_weight))
        key_projected = low_back(matmul(hidden_one, key_matrix))
        value_rows = lower_precision(low_back(matmul(hidden_one, value_matrix)))
        query_rows = lower_precision(rotary_apply(query_proj.reshape(grand_total, QUERY_HEAD_COUNT, HEAD_SIZE), cosine_table, sine_table, 1.0)).reshape(grand_total, QUERY_HEAD_COUNT * HEAD_SIZE)
        key_rows = lower_precision(rotary_apply(key_projected.reshape(grand_total, KEY_VALUE_HEADS, HEAD_SIZE), cosine_table, sine_table, 1.0)).reshape(grand_total, KEY_VALUE_HEADS * HEAD_SIZE)
        attended = lower_precision(low_back(attention(query_rows, key_rows, value_rows, lineage)))
        middle = inputs + branch_scale * low_back(matmul(attended, o_weight))
        inv_two = lax.rsqrt(lax.optimization_barrier(jnp.mean(middle * middle, axis=-1, keepdims=True)) + norm_eps)
        hidden_two = lower_precision(middle * inv_two * mlp_gain)
        gate_pre = low_back(matmul(hidden_two, gate_weight))
        up_pre = low_back(matmul(hidden_two, up_weight))
        activated = lower_precision(jax.nn.silu(gate_pre) * up_pre)
        return middle + branch_scale * low_back(matmul(activated, down_weight))
    mixed, pullback = jax.vjp(layer_forward, tokens.astype(jnp.float32), norm_gain.astype(jnp.float32), q_weight.astype(jnp.float32), key_matrix.astype(jnp.float32), value_matrix.astype(jnp.float32), o_weight.astype(jnp.float32), mlp_gain.astype(jnp.float32), gate_weight.astype(jnp.float32), up_weight.astype(jnp.float32), down_weight.astype(jnp.float32))
    gradients = pullback(out_grad.astype(jnp.float32))
    return (mixed.astype(jnp.bfloat16), gradients[0].astype(jnp.bfloat16), gradients[1], gradients[2], gradients[3], gradients[4], gradients[5], gradients[6], gradients[7], gradients[8], gradients[9])
```

```python
import jax
import jax.numpy as jnp
from jax import lax
from jax.sharding import PartitionSpec as P

HEAD_SIZE = 64
SEG = 256


attn_scale = 0.015625
branch_scale = 0.22
norm_eps = 1e-05
rope_base = 10000000.0
masked_score = -1e30


def ancestry(parents):
    seg_total = parents.shape[0]
    seg_ids = jnp.arange(seg_total, dtype=jnp.int32)
    current = seg_ids
    lineage = current[:, None] == seg_ids[None, :]
    for repeat in range(9):
        current = parents[current]
        lineage = lineage | (current[:, None] == seg_ids[None, :])
    depth = jnp.sum(lineage.astype(jnp.int32), axis=1) - 1
    return (lineage, depth)


def rope_tables(position, head_dim):
    half_dim = head_dim // 2
    exponent = jnp.arange(half_dim, dtype=jnp.float32) * (2.0 / head_dim)
    inverse = jnp.power(rope_base, -exponent)
    angles = position.astype(jnp.float32)[:, None] * inverse[None, :]
    return (jnp.cos(angles), jnp.sin(angles))


def rotary_apply(value_rows, cosine_table, sine_table, direction):
    half_dim = value_rows.shape[-1] // 2
    first_half = value_rows[..., :half_dim]
    second = value_rows[..., half_dim:]
    cos_part = cosine_table[:, None, :]
    sin_part = sine_table[:, None, :] * direction
    return jnp.concatenate(
        [first_half * cos_part - second * sin_part, second * cos_part + first_half * sin_part],
        axis=-1,
    )


def rotated(value, axis, size, step):
    return lax.ppermute(value, axis, [(i, (i + step) % size) for i in range(size)])


def relative_pieces(value, axis, size):
    return [value] + [rotated(value, axis, size, k) for k in range(1, size)]


def natural_pieces(pieces, axis):
    size = len(pieces)
    place = lax.axis_index(axis)
    return [
        lax.select_n(place, *[pieces[(i - j) % size] for i in range(size)]) for j in range(size)
    ]


def exchanged(value, axis, size, dim):
    place = lax.axis_index(axis)
    width = value.shape[dim] // size
    pieces = []
    for k in range(size):
        target = lax.rem(place + k, size)
        block = lax.dynamic_slice_in_dim(value, target * width, width, dim)
        pieces.append(block if k == 0 else rotated(block, axis, size, k))
    return natural_pieces(pieces, axis)


def summed_pieces(pieces, axis):
    size = len(pieces)
    total = pieces[0].astype(jnp.float32)
    for k in range(1, size):
        sent = rotated(pieces[k].astype(jnp.bfloat16), axis, size, -k)
        total = total + sent.astype(jnp.float32)
    return total


def relative_columns(value, blocks, axis):
    size = lax.axis_size(axis)
    place = lax.axis_index(axis)
    rows = value.shape[0]
    split = value.reshape(rows, blocks, size, -1)
    return jnp.concatenate(
        [
            lax.dynamic_index_in_dim(
                split, lax.rem(place - k + size, size), 2, keepdims=False
            ).reshape(rows, -1)
            for k in range(size)
        ],
        axis=1,
    )


def natural_columns(value, blocks, axis):
    size = lax.axis_size(axis)
    rows = value.shape[0]
    split = value.reshape(rows, size, blocks, -1)
    parts = natural_pieces([split[:, k] for k in range(size)], axis)
    return jnp.stack(parts, axis=2).reshape(rows, -1)


def unchanged(inner_state):
    return inner_state


def local(
    tokens,
    norm_gain,
    q_weight,
    key_matrix,
    value_matrix,
    o_weight,
    mlp_gain,
    gate_weight,
    up_weight,
    down_weight,
    parents,
    out_grad,
):
    z_size, y_size, x_size = (lax.axis_size(name) for name in ("z", "y", "x"))
    tensor_size = x_size * lax.axis_size("c")
    dp_size = z_size * y_size
    local_rows = tokens.shape[0]
    group_rows = local_rows * tensor_size
    total_rows = group_rows * dp_size
    q_local = q_weight.shape[1] // HEAD_SIZE
    kv_local = key_matrix.shape[1] // HEAD_SIZE
    per_group = q_local // kv_local
    kv_cols = kv_local * HEAD_SIZE
    lineage, depth = ancestry(parents)
    group_start = lax.axis_index(("z", "y")) * group_rows
    query_index = group_start + jnp.arange(group_rows, dtype=jnp.int32)
    query_seg = query_index // SEG
    position = depth[query_seg] * SEG + query_index % SEG
    cosine_table, sine_table = rope_tables(position, HEAD_SIZE)
    seg_count = group_rows // SEG
    query_lineage = lax.dynamic_slice_in_dim(lineage, group_start // SEG, seg_count, 0)
    key_block = group_rows * min(dp_size, max(1, 1024 // group_rows))
    block_count = total_rows // key_block
    block_segs = key_block // SEG

    def block_mask(key_start):
        seg_allowed = lax.dynamic_slice_in_dim(query_lineage, key_start // SEG, block_segs, 1)
        widened = jnp.broadcast_to(
            seg_allowed[:, None, :, None], (seg_count, SEG, block_segs, SEG)
        ).reshape(group_rows, key_block)
        key_index = key_start + jnp.arange(key_block, dtype=jnp.int32)
        causal = (query_seg[:, None] != (key_index // SEG)[None, :]) | (
            key_index[None, :] <= query_index[:, None]
        )
        return (widened & causal, jnp.any(seg_allowed))

    def block_scores(query_heads, key_slab, allowed):
        raw_scores = jnp.einsum(
            "qhgd,khd->hgqk", query_heads, key_slab, preferred_element_type=jnp.float32
        )
        return jnp.where(allowed[None, None], raw_scores * attn_scale, masked_score)

    gains = jnp.stack([norm_gain, mlp_gain])
    gain_z = jnp.stack(natural_pieces(relative_pieces(gains, "z", z_size), "z"), 1)
    gain_zy = jnp.stack(natural_pieces(relative_pieces(gain_z, "y", y_size), "y"), 2)
    gain_one, gain_two = gain_zy.reshape(2, -1)
    q_full = lax.all_gather(q_weight, ("z", "y"), axis=0, tiled=True)
    k_full = lax.all_gather(key_matrix, ("z", "y"), axis=0, tiled=True)
    v_full = lax.all_gather(value_matrix, ("z", "y"), axis=0, tiled=True)
    o_full = lax.all_gather(o_weight, ("z", "y"), axis=1, tiled=True)

    def hidden_block(weight, feature_dim):
        own = jnp.concatenate(exchanged(weight, "z", z_size, 1 - feature_dim), axis=feature_dim)
        full = jnp.concatenate(relative_pieces(own, "y", y_size), axis=feature_dim)
        return jnp.concatenate(relative_pieces(full, "x", x_size), axis=1 - feature_dim)

    gate_block = hidden_block(gate_weight, 0)
    up_block = hidden_block(up_weight, 0)
    down_block = hidden_block(down_weight, 1)
    inputs = tokens.astype(jnp.float32)
    inv_one = lax.rsqrt(jnp.mean(inputs * inputs, axis=-1, keepdims=True) + norm_eps)
    normed_one = inputs * inv_one
    hidden_one = (normed_one * gain_one.astype(jnp.float32)).astype(jnp.bfloat16)
    rows_one = lax.all_gather(hidden_one, ("x", "c"), axis=0, tiled=True)
    query_proj = jnp.dot(rows_one, q_full, preferred_element_type=jnp.float32)
    key_projected = jnp.dot(rows_one, k_full, preferred_element_type=jnp.float32)
    value_proj = jnp.dot(rows_one, v_full, preferred_element_type=jnp.float32)
    query_rows = rotary_apply(
        query_proj.reshape(group_rows, q_local, HEAD_SIZE), cosine_table, sine_table, 1.0
    ).astype(jnp.bfloat16)
    key_rows = (
        rotary_apply(
            key_projected.reshape(group_rows, kv_local, HEAD_SIZE), cosine_table, sine_table, 1.0
        )
        .astype(jnp.bfloat16)
        .reshape(group_rows, kv_cols)
    )
    value_rows = value_proj.astype(jnp.bfloat16)
    all_keys, all_values = (
        lax.all_gather(key_rows, ("z", "y"), axis=0, tiled=True),
        lax.all_gather(value_rows, ("z", "y"), axis=0, tiled=True),
    )
    query_heads = query_rows.reshape(group_rows, kv_local, per_group, HEAD_SIZE)

    def lse_turn(block_id, loop_state):
        key_start = block_id * key_block
        allowed, visited = block_mask(key_start)

        def lse_visit_block(inner_state):
            row_max, row_total = inner_state
            key_slab = lax.dynamic_slice_in_dim(all_keys, key_start, key_block, 0).reshape(
                key_block, kv_local, HEAD_SIZE
            )
            scores = block_scores(query_heads, key_slab, allowed)
            new_max = jnp.maximum(row_max, jnp.max(scores, axis=-1))
            exp_terms = jnp.where(allowed[None, None], jnp.exp(scores - new_max[..., None]), 0.0)
            return (new_max, row_total * jnp.exp(row_max - new_max) + jnp.sum(exp_terms, axis=-1))

        return lax.cond(visited, lse_visit_block, unchanged, loop_state)

    stat_shape = (kv_local, per_group, group_rows)
    row_max, row_total = lax.fori_loop(
        0,
        block_count,
        lse_turn,
        (jnp.full(stat_shape, masked_score, jnp.float32), jnp.zeros(stat_shape, jnp.float32)),
    )
    log_total = row_max + jnp.log(row_total)

    def out_turn(block_id, loop_state):
        key_start = block_id * key_block
        allowed, visited = block_mask(key_start)

        def out_visit_block(inner_state):
            key_slab = lax.dynamic_slice_in_dim(all_keys, key_start, key_block, 0).reshape(
                key_block, kv_local, HEAD_SIZE
            )
            value_slab = lax.dynamic_slice_in_dim(all_values, key_start, key_block, 0).reshape(
                key_block, kv_local, HEAD_SIZE
            )
            scores = block_scores(query_heads, key_slab, allowed)
            probabilities = jnp.where(
                allowed[None, None], jnp.exp(scores - log_total[..., None]), 0.0
            ).astype(jnp.bfloat16)
            return inner_state + jnp.einsum(
                "hgqk,khd->hgqd", probabilities, value_slab, preferred_element_type=jnp.float32
            )

        return lax.cond(visited, out_visit_block, unchanged, loop_state)

    attended = lax.fori_loop(
        0,
        block_count,
        out_turn,
        jnp.zeros((kv_local, per_group, group_rows, HEAD_SIZE), jnp.float32),
    )
    attn_low = (
        attended.transpose(2, 0, 1, 3).reshape(group_rows, q_local * HEAD_SIZE).astype(jnp.bfloat16)
    )
    attn_part = jnp.dot(attn_low, o_full, preferred_element_type=jnp.float32)
    attn_mine = lax.psum_scatter(
        attn_part.astype(jnp.bfloat16), ("x", "c"), scatter_dimension=0, tiled=True
    ).astype(jnp.float32)
    middle = inputs + branch_scale * attn_mine
    inv_two = lax.rsqrt(jnp.mean(middle * middle, axis=-1, keepdims=True) + norm_eps)
    normed_two = middle * inv_two
    hidden_two = (normed_two * gain_two.astype(jnp.float32)).astype(jnp.bfloat16)
    rows_two = lax.all_gather(
        relative_columns(hidden_two, z_size, "y"), ("z", "c"), axis=0, tiled=True
    )
    grad_out = out_grad.astype(jnp.float32)
    grad_mlp = (branch_scale * grad_out).astype(jnp.bfloat16)
    grad_mlp_rows = lax.all_gather(
        relative_columns(grad_mlp, z_size, "y"), ("z", "c"), axis=0, tiled=True
    )
    gate_pre = jnp.dot(rows_two, gate_block, preferred_element_type=jnp.float32)
    up_pre = jnp.dot(rows_two, up_block, preferred_element_type=jnp.float32)
    gate_sigmoid = jax.nn.sigmoid(gate_pre)
    activated = (gate_pre * gate_sigmoid * up_pre).astype(jnp.bfloat16)
    grad_hidden = jnp.einsum(
        "td,fd->tf", grad_mlp_rows, down_block, preferred_element_type=jnp.float32
    )
    grad_gate_act = (
        grad_hidden * up_pre * gate_sigmoid * (1.0 + gate_pre * (1.0 - gate_sigmoid))
    ).astype(jnp.bfloat16)
    grad_up_act = (grad_hidden * gate_pre * gate_sigmoid).astype(jnp.bfloat16)
    input_part = jnp.einsum(
        "tf,df->td", grad_gate_act, gate_block, preferred_element_type=jnp.float32
    ) + jnp.einsum("tf,df->td", grad_up_act, up_block, preferred_element_type=jnp.float32)
    grad_rows_two = natural_columns(
        lax.psum_scatter(
            input_part.astype(jnp.bfloat16), ("z", "c"), scatter_dimension=0, tiled=True
        ),
        z_size,
        "y",
    ).astype(jnp.float32)
    mlp_part = jnp.dot(activated, down_block, preferred_element_type=jnp.float32)
    mlp_mine = natural_columns(
        lax.psum_scatter(
            mlp_part.astype(jnp.bfloat16), ("z", "c"), scatter_dimension=0, tiled=True
        ),
        z_size,
        "y",
    ).astype(jnp.float32)
    mixed = (middle + branch_scale * mlp_mine).astype(jnp.bfloat16)

    def owned_block(left, right, feature_dim):
        pieces = []
        for far in range(y_size):
            near = [left, right]
            width = near[feature_dim].shape[1] // y_size
            near[feature_dim] = near[feature_dim][:, far * width : (far + 1) * width]
            pieces.append(jnp.einsum("ta,tb->ab", *near, preferred_element_type=jnp.float32))
        mine = summed_pieces(pieces, "y")
        width = mine.shape[1 - feature_dim] // x_size
        mine = summed_pieces(
            [
                lax.slice_in_dim(mine, far * width, (far + 1) * width, axis=1 - feature_dim)
                for far in range(x_size)
            ],
            "x",
        ).astype(jnp.bfloat16)
        return jnp.concatenate(
            exchanged(mine, "z", z_size, feature_dim), axis=1 - feature_dim
        ).astype(jnp.float32)

    grad_down = owned_block(activated, grad_mlp_rows, 1)
    grad_gate = owned_block(rows_two, grad_gate_act, 0)
    grad_up = owned_block(rows_two, grad_up_act, 0)
    gain_two_part = jnp.sum(grad_rows_two * normed_two, axis=0)
    grad_normed_two = grad_rows_two * gain_two.astype(jnp.float32)
    grad_middle = grad_out + inv_two * (
        grad_normed_two
        - normed_two * jnp.mean(grad_normed_two * normed_two, axis=-1, keepdims=True)
    )
    grad_attn = (branch_scale * grad_middle).astype(jnp.bfloat16)
    grad_attn_rows = lax.all_gather(grad_attn, ("x", "c"), axis=0, tiled=True)
    grad_o = jnp.einsum("tc,td->cd", attn_low, grad_attn_rows, preferred_element_type=jnp.float32)
    grad_heads = (
        jnp.einsum("td,cd->tc", grad_attn_rows, o_full, preferred_element_type=jnp.float32)
        .astype(jnp.bfloat16)
        .reshape(group_rows, kv_local, per_group, HEAD_SIZE)
    )
    delta_rows = jnp.einsum("qhgd,hgqd->hgq", grad_heads.astype(jnp.float32), attended)

    def back_turn(block_id, loop_state):
        key_start = block_id * key_block
        allowed, visited = block_mask(key_start)

        def back_visit_block(inner_state):
            grad_query, grad_kv = inner_state
            key_slab = lax.dynamic_slice_in_dim(all_keys, key_start, key_block, 0).reshape(
                key_block, kv_local, HEAD_SIZE
            )
            value_slab = lax.dynamic_slice_in_dim(all_values, key_start, key_block, 0).reshape(
                key_block, kv_local, HEAD_SIZE
            )
            scores = block_scores(query_heads, key_slab, allowed)
            probabilities = jnp.where(
                allowed[None, None], jnp.exp(scores - log_total[..., None]), 0.0
            )
            grad_probs = jnp.einsum(
                "qhgd,khd->hgqk", grad_heads, value_slab, preferred_element_type=jnp.float32
            )
            grad_scores = (
                probabilities * (grad_probs - delta_rows[..., None]) * attn_scale
            ).astype(jnp.bfloat16)
            grad_query = grad_query + jnp.einsum(
                "hgqk,khd->hgqd", grad_scores, key_slab, preferred_element_type=jnp.float32
            )
            key_part = jnp.einsum(
                "hgqk,qhgd->khd", grad_scores, query_heads, preferred_element_type=jnp.float32
            ).reshape(key_block, kv_cols)
            value_part = jnp.einsum(
                "hgqk,qhgd->khd",
                probabilities.astype(jnp.bfloat16),
                grad_heads,
                preferred_element_type=jnp.float32,
            ).reshape(key_block, kv_cols)
            current = lax.dynamic_slice_in_dim(grad_kv, key_start, key_block, 0)
            grad_kv = lax.dynamic_update_slice_in_dim(
                grad_kv, current + jnp.concatenate([key_part, value_part], axis=1), key_start, 0
            )
            return (grad_query, grad_kv)

        return lax.cond(visited, back_visit_block, unchanged, loop_state)

    grad_query, grad_kv = lax.fori_loop(
        0,
        block_count,
        back_turn,
        (
            jnp.zeros((kv_local, per_group, group_rows, HEAD_SIZE), jnp.float32),
            jnp.zeros((total_rows, 2 * kv_cols), jnp.float32),
        ),
    )
    grad_kv_mine = lax.psum_scatter(
        grad_kv.astype(jnp.bfloat16), ("z", "y"), scatter_dimension=0, tiled=True
    ).astype(jnp.float32)
    grad_keys = (
        rotary_apply(
            grad_kv_mine[:, :kv_cols].reshape(group_rows, kv_local, HEAD_SIZE),
            cosine_table,
            sine_table,
            -1.0,
        )
        .astype(jnp.bfloat16)
        .reshape(group_rows, kv_cols)
    )
    grad_values = grad_kv_mine[:, kv_cols:].astype(jnp.bfloat16)
    grad_queries = (
        rotary_apply(
            grad_query.transpose(2, 0, 1, 3).reshape(group_rows, q_local, HEAD_SIZE),
            cosine_table,
            sine_table,
            -1.0,
        )
        .astype(jnp.bfloat16)
        .reshape(group_rows, q_local * HEAD_SIZE)
    )
    grad_q = jnp.einsum("td,tc->dc", rows_one, grad_queries, preferred_element_type=jnp.float32)
    grad_k = jnp.einsum("td,tc->dc", rows_one, grad_keys, preferred_element_type=jnp.float32)
    grad_v = jnp.einsum("td,tc->dc", rows_one, grad_values, preferred_element_type=jnp.float32)
    input_one = jnp.einsum("tc,dc->td", grad_queries, q_full, preferred_element_type=jnp.float32)
    input_one = input_one + jnp.einsum(
        "tc,dc->td", grad_keys, k_full, preferred_element_type=jnp.float32
    )
    input_one = input_one + jnp.einsum(
        "tc,dc->td", grad_values, v_full, preferred_element_type=jnp.float32
    )
    grad_rows_one = lax.psum_scatter(
        input_one.astype(jnp.bfloat16), ("x", "c"), scatter_dimension=0, tiled=True
    ).astype(jnp.float32)
    gain_one_part = jnp.sum(grad_rows_one * normed_one, axis=0)
    grad_normed_one = grad_rows_one * gain_one.astype(jnp.float32)
    grad_inputs = grad_middle + inv_one * (
        grad_normed_one
        - normed_one * jnp.mean(grad_normed_one * normed_one, axis=-1, keepdims=True)
    )
    summed = (
        lax.psum_scatter(
            jnp.stack([gain_one_part, gain_two_part], 1).astype(jnp.bfloat16),
            ("z", "y"),
            scatter_dimension=0,
            tiled=True,
        ).astype(jnp.float32),
        lax.psum_scatter(
            grad_q.astype(jnp.bfloat16), ("z", "y"), scatter_dimension=0, tiled=True
        ).astype(jnp.float32),
        lax.psum_scatter(
            grad_k.astype(jnp.bfloat16), ("z", "y"), scatter_dimension=0, tiled=True
        ).astype(jnp.float32),
        lax.psum_scatter(
            grad_v.astype(jnp.bfloat16), ("z", "y"), scatter_dimension=0, tiled=True
        ).astype(jnp.float32),
        lax.psum_scatter(
            grad_o.astype(jnp.bfloat16), ("z", "y"), scatter_dimension=1, tiled=True
        ).astype(jnp.float32),
    )
    gain_sums = lax.psum(summed[0], ("x", "c"))
    return (
        mixed,
        grad_inputs.astype(jnp.bfloat16),
        gain_sums[:, 0],
        summed[1],
        summed[2],
        summed[3],
        summed[4],
        gain_sums[:, 1],
        grad_gate,
        grad_up,
        grad_down,
    )


def solution(mesh):
    dp_size, tensor_size = mesh.shape["dp"], mesh.shape["tensor"]
    fine = jax.sharding.Mesh(
        mesh.devices.reshape(4, dp_size // 4, tensor_size // 2, 2), ("z", "y", "x", "c")
    )
    dp, tensor = ("z", "y"), ("x", "c")
    tokens = P(dp + tensor, None)
    rows = P(dp, tensor)
    columns = P(tensor, dp)
    in_specs = (
        tokens,
        P(dp),
        rows,
        rows,
        rows,
        columns,
        P(dp),
        rows,
        rows,
        columns,
        P(),
        tokens,
    )
    out_specs = (
        tokens,
        tokens,
        P(dp),
        rows,
        rows,
        rows,
        columns,
        P(dp),
        rows,
        rows,
        columns,
    )
    return jax.shard_map(local, mesh=fine, in_specs=in_specs, out_specs=out_specs, check_vma=False)
```

```python
import jax
import jax.numpy as jnp
from jax import lax
from jax.experimental import pallas as pl
from jax.experimental.pallas import tpu as pltpu
from jax.sharding import PartitionSpec as P

HEAD_SIZE = 64
SEG = 256
MAX_STEPS = 9


attn_scale = 0.015625
branch_scale = 0.22
norm_eps = 1e-05
rope_base = 10000000.0
masked_score = -1e30


def segment_depth(parents):
    seg_total = parents.shape[0]
    seg_ids = jnp.arange(seg_total, dtype=jnp.int32)
    reach = (parents[:, None] == seg_ids[None, :]) | (seg_ids[:, None] == seg_ids[None, :])
    reach = reach.astype(jnp.float32)
    for doubling in range(4):
        reach = jnp.minimum(jnp.dot(reach, reach, preferred_element_type=jnp.float32), 1.0)
    return jnp.sum(reach, axis=1).astype(jnp.int32) - 1


def rope_tables(position, head_dim):
    half_dim = head_dim // 2
    exponent = jnp.arange(half_dim, dtype=jnp.float32) * (2.0 / head_dim)
    inverse = jnp.power(rope_base, -exponent)
    angles = position.astype(jnp.float32)[:, None] * inverse[None, :]
    return (jnp.cos(angles), jnp.sin(angles))


def rotary_apply(value_rows, cosine_table, sine_table, direction):
    half_dim = value_rows.shape[-1] // 2
    first_half = value_rows[..., :half_dim]
    second = value_rows[..., half_dim:]
    cos_part = cosine_table[:, None, :]
    sin_part = sine_table[:, None, :] * direction
    return jnp.concatenate(
        [first_half * cos_part - second * sin_part, second * cos_part + first_half * sin_part],
        axis=-1,
    )


def rotated(value, axis, step):
    size = lax.axis_size(axis)
    return lax.ppermute(value, axis, [(i, (i + step) % size) for i in range(size)])


def relative_pieces(value, axis):
    return [value] + [rotated(value, axis, k) for k in range(1, lax.axis_size(axis))]


def natural_pieces(pieces, axis):
    size = len(pieces)
    place = lax.axis_index(axis)
    return [
        lax.select_n(place, *[pieces[(i - j) % size] for i in range(size)]) for j in range(size)
    ]


def gathered(value, axis):
    size = lax.axis_size(axis)
    copies = jnp.broadcast_to(value[None], (size, *value.shape))
    return lax.all_to_all(copies, axis, 0, 0, tiled=True)


def exchanged(blocks, axis):
    return lax.all_to_all(blocks, axis, 0, 0, tiled=True)


def summed_pieces(pieces, axis):
    sent = [rotated(pieces[k].astype(jnp.bfloat16), axis, -k) for k in range(1, len(pieces))]
    total = pieces[0].astype(jnp.float32)
    for value in sent:
        total = total + value.astype(jnp.float32)
    return total


def summed_blocks(blocks, axis):
    return jnp.sum(exchanged(blocks.astype(jnp.bfloat16), axis).astype(jnp.float32), axis=0)


def column_blocks(value, count):
    return value.reshape(value.shape[0], count, -1).transpose(1, 0, 2)


def joined_columns(blocks):
    return blocks.transpose(1, 0, 2).reshape(blocks.shape[1], -1)


def relative_columns(value):
    size = lax.axis_size("y")
    place = lax.axis_index("y")
    rows = value.shape[0]
    split = value.reshape(rows, lax.axis_size("z"), size, -1)
    flat = [split[:, :, i].reshape(rows, -1) for i in range(size)]
    return jnp.concatenate(
        [
            lax.select_n(place, *[flat[(i - k) % size] for i in range(size)])
            for k in range(size)
        ],
        axis=1,
    )


def natural_columns(value):
    size = lax.axis_size("y")
    rows = value.shape[0]
    split = value.reshape(rows, size, lax.axis_size("z"), -1)
    parts = natural_pieces([split[:, k] for k in range(size)], "y")
    return jnp.stack(parts, axis=2).reshape(rows, -1)


def after(value, *others):
    return lax.optimization_barrier((value, *others))[0]


def ancestor_count(parents, seg):
    def climb(step, state):
        current, count = state
        above = parents[current]
        return above, count + jnp.where(above != current, 1, 0)

    return lax.fori_loop(0, MAX_STEPS, climb, (seg, jnp.int32(1)))[1]


def left_lanes(shape):
    return lax.broadcasted_iota(jnp.int32, shape, 1) < HEAD_SIZE


def stacked_heads(pairs, group):
    left = left_lanes((SEG, 2 * HEAD_SIZE))
    own = left == (group == 0)
    stack = []
    for pair in pairs:
        swapped = pltpu.roll(pair, HEAD_SIZE, 1)
        even = jnp.where(group == 0, pair, swapped)
        odd = jnp.where(group == 0, swapped, pair)
        stack += [jnp.where(own, even, 0.0), jnp.where(own, odd, 0.0)]
    return jnp.concatenate(stack, axis=0)


def unstacked_heads(stack, group):
    left = left_lanes((SEG, 2 * HEAD_SIZE))
    pairs = []
    for first in range(0, stack.shape[0], 2 * SEG):
        even, odd = stack[first : first + SEG], stack[first + SEG : first + 2 * SEG]
        even = jnp.where(group == 0, even, pltpu.roll(even, HEAD_SIZE, 1))
        odd = jnp.where(group == 0, pltpu.roll(odd, HEAD_SIZE, 1), odd)
        pairs.append(jnp.where(left, even, odd))
    return pairs


def turned(value, cosine, sine, direction):
    half = HEAD_SIZE // 2
    lane = lax.broadcasted_iota(jnp.int32, value.shape, 1)
    first = lax.rem(lane, HEAD_SIZE) < half
    ahead = pltpu.roll(value, 2 * HEAD_SIZE - half, 1)
    behind = pltpu.roll(value, half, 1)
    signed = sine * direction
    return value * cosine + jnp.where(first, -ahead * signed, behind * signed)


def nt_dot(left, right):
    return lax.dot_general(
        left, right, (((1,), (1,)), ((), ())), preferred_element_type=jnp.float32
    )


def nn_dot(left, right):
    return lax.dot_general(
        left, right, (((1,), (0,)), ((), ())), preferred_element_type=jnp.float32
    )


def causal_tile(rows):
    query = lax.rem(lax.broadcasted_iota(jnp.int32, (rows, SEG), 0), SEG)
    return lax.broadcasted_iota(jnp.int32, (rows, SEG), 1) <= query


def attend_kernel(
    parents, first_seg, proj, cosine, sine, keys_values, out, out_low, stats, queries, scores
):
    seg = first_seg[0] + pl.program_id(0)
    group = pl.program_id(1)
    count = ancestor_count(parents, seg)
    cos, sin = cosine[...], sine[...]
    lanes = 2 * HEAD_SIZE
    pairs = [
        turned(proj[:, at : at + lanes], cos, sin, 1.0) * attn_scale
        for at in range(0, proj.shape[1], lanes)
    ]
    stack = stacked_heads(pairs, group).astype(jnp.bfloat16)
    queries[0, 0] = stack
    rows = stack.shape[0]

    first = jnp.where(causal_tile(rows), nt_dot(stack, keys_values[seg, :, :lanes]), masked_score)
    scores[0] = first

    def measure(step, state):
        current, top = state
        current = parents[current]
        tile = nt_dot(stack, keys_values[current, :, :lanes])
        scores[step] = tile
        return current, jnp.maximum(top, tile)

    top = lax.fori_loop(1, count, measure, (seg, first))[1]
    row_max = jnp.max(top, axis=1, keepdims=True)

    def gather(step, state):
        current, total, mixed = state
        terms = jnp.exp(scores[step] - row_max)
        mixed = mixed + nn_dot(terms.astype(jnp.bfloat16), keys_values[current, :, lanes:])
        return parents[current], total + terms, mixed

    start = (seg, jnp.zeros((rows, SEG), jnp.float32), jnp.zeros((rows, lanes), jnp.float32))
    total, mixed = lax.fori_loop(0, count, gather, start)[1:]
    total = jnp.sum(total, axis=1, keepdims=True)
    mixed = mixed / total
    stats[0, 0] = row_max + jnp.log(total)
    for place, pair in enumerate(unstacked_heads(mixed, group)):
        out[:, place * lanes : (place + 1) * lanes] = pair
        out_low[:, place * lanes : (place + 1) * lanes] = pair.astype(jnp.bfloat16)


def attend_back_kernel(
    parents, first_seg, queries, grads, attended, stats, cosine, sine, keys_values,
    grad_proj, grad_kv, key_sum, value_sum,
):
    seg = first_seg[0] + pl.program_id(0)
    group = pl.program_id(1)
    count = ancestor_count(parents, seg)
    lanes = 2 * HEAD_SIZE

    @pl.when((pl.program_id(0) == 0) & (group == 0))
    def _():
        key_sum[...] = jnp.zeros_like(key_sum)
        value_sum[...] = jnp.zeros_like(value_sum)

    stack = queries[0, 0]
    rows = stack.shape[0]
    grad_pairs = [
        grads[:, at : at + lanes].astype(jnp.float32) for at in range(0, grads.shape[1], lanes)
    ]
    left = left_lanes((SEG, lanes))
    deltas = []
    for place, pair in enumerate(grad_pairs):
        product = pair * attended[:, place * lanes : (place + 1) * lanes]
        deltas.append(jnp.sum(jnp.where(left, product, 0.0), axis=1, keepdims=True))
        deltas.append(jnp.sum(jnp.where(left, 0.0, product), axis=1, keepdims=True))
    delta = jnp.concatenate(deltas, axis=0)
    grad_wide = stacked_heads(grad_pairs, group)
    grad_stack = grad_wide.astype(jnp.bfloat16)
    grad_turned = grad_wide.T.astype(jnp.bfloat16)
    query_turned = stack.astype(jnp.float32).T.astype(jnp.bfloat16)
    log_total = stats[0, 0]

    def visit(current, total, diagonal):
        tile_keys, tile_values = keys_values[current, :, :lanes], keys_values[current, :, lanes:]
        tile = nt_dot(stack, tile_keys)
        if diagonal:
            tile = jnp.where(causal_tile(rows), tile, masked_score)
        probs = jnp.exp(tile - log_total)
        grad_probs = nt_dot(grad_stack, tile_values)
        grad_tile = (probs * (grad_probs - delta)).astype(jnp.bfloat16)
        key_sum[current] += nn_dot(query_turned, grad_tile)
        value_sum[current] += nn_dot(grad_turned, probs.astype(jnp.bfloat16))
        return total + nn_dot(grad_tile, tile_keys)

    total = visit(seg, jnp.zeros((rows, lanes), jnp.float32), True)

    def climb(step, state):
        current, total = state
        current = parents[current]
        return current, visit(current, total, False)

    total = lax.fori_loop(1, count, climb, (seg, total))[1]
    cos, sin = cosine[...], sine[...]
    for place, pair in enumerate(unstacked_heads(total * attn_scale, group)):
        grad_proj[:, place * lanes : (place + 1) * lanes] = turned(pair, cos, sin, -1.0).astype(
            jnp.bfloat16
        )

    @pl.when((pl.program_id(0) == pl.num_programs(0) - 1) & (group == pl.num_programs(1) - 1))
    def _():
        grad_kv[:, :lanes, :] = key_sum[...].astype(jnp.bfloat16)
        grad_kv[:, lanes:, :] = value_sum[...].astype(jnp.bfloat16)


def attention_specs(group_rows, cols, groups, segs):
    width = cols // groups
    lanes = 2 * HEAD_SIZE
    block = pl.BlockSpec((SEG, width), lambda s, g: (s, g))
    table = pl.BlockSpec((SEG, lanes), lambda s, g: (s, 0))
    whole = pl.BlockSpec((segs, SEG, 2 * lanes), lambda s, g: (0, 0, 0))
    rows = SEG * (width // HEAD_SIZE)
    stack = pl.BlockSpec((1, 1, rows, lanes), lambda s, g: (s, g, 0, 0))
    stat = pl.BlockSpec((1, 1, rows, 1), lambda s, g: (s, g, 0, 0))
    scalar = pl.BlockSpec(memory_space=pltpu.SMEM)
    return block, table, whole, rows, stack, stat, scalar


def attend(parents, first_seg, proj, cosine, sine, keys_values, groups):
    group_rows, cols = proj.shape
    segs = keys_values.shape[0]
    lanes = 2 * HEAD_SIZE
    block, table, whole, rows, stack, stat, scalar = attention_specs(group_rows, cols, groups, segs)
    grid = (group_rows // SEG, groups)
    tiles = grid[0] * grid[1] * 8 * rows * SEG
    return pl.pallas_call(
        attend_kernel,
        grid=grid,
        in_specs=[scalar, scalar, block, table, table, whole],
        out_specs=[block, block, stat, stack],
        out_shape=[
            jax.ShapeDtypeStruct((group_rows, cols), jnp.float32),
            jax.ShapeDtypeStruct((group_rows, cols), jnp.bfloat16),
            jax.ShapeDtypeStruct((*grid, rows, 1), jnp.float32),
            jax.ShapeDtypeStruct((*grid, rows, lanes), jnp.bfloat16),
        ],
        scratch_shapes=[pltpu.VMEM((MAX_STEPS + 1, rows, SEG), jnp.float32)],
        compiler_params=pltpu.CompilerParams(vmem_limit_bytes=56 * 2**20),
        cost_estimate=pl.CostEstimate(
            flops=4 * tiles * lanes, bytes_accessed=8 * 2**20, transcendentals=tiles
        ),
    )(parents, first_seg, proj, cosine, sine, keys_values)


def attend_back(
    parents, first_seg, queries, grads, attended, stats, cosine, sine, keys_values, groups
):
    group_rows, cols = grads.shape
    segs = keys_values.shape[0]
    lanes = 2 * HEAD_SIZE
    block, table, whole, rows, stack, stat, scalar = attention_specs(group_rows, cols, groups, segs)
    grid = (group_rows // SEG, groups)
    tiles = grid[0] * grid[1] * 8 * rows * SEG
    return pl.pallas_call(
        attend_back_kernel,
        grid=grid,
        in_specs=[scalar, scalar, stack, block, block, stat, table, table, whole],
        out_specs=[block, pl.BlockSpec((segs, 2 * lanes, SEG), lambda s, g: (0, 0, 0))],
        out_shape=[
            jax.ShapeDtypeStruct((group_rows, cols), jnp.bfloat16),
            jax.ShapeDtypeStruct((segs, 2 * lanes, SEG), jnp.bfloat16),
        ],
        scratch_shapes=[
            pltpu.VMEM((segs, lanes, SEG), jnp.float32),
            pltpu.VMEM((segs, lanes, SEG), jnp.float32),
        ],
        compiler_params=pltpu.CompilerParams(vmem_limit_bytes=60 * 2**20),
        cost_estimate=pl.CostEstimate(
            flops=10 * tiles * lanes, bytes_accessed=8 * 2**20, transcendentals=tiles
        ),
    )(parents, first_seg, queries, grads, attended, stats, cosine, sine, keys_values)


def row_norm(value):
    inverse = lax.rsqrt(jnp.mean(value * value, axis=-1, keepdims=True) + norm_eps)
    return value * inverse, inverse


def norm_back(grad, normed, inverse, gain):
    scaled = grad * gain
    return inverse * (scaled - normed * jnp.mean(scaled * normed, axis=-1, keepdims=True))


def silu_parts(gate_pre):
    sigmoid = jax.nn.sigmoid(gate_pre)
    return sigmoid, gate_pre * sigmoid


def matmul(left, right):
    return jnp.dot(left, right, preferred_element_type=jnp.float32)


def matmul_turned(left, right):
    return nt_dot(left, right)


def turned_matmul(left, right):
    return lax.dot_general(
        left, right, (((0,), (0,)), ((), ())), preferred_element_type=jnp.float32
    )


def tensor_sum(part, rows):
    x_size, c_size = lax.axis_size("x"), lax.axis_size("c")
    blocks = part.reshape(x_size, c_size, rows, -1)
    c_place, x_place = lax.axis_index("c"), lax.axis_index("x")

    def block(value, place, k, axis):
        size = value.shape[axis]
        return lax.dynamic_index_in_dim(
            value, lax.rem(place - k + size, size), axis, keepdims=False
        )

    mine = summed_pieces([block(blocks, c_place, k, 1) for k in range(c_size)], "c")
    mine = mine.astype(jnp.bfloat16)
    return summed_pieces([block(mine, x_place, k, 0) for k in range(x_size)], "x")


def local(
    tokens,
    norm_gain,
    q_weight,
    key_matrix,
    value_matrix,
    o_weight,
    mlp_gain,
    gate_weight,
    up_weight,
    down_weight,
    parents,
    out_grad,
):
    z_size, y_size, x_size = (lax.axis_size(name) for name in ("z", "y", "x"))
    tensor_size = x_size * lax.axis_size("c")
    low = jnp.bfloat16
    local_rows, width = tokens.shape
    group_rows = local_rows * tensor_size
    kv_cols = key_matrix.shape[1]
    kv_local = kv_cols // HEAD_SIZE
    q_cols = q_weight.shape[1]
    own_width = norm_gain.shape[0]

    own_tokens = relative_columns(tokens)
    own_grad = relative_columns(out_grad).astype(jnp.float32)
    group_tokens = lax.all_gather(own_tokens, ("x", "c"), axis=0, tiled=True)

    both_gains = jnp.concatenate([norm_gain, mlp_gain])
    both_gains = jnp.pad(both_gains, (0, -both_gains.shape[0] % (2 * kv_cols)))
    kv_shard = jnp.concatenate(
        [
            jnp.concatenate([key_matrix, value_matrix], axis=1),
            both_gains.reshape(-1, 2 * kv_cols),
        ],
        axis=0,
    )
    kv_z = gathered(kv_shard, "z")
    kv_zy = jnp.stack(relative_pieces(kv_z, "y"))
    kv_full = kv_zy[:, :, :own_width].reshape(width, 2 * kv_cols)
    gains = kv_zy[:, :, own_width:].reshape(z_size * y_size, -1).astype(jnp.float32)
    gains = gains[:, : 2 * own_width].reshape(-1, 2, own_width)
    gain_one, gain_two = gains[:, 0].reshape(-1), gains[:, 1].reshape(-1)

    q_z = gathered(after(q_weight, kv_z), "z")
    q_full = jnp.stack(relative_pieces(q_z, "y")).reshape(width, q_cols)

    depth = segment_depth(parents)
    dp_place = lax.axis_index(("z", "y"))
    seg_count = group_rows // SEG
    first_seg = (dp_place * seg_count).astype(jnp.int32)
    own_depth = lax.dynamic_slice_in_dim(depth, first_seg, seg_count, 0)
    position = (own_depth[:, None] * SEG + jnp.arange(SEG, dtype=jnp.int32)[None, :]).reshape(-1)
    cosine_table, sine_table = rope_tables(position, HEAD_SIZE)
    cosine_lanes = jnp.tile(cosine_table, (1, 4))
    sine_lanes = jnp.tile(sine_table, (1, 4))
    first_seg = first_seg.reshape(1)

    inputs = own_tokens.astype(jnp.float32)
    normed_one, inv_one = row_norm(inputs)
    group_normed, _ = row_norm(group_tokens.astype(jnp.float32))
    rows_one = (group_normed * gain_one).astype(low)
    kv_proj = matmul(rows_one, kv_full)
    key_rows = rotary_apply(
        kv_proj[:, :kv_cols].reshape(group_rows, kv_local, HEAD_SIZE),
        cosine_table,
        sine_table,
        1.0,
    ).reshape(group_rows, kv_cols)
    kv_rows = jnp.concatenate([key_rows, kv_proj[:, kv_cols:]], axis=1).astype(low)
    all_z = gathered(after(kv_rows, q_z), "z")
    all_kv = jnp.stack(natural_pieces(relative_pieces(all_z, "y"), "y"), axis=1)
    all_kv = all_kv.reshape(-1, SEG, 2 * kv_cols)

    gate_z = exchanged(column_blocks(after(gate_weight, all_z), z_size), "z")
    gate_z = gate_z.reshape(z_size * own_width, -1)
    o_z = joined_columns(gathered(after(o_weight, gate_z), "z"))
    o_full = jnp.concatenate(relative_pieces(o_z, "y"), axis=1)
    up_z = exchanged(column_blocks(after(up_weight, o_z), z_size), "z")
    up_z = up_z.reshape(z_size * own_width, -1)
    down_z = joined_columns(
        exchanged(after(down_weight, up_z).reshape(z_size, -1, own_width), "z")
    )
    gate_block = jnp.concatenate(relative_pieces(gate_z, "y"), axis=0)
    gate_block = jnp.concatenate(relative_pieces(gate_block, "x"), axis=1)
    up_block = jnp.concatenate(relative_pieces(up_z, "x"), axis=1)
    up_block = jnp.concatenate(relative_pieces(up_block, "y"), axis=0)
    down_block = jnp.concatenate(relative_pieces(down_z, "x"), axis=0)
    down_block = jnp.concatenate(relative_pieces(down_block, "y"), axis=1)

    query_proj = matmul(rows_one, q_full)
    attended, attn_low, stats, query_stack = attend(
        parents, first_seg, query_proj, cosine_lanes, sine_lanes, all_kv, kv_local
    )
    attn_part = matmul(attn_low, o_full).astype(low)
    attn_mine = tensor_sum(attn_part, local_rows)
    middle = inputs + branch_scale * attn_mine
    normed_two, inv_two = row_norm(middle)
    hidden_two = (normed_two * gain_two).astype(low)

    rows_two = lax.all_gather(hidden_two, ("z", "c"), axis=0, tiled=True)
    grad_mlp = (branch_scale * own_grad).astype(low)
    grad_mlp_rows = lax.all_gather(grad_mlp, ("z", "c"), axis=0, tiled=True)
    gate_pre = matmul(rows_two, gate_block)
    up_pre = matmul(rows_two, up_block)
    gate_sigmoid, gate_silu = silu_parts(gate_pre)
    activated = (gate_silu * up_pre).astype(low)
    mlp_part = matmul(activated, down_block).astype(low)
    grad_hidden = matmul_turned(grad_mlp_rows, down_block)
    grad_gate_act = (
        grad_hidden * up_pre * gate_sigmoid * (1.0 + gate_pre * (1.0 - gate_sigmoid))
    ).astype(low)
    grad_up_act = (grad_hidden * gate_silu).astype(low)
    input_part = (
        matmul_turned(grad_gate_act, gate_block) + matmul_turned(grad_up_act, up_block)
    ).astype(low)
    grad_rows_two = lax.psum_scatter(
        input_part, ("z", "c"), scatter_dimension=0, tiled=True
    ).astype(jnp.float32)
    mlp_mine = lax.psum_scatter(
        mlp_part, ("z", "c"), scatter_dimension=0, tiled=True
    ).astype(jnp.float32)
    mixed = natural_columns((middle + branch_scale * mlp_mine).astype(low))

    gain_two_part = jnp.sum(grad_rows_two * normed_two, axis=0)
    grad_middle = own_grad + norm_back(grad_rows_two, normed_two, inv_two, gain_two)
    grad_attn = (branch_scale * grad_middle).astype(low)
    grad_attn_rows = lax.all_gather(grad_attn, ("x", "c"), axis=0, tiled=True)

    def halves(value, count):
        part = value.shape[1] // count
        return [value[:, i * part : (i + 1) * part] for i in range(count)]

    down_pieces = [
        summed_pieces(
            [turned_matmul(near, far) for far in halves(grad_mlp_rows, y_size)], "y"
        ).astype(low)
        for near in halves(activated, x_size)
    ]
    grad_down_z = summed_pieces(down_pieces, "x")
    grad_down = exchanged(column_blocks(grad_down_z.astype(low), z_size), "z")
    grad_down = grad_down.reshape(-1, own_width).astype(jnp.float32)

    def gate_grad(first, second, right):
        lefts, rights = halves(rows_two, y_size), halves(right, x_size)
        if first == "y":
            pieces = [
                summed_pieces([turned_matmul(a, b) for a in lefts], "y").astype(low)
                for b in rights
            ]
        else:
            pieces = [
                summed_pieces([turned_matmul(a, b) for b in rights], "x").astype(low)
                for a in lefts
            ]
        mine = summed_pieces(pieces, second).astype(low)
        blocks = exchanged(mine.reshape(z_size, own_width, -1), "z")
        return joined_columns(blocks).astype(jnp.float32)

    grad_gate = gate_grad("y", "x", grad_gate_act)
    grad_up = gate_grad("x", "y", grad_up_act)

    grad_heads = matmul_turned(grad_attn_rows, o_full).astype(low)
    grad_o_part = turned_matmul(attn_low, grad_attn_rows)
    grad_o_y = summed_pieces(halves(grad_o_part, y_size), "y")
    grad_o = summed_blocks(column_blocks(grad_o_y, z_size), "z")
    grad_queries, grad_kv = attend_back(
        parents, first_seg, query_stack, grad_heads, attended, stats, cosine_lanes, sine_lanes,
        all_kv, kv_local,
    )
    kv_split = grad_kv.reshape(z_size, y_size, seg_count, 2 * kv_cols, SEG)
    y_place = lax.axis_index("y")
    kv_pieces = [
        lax.dynamic_index_in_dim(
            kv_split, lax.rem(y_place - k + y_size, y_size), 1, keepdims=False
        )
        for k in range(y_size)
    ]
    kv_mine = summed_blocks(summed_pieces(kv_pieces, "y"), "z")
    kv_mine = kv_mine.transpose(0, 2, 1).reshape(group_rows, 2 * kv_cols)
    grad_keys = rotary_apply(
        kv_mine[:, :kv_cols].reshape(group_rows, kv_local, HEAD_SIZE),
        cosine_table,
        sine_table,
        -1.0,
    ).reshape(group_rows, kv_cols)
    grad_kv_rows = jnp.concatenate([grad_keys, kv_mine[:, kv_cols:]], axis=1).astype(low)

    def owned_rows(part):
        mine = summed_pieces([part[i * width // y_size : (i + 1) * width // y_size] for i in range(y_size)], "y")
        return summed_blocks(mine.reshape(z_size, own_width, -1), "z")

    grad_q = owned_rows(turned_matmul(rows_one, grad_queries))
    grad_kv_weight = owned_rows(turned_matmul(rows_one, grad_kv_rows))
    input_one = matmul_turned(grad_queries, q_full) + matmul_turned(grad_kv_rows, kv_full)
    grad_rows_one = tensor_sum(input_one.astype(low), local_rows)
    gain_one_part = jnp.sum(grad_rows_one * normed_one, axis=0)
    grad_inputs = grad_middle + norm_back(grad_rows_one, normed_one, inv_one, gain_one)
    grad_tokens = natural_columns(grad_inputs.astype(low))

    gain_parts = jnp.stack([gain_one_part, gain_two_part], axis=0)
    gain_parts = natural_columns(gain_parts).reshape(2, z_size * y_size, 1, own_width)
    gain_parts = jnp.broadcast_to(
        gain_parts, (2, z_size * y_size, tensor_size, own_width)
    ).reshape(2, -1, own_width).transpose(1, 0, 2)
    gain_sums = jnp.sum(exchanged(gain_parts, ("z", "y", "x", "c")), axis=0)
    return (
        mixed,
        grad_tokens,
        gain_sums[0],
        grad_q,
        grad_kv_weight[:, :kv_cols],
        grad_kv_weight[:, kv_cols:],
        grad_o,
        gain_sums[1],
        grad_gate,
        grad_up,
        grad_down,
    )


def solution(mesh):
    dp_size, tensor_size = mesh.shape["dp"], mesh.shape["tensor"]
    fine = jax.sharding.Mesh(
        mesh.devices.reshape(4, dp_size // 4, tensor_size // 2, 2), ("z", "y", "x", "c")
    )
    dp, tensor = ("z", "y"), ("x", "c")
    tokens = P(dp + tensor, None)
    rows = P(dp, tensor)
    columns = P(tensor, dp)
    in_specs = (
        tokens,
        P(dp),
        rows,
        rows,
        rows,
        columns,
        P(dp),
        rows,
        rows,
        columns,
        P(),
        tokens,
    )
    out_specs = (
        tokens,
        tokens,
        P(dp),
        rows,
        rows,
        rows,
        columns,
        P(dp),
        rows,
        rows,
        columns,
    )
    return jax.shard_map(local, mesh=fine, in_specs=in_specs, out_specs=out_specs, check_vma=False)
```

```python
import functools

import jax
import jax.numpy as jnp
from jax import lax
from jax.experimental import pallas as pl
from jax.experimental.pallas import tpu as pltpu
from jax.sharding import PartitionSpec as P

HEAD_SIZE = 64
SEG = 256
MAX_STEPS = 9
LANES = 2 * HEAD_SIZE
KERNEL_VMEM = 56 * 2**20
SMALL_COST = pl.CostEstimate(flops=2**28, bytes_accessed=2**18, transcendentals=0)


attn_scale = 0.015625
branch_scale = 0.22
norm_eps = 1e-05
rope_base = 10000000.0
masked_score = -1e30


def segment_depth(parents):
    seg_total = parents.shape[0]
    seg_ids = jnp.arange(seg_total, dtype=jnp.int32)
    reach = (parents[:, None] == seg_ids[None, :]) | (seg_ids[:, None] == seg_ids[None, :])
    reach = reach.astype(jnp.float32)
    for doubling in range(4):
        reach = jnp.minimum(jnp.dot(reach, reach, preferred_element_type=jnp.float32), 1.0)
    return jnp.sum(reach, axis=1).astype(jnp.int32) - 1


def rope_tables(position, head_dim):
    half_dim = head_dim // 2
    exponent = jnp.arange(half_dim, dtype=jnp.float32) * (2.0 / head_dim)
    inverse = jnp.power(rope_base, -exponent)
    angles = position.astype(jnp.float32)[:, None] * inverse[None, :]
    return (jnp.cos(angles), jnp.sin(angles))


def rotated(value, axis, step):
    size = lax.axis_size(axis)
    return lax.ppermute(value, axis, [(i, (i + step) % size) for i in range(size)])


def relative_pieces(value, axis):
    return [value] + [rotated(value, axis, k) for k in range(1, lax.axis_size(axis))]


def natural_pieces(pieces, axis):
    size = len(pieces)
    place = lax.axis_index(axis)
    return [
        lax.select_n(place, *[pieces[(i - j) % size] for i in range(size)]) for j in range(size)
    ]


def gathered(value, axis):
    size = lax.axis_size(axis)
    copies = jnp.broadcast_to(value[None], (size, *value.shape))
    return lax.all_to_all(copies, axis, 0, 0, tiled=True)


def exchanged(blocks, axis):
    return lax.all_to_all(blocks, axis, 0, 0, tiled=True)


def summed_pieces(pieces, axis):
    sent = [rotated(pieces[k].astype(jnp.bfloat16), axis, -k) for k in range(1, len(pieces))]
    total = pieces[0].astype(jnp.float32)
    for value in sent:
        total = total + value.astype(jnp.float32)
    return total


def summed_blocks(blocks, axis):
    return jnp.sum(exchanged(blocks.astype(jnp.bfloat16), axis).astype(jnp.float32), axis=0)


def column_blocks(value, count):
    return value.reshape(value.shape[0], count, -1).transpose(1, 0, 2)


def joined_columns(blocks):
    return blocks.transpose(1, 0, 2).reshape(blocks.shape[1], -1)


def relative_columns(value):
    size = lax.axis_size("y")
    place = lax.axis_index("y")
    rows = value.shape[0]
    split = value.reshape(rows, lax.axis_size("z"), size, -1)
    flat = [split[:, :, i].reshape(rows, -1) for i in range(size)]
    return jnp.concatenate(
        [
            lax.select_n(place, *[flat[(i - k) % size] for i in range(size)])
            for k in range(size)
        ],
        axis=1,
    )


def natural_columns(value):
    size = lax.axis_size("y")
    rows = value.shape[0]
    split = value.reshape(rows, size, lax.axis_size("z"), -1)
    parts = natural_pieces([split[:, k] for k in range(size)], "y")
    return jnp.stack(parts, axis=2).reshape(rows, -1)


def together(*values):
    return lax.optimization_barrier(values)


def ancestor_count(parents, seg):
    def climb(step, state):
        current, count = state
        above = parents[current]
        return above, count + jnp.where(above != current, 1, 0)

    return lax.fori_loop(0, MAX_STEPS, climb, (seg, jnp.int32(1)))[1]


def left_lanes(shape):
    return lax.broadcasted_iota(jnp.int32, shape, 1) < HEAD_SIZE


def stacked_heads(pairs, to_left):
    left = left_lanes(pairs[0].shape)
    stack = []
    for pair in pairs:
        swapped = pltpu.roll(pair, HEAD_SIZE, 1)
        for head in (pair, swapped) if to_left else (swapped, pair):
            stack.append(jnp.where(left, head, 0.0) if to_left else jnp.where(left, 0.0, head))
    return jnp.concatenate(stack, axis=0)


def unstacked_heads(stack, from_left):
    left = left_lanes((SEG, 2 * HEAD_SIZE))
    pairs = []
    for first in range(0, stack.shape[0], 2 * SEG):
        even, odd = stack[first : first + SEG], stack[first + SEG : first + 2 * SEG]
        if from_left:
            odd = pltpu.roll(odd, HEAD_SIZE, 1)
        else:
            even = pltpu.roll(even, HEAD_SIZE, 1)
        pairs.append(jnp.where(left, even, odd))
    return pairs


def turned(value, cosine, sine, direction):
    half = HEAD_SIZE // 2
    lane = lax.broadcasted_iota(jnp.int32, value.shape, 1)
    first = lax.rem(lane, HEAD_SIZE) < half
    ahead = pltpu.roll(value, LANES - half, 1)
    behind = pltpu.roll(value, half, 1)
    signed = sine * direction
    return value * cosine + jnp.where(first, -ahead * signed, behind * signed)


def nt_dot(left, right):
    return lax.dot_general(
        left, right, (((1,), (1,)), ((), ())), preferred_element_type=jnp.float32
    )


def nn_dot(left, right):
    return lax.dot_general(
        left, right, (((1,), (0,)), ((), ())), preferred_element_type=jnp.float32
    )


def causal_tile(rows):
    query = lax.rem(lax.broadcasted_iota(jnp.int32, (rows, SEG), 0), SEG)
    return lax.broadcasted_iota(jnp.int32, (rows, SEG), 1) <= query


def lane_blocks(ref):
    return [ref[:, at : at + LANES] for at in range(0, ref.shape[1], LANES)]


def project_kernel(parts, rows, *refs):
    weights, (cosine, sine, out) = refs[:parts], refs[parts:]
    depth = weights[0].shape[0]
    product = sum(nn_dot(rows[:, i * depth : (i + 1) * depth], w[...]) for i, w in enumerate(weights))
    cos, sin = cosine[...], sine[...]
    for at in range(0, product.shape[1], LANES):
        block = turned(product[:, at : at + LANES], cos, sin, 1.0)
        out[:, at : at + LANES] = block.astype(jnp.bfloat16)


def project(rows, weights, cosine, sine):
    count, width = rows.shape
    depth, cols = weights[0].shape
    step = 2 * LANES
    table = pl.BlockSpec((count, LANES), lambda j: (0, 0))
    return pl.pallas_call(
        functools.partial(project_kernel, len(weights)),
        grid=(cols // step,),
        in_specs=[pl.BlockSpec((count, width), lambda j: (0, 0))]
        + [pl.BlockSpec((depth, step), lambda j: (0, j))] * len(weights)
        + [table, table],
        out_specs=pl.BlockSpec((count, step), lambda j: (0, j)),
        out_shape=jax.ShapeDtypeStruct((count, cols), jnp.bfloat16),
        compiler_params=pltpu.CompilerParams(vmem_limit_bytes=KERNEL_VMEM),
        cost_estimate=SMALL_COST,
    )(rows, *weights, cosine, sine)


def attend_kernel(parents, segs, queries, keys_values, out, stats, scores):
    seg = segs[pl.program_id(0)]
    count = ancestor_count(parents, seg)
    pairs = [block.astype(jnp.float32) * attn_scale for block in lane_blocks(queries)]
    stack = stacked_heads(pairs, True).astype(jnp.bfloat16)
    rows = stack.shape[0]

    first = jnp.where(causal_tile(rows), nt_dot(stack, keys_values[seg]), masked_score)
    scores[0] = first

    def folded(tile):
        return jnp.maximum(tile[:, :LANES], tile[:, LANES:])

    def measure(step, state):
        current, top = state
        current = parents[current]
        tile = nt_dot(stack, keys_values[current])
        scores[step] = tile
        return current, jnp.maximum(top, folded(tile))

    top = lax.fori_loop(1, count, measure, (seg, folded(first)))[1]
    row_max = jnp.max(top, axis=1, keepdims=True)
    left = left_lanes((SEG, LANES))

    def gather(step, state):
        current, mixed = state
        terms = jnp.exp(scores[step] - row_max).astype(jnp.bfloat16)
        tile = jnp.where(left, jnp.ones((SEG, LANES), jnp.bfloat16), keys_values[current])
        return parents[current], mixed + nn_dot(terms, tile)

    start = (seg, jnp.zeros((rows, LANES), jnp.float32))
    mixed = lax.fori_loop(0, count, gather, start)[1]
    total = mixed[:, :1]
    mixed = mixed / total
    stats[0] = row_max + jnp.log(total)
    for place, pair in enumerate(unstacked_heads(mixed, False)):
        out[:, place * LANES : (place + 1) * LANES] = pair


def attend_back_kernel(
    parents, segs, queries, grads, attended, stats, cosine, sine, keys_values, *refs
):
    earlier, (grad_queries, grad_kv, kv_sum) = refs[:-3], refs[-3:]
    seg = segs[pl.program_id(0)]
    count = ancestor_count(parents, seg)

    @pl.when(pl.program_id(0) == 0)
    def _():
        kv_sum[...] = earlier[0][...] if earlier else jnp.zeros_like(kv_sum)

    query_pairs = [block.astype(jnp.float32) * attn_scale for block in lane_blocks(queries)]
    grad_pairs = [block.astype(jnp.float32) for block in lane_blocks(grads)]
    left = left_lanes((SEG, LANES))
    deltas = []
    for pair, out in zip(grad_pairs, lane_blocks(attended)):
        product = pair * out
        deltas.append(jnp.sum(jnp.where(left, product, 0.0), axis=1, keepdims=True))
        deltas.append(jnp.sum(jnp.where(left, 0.0, product), axis=1, keepdims=True))
    delta = jnp.concatenate(deltas, axis=0)
    query_wide = stacked_heads(query_pairs, True)
    grad_wide = stacked_heads(grad_pairs, False)
    query_stack, grad_stack = query_wide.astype(jnp.bfloat16), grad_wide.astype(jnp.bfloat16)
    query_turned = query_wide.T.astype(jnp.bfloat16)
    grad_turned = grad_wide.T.astype(jnp.bfloat16)
    log_total = stats[0]
    rows = query_stack.shape[0]

    def visit(current, total, diagonal):
        tile_kv = keys_values[current]
        tile = nt_dot(query_stack, tile_kv)
        if diagonal:
            tile = jnp.where(causal_tile(rows), tile, masked_score)
        probs = jnp.exp(tile - log_total)
        grad_probs = nt_dot(grad_stack, tile_kv)
        grad_tile = (probs * (grad_probs - delta)).astype(jnp.bfloat16)
        kv_sum[current] += nn_dot(query_turned, grad_tile) + nn_dot(
            grad_turned, probs.astype(jnp.bfloat16)
        )
        return total + nn_dot(grad_tile, tile_kv)

    total = visit(seg, jnp.zeros((rows, LANES), jnp.float32), True)

    def climb(step, state):
        current, total = state
        current = parents[current]
        return current, visit(current, total, False)

    total = lax.fori_loop(1, count, climb, (seg, total))[1]
    cos, sin = cosine[...], sine[...]
    for place, pair in enumerate(unstacked_heads(total * attn_scale, True)):
        grad_queries[:, place * LANES : (place + 1) * LANES] = turned(
            pair, cos, sin, -1.0
        ).astype(jnp.bfloat16)

    @pl.when(pl.program_id(0) == pl.num_programs(0) - 1)
    def _():
        grad_kv[...] = kv_sum[...].astype(grad_kv.dtype)


def attention_specs(cols, seg_total):
    block = pl.BlockSpec((SEG, cols), lambda s: (s, 0))
    table = pl.BlockSpec((SEG, LANES), lambda s: (s, 0))
    whole = pl.BlockSpec((seg_total, SEG, LANES), lambda s: (0, 0, 0))
    rows = SEG * (cols // HEAD_SIZE)
    stat = pl.BlockSpec((1, rows, 1), lambda s: (s, 0, 0))
    return block, table, whole, rows, stat, pl.BlockSpec(memory_space=pltpu.SMEM)


def attend(parents, segs, queries, keys_values):
    count, cols = queries.shape
    block, table, whole, rows, stat, scalar = attention_specs(cols, keys_values.shape[0])
    steps = count // SEG
    return pl.pallas_call(
        attend_kernel,
        grid=(steps,),
        in_specs=[scalar, scalar, block, whole],
        out_specs=[block, stat],
        out_shape=[
            jax.ShapeDtypeStruct((count, cols), jnp.float32),
            jax.ShapeDtypeStruct((steps, rows, 1), jnp.float32),
        ],
        scratch_shapes=[pltpu.VMEM((MAX_STEPS + 1, rows, SEG), jnp.float32)],
        compiler_params=pltpu.CompilerParams(vmem_limit_bytes=KERNEL_VMEM),
        cost_estimate=SMALL_COST,
    )(parents, segs, queries, keys_values)


def attend_back(
    parents, segs, queries, grads, attended, stats, cosine, sine, keys_values, earlier=None
):
    count, cols = queries.shape
    seg_total = keys_values.shape[0]
    block, table, whole, rows, stat, scalar = attention_specs(cols, seg_total)
    sums = pl.BlockSpec((seg_total, LANES, SEG), lambda s: (0, 0, 0))
    last = earlier is not None
    sum_type = jnp.bfloat16 if last else jnp.float32
    return pl.pallas_call(
        attend_back_kernel,
        grid=(count // SEG,),
        in_specs=[scalar, scalar, block, block, block, stat, table, table, whole] + [sums] * last,
        out_specs=[block, sums],
        out_shape=[
            jax.ShapeDtypeStruct((count, cols), jnp.bfloat16),
            jax.ShapeDtypeStruct((seg_total, LANES, SEG), sum_type),
        ],
        scratch_shapes=[pltpu.VMEM((seg_total, LANES, SEG), jnp.float32)],
        compiler_params=pltpu.CompilerParams(vmem_limit_bytes=KERNEL_VMEM),
        cost_estimate=SMALL_COST,
    )(
        parents, segs, queries, grads, attended, stats, cosine, sine, keys_values,
        *([earlier] if last else []),
    )


def in_turn(per, count, step):
    for i in range(count):
        pl.when(pl.program_id(1) // per == i)(functools.partial(step, i))


def gate_kernel(per, parts, pieces, rows, *refs):
    gates, ups = refs[: parts * pieces], refs[parts * pieces : 2 * parts * pieces]
    activated, gate_slope, up_slope = refs[2 * parts * pieces :]
    depth = gates[0].shape[0]

    def product(weights, i):
        return sum(
            nn_dot(rows[:, k * depth : (k + 1) * depth], weights[k * pieces + i][...])
            for k in range(parts)
        )

    def step(i):
        gate, up = product(gates, i), product(ups, i)
        sigmoid = 1.0 / (1.0 + jnp.exp(-gate))
        silu = gate * sigmoid
        activated[...] = (silu * up).astype(jnp.bfloat16)
        gate_slope[...] = up * sigmoid * (1.0 + gate * (1.0 - sigmoid))
        up_slope[...] = silu

    in_turn(per, pieces, step)


def gate_back_kernel(per, parts, pieces, *refs):
    grads, weights = refs[:parts], refs[parts : parts + parts * pieces]
    gate_slope, up_slope, grad_gate, grad_up = refs[parts + parts * pieces :]

    def step(i):
        grad = sum(nt_dot(grads[k][...], weights[k * pieces + i][...]) for k in range(parts))
        grad_gate[...] = (grad * gate_slope[...]).astype(jnp.bfloat16)
        grad_up[...] = (grad * up_slope[...]).astype(jnp.bfloat16)

    in_turn(per, pieces, step)


def down_kernel(per, parts, pieces, acts, *refs):
    weights, out = refs[:-1], refs[-1]
    depth = weights[0].shape[0]

    def step(k):
        total = sum(
            nn_dot(acts[:, i * depth : (i + 1) * depth], weights[k * pieces + i][...])
            for i in range(pieces)
        )
        out[...] = total.astype(jnp.bfloat16)

    in_turn(per, parts, step)


def pair_kernel(per, parts, pieces, first, second, *refs):
    gates, ups, out = refs[: parts * pieces], refs[parts * pieces : -1], refs[-1]
    depth = gates[0].shape[1]

    def step(k):
        total = 0.0
        for i in range(pieces):
            columns = slice(i * depth, (i + 1) * depth)
            total = total + nt_dot(first[:, columns], gates[k * pieces + i][...])
            total = total + nt_dot(second[:, columns], ups[k * pieces + i][...])
        out[...] = total.astype(jnp.bfloat16)

    in_turn(per, parts, step)


def wide_call(kernel, whole, weights, tiled, axis, by_piece, outs):
    parts, pieces = len(weights[0]), len(weights[0][0])
    shape = weights[0][0][0].shape
    groups = pieces if by_piece else parts
    tile = (min(whole[0].shape[0], 1024), min(shape[axis], 256))
    per = shape[axis] // tile[1]
    count, cols = whole[0].shape[0], groups * shape[axis]

    def piece_spec(k, i):
        group = i if by_piece else k

        def place(row, col):
            at = jnp.clip(col - group * per, 0, per - 1)
            return (0, at) if axis == 1 else (at, 0)

        return pl.BlockSpec((shape[0], tile[1]) if axis == 1 else (tile[1], shape[1]), place)

    tile_spec = pl.BlockSpec(tile, lambda row, col: (row, col))
    flat = [v for weight in weights for row in weight for v in row]
    return pl.pallas_call(
        functools.partial(kernel, per, parts, pieces),
        grid=(count // tile[0], groups * per),
        in_specs=[pl.BlockSpec((tile[0], v.shape[1]), lambda row, col: (row, 0)) for v in whole]
        + [piece_spec(k, i) for _ in weights for k in range(parts) for i in range(pieces)]
        + [tile_spec] * len(tiled),
        out_specs=[tile_spec] * len(outs),
        out_shape=[jax.ShapeDtypeStruct((count, cols), t) for t in outs],
        compiler_params=pltpu.CompilerParams(vmem_limit_bytes=KERNEL_VMEM),
        cost_estimate=SMALL_COST,
    )(*whole, *flat, *tiled)


def gate_forward(rows, gates, ups):
    outs = (jnp.bfloat16, jnp.float32, jnp.float32)
    return wide_call(gate_kernel, [rows], [gates, ups], [], 1, True, outs)


def gate_backward(grads, downs, gate_slope, up_slope):
    outs = (jnp.bfloat16, jnp.bfloat16)
    return wide_call(gate_back_kernel, grads, [downs], [gate_slope, up_slope], 0, True, outs)


def down_forward(acts, downs):
    return wide_call(down_kernel, [acts], [downs], [], 1, False, (jnp.bfloat16,))[0]


def pair_product(grad_gate, grad_up, gates, ups):
    whole = [grad_gate, grad_up]
    return wide_call(pair_kernel, whole, [gates, ups], [], 0, False, (jnp.bfloat16,))[0]


def row_norm(value):
    inverse = lax.rsqrt(jnp.mean(value * value, axis=-1, keepdims=True) + norm_eps)
    return value * inverse, inverse


def norm_back(grad, normed, inverse, gain):
    scaled = grad * gain
    return inverse * (scaled - normed * jnp.mean(scaled * normed, axis=-1, keepdims=True))


def silu_parts(gate_pre):
    sigmoid = jax.nn.sigmoid(gate_pre)
    return sigmoid, gate_pre * sigmoid


def halves(value, count):
    part = value.shape[1] // count
    return [value[:, i * part : (i + 1) * part] for i in range(count)]


def joined(pieces, outer, inner):
    return jnp.concatenate([jnp.concatenate(row, axis=inner) for row in pieces], axis=outer)


def matmul(left, right):
    return jnp.dot(left, right, preferred_element_type=jnp.float32)


def matmul_turned(left, right):
    return nt_dot(left, right)


def turned_matmul(left, right):
    return lax.dot_general(
        left, right, (((0,), (0,)), ((), ())), preferred_element_type=jnp.float32
    )


def sent_groups(value):
    size = lax.axis_size("y")
    place = lax.axis_index("y")
    width = value.shape[1] // size
    pieces = []
    for k in range(size):
        start = lax.rem(place + k, size) * width
        piece = lax.dynamic_slice_in_dim(value, start, width, 1)
        pieces.append(rotated(piece, "y", k) if k else piece)
    return pieces


def in_groups(pieces):
    size = len(pieces)
    place = lax.axis_index("y")
    return jnp.concatenate(
        [
            lax.select_n(place, *[pieces[(j - i) % size] for i in range(size)])
            for j in range(size)
        ],
        axis=1,
    )


def turned_back(value, cosine_table, sine_table):
    first, second = halves(value, 2)
    return jnp.concatenate(
        [
            first * cosine_table + second * sine_table,
            second * cosine_table - first * sine_table,
        ],
        axis=1,
    )


def tensor_gather(value):
    rows = jnp.stack(natural_pieces(relative_pieces(value, "x"), "x"))
    rows = jnp.stack(natural_pieces(relative_pieces(rows, "c"), "c"), axis=1)
    return rows.reshape(-1, value.shape[1])


def tensor_sum(part, rows):
    x_size, c_size = lax.axis_size("x"), lax.axis_size("c")
    blocks = part.reshape(x_size, c_size, rows, -1)
    c_place, x_place = lax.axis_index("c"), lax.axis_index("x")

    def block(value, place, k, axis):
        size = value.shape[axis]
        return lax.dynamic_index_in_dim(
            value, lax.rem(place - k + size, size), axis, keepdims=False
        )

    mine = summed_pieces([block(blocks, c_place, k, 1) for k in range(c_size)], "c")
    mine = mine.astype(jnp.bfloat16)
    return summed_pieces([block(mine, x_place, k, 0) for k in range(x_size)], "x")


def local(
    tokens,
    norm_gain,
    q_weight,
    key_matrix,
    value_matrix,
    o_weight,
    mlp_gain,
    gate_weight,
    up_weight,
    down_weight,
    parents,
    out_grad,
):
    z_size, y_size, x_size = (lax.axis_size(name) for name in ("z", "y", "x"))
    tensor_size = x_size * lax.axis_size("c")
    low = jnp.bfloat16
    local_rows, width = tokens.shape
    group_rows = local_rows * tensor_size
    kv_cols = key_matrix.shape[1]
    kv_local = kv_cols // HEAD_SIZE
    q_cols = q_weight.shape[1]
    own_width = norm_gain.shape[0]

    own_tokens = relative_columns(tokens)
    own_grad = relative_columns(out_grad).astype(jnp.float32)
    group_tokens = tensor_gather(own_tokens)

    both_gains = jnp.concatenate([norm_gain, mlp_gain])
    both_gains = jnp.pad(both_gains, (0, -both_gains.shape[0] % (2 * kv_cols)))
    key_heads, value_heads = halves(key_matrix, kv_local), halves(value_matrix, kv_local)
    kv_shard = jnp.concatenate(
        [
            jnp.concatenate([v for kv in zip(key_heads, value_heads) for v in kv], axis=1),
            both_gains.reshape(-1, 2 * kv_cols),
        ],
        axis=0,
    )
    kv_z = gathered(kv_shard, "z")
    q_z = lax.all_gather(q_weight, "z", axis=0, tiled=True)
    kv_z, o_weight, group_tokens = together(kv_z, o_weight, group_tokens)

    depth = segment_depth(parents)
    seg_count = group_rows // SEG
    z_place, y_place = lax.axis_index("z"), lax.axis_index("y")
    sources = [lax.rem(y_place - k + y_size, y_size) for k in range(y_size)]
    segs = jnp.concatenate(
        [
            (z_place * y_size + source) * seg_count + jnp.arange(seg_count, dtype=jnp.int32)
            for source in sources
        ]
    )
    seg_ids = jnp.arange(depth.shape[0], dtype=jnp.int32)
    seg_depth = jnp.sum(jnp.where(segs[:, None] == seg_ids[None, :], depth[None, :], 0), axis=1)
    position = (seg_depth[:, None] * SEG + jnp.arange(SEG, dtype=jnp.int32)[None, :]).reshape(-1)
    cosine_table, sine_table = rope_tables(position, HEAD_SIZE)
    cosine_lanes = jnp.tile(cosine_table, (1, 4))
    sine_lanes = jnp.tile(sine_table, (1, 4))
    key_lanes = jnp.arange(LANES) < HEAD_SIZE
    cosine_keys = jnp.where(key_lanes, cosine_lanes[:group_rows], 1.0)
    sine_keys = jnp.where(key_lanes, sine_lanes[:group_rows], 0.0)

    o_z = lax.all_gather(o_weight, "z", axis=0)
    kv_zy = relative_pieces(kv_z, "y")
    kv_weights = [v[:, :own_width].reshape(-1, 2 * kv_cols) for v in kv_zy]
    gains = [
        v[:, own_width:].reshape(z_size, -1)[:, : 2 * own_width].reshape(z_size, 2, own_width)
        for v in kv_zy
    ]
    gains = jnp.stack(gains).astype(jnp.float32)
    gain_one, gain_two = gains[:, :, 0].reshape(-1), gains[:, :, 1].reshape(-1)
    inputs = own_tokens.astype(jnp.float32)
    normed_one, inv_one = row_norm(inputs)
    group_normed, _ = row_norm(group_tokens.astype(jnp.float32))
    rows_one = (group_normed * gain_one).astype(low)
    kv_rows = project(rows_one, kv_weights, cosine_keys, sine_keys)
    kv_swapped = jnp.stack(natural_pieces(sent_groups(kv_rows), "y"))
    q_z, kv_swapped = together(q_z, kv_swapped)

    all_kv = gathered(kv_swapped, "z").reshape(-1, SEG, LANES)
    q_weights = relative_pieces(q_z, "y")
    q_weights, o_z = together(q_weights, o_z)
    o_zy = relative_pieces(joined_columns(o_z), "y")
    query_rows = project(rows_one, q_weights, cosine_lanes[:group_rows], sine_lanes[:group_rows])
    queries = sent_groups(query_rows)
    all_kv, queries, gate_weight, up_weight = together(all_kv, queries, gate_weight, up_weight)

    gate_z = exchanged(column_blocks(gate_weight, z_size), "z")
    seg_lists = jnp.split(segs, y_size)
    attends = [None] * y_size
    for k in range(y_size - 1, 0, -1):
        attends[k] = attend(parents, seg_lists[k], queries[k], all_kv)
    queries[0], attends, o_zy = together(queries[0], attends, o_zy)
    returned = [rotated(attends[k][0].astype(low), "y", -k) for k in range(1, y_size)]
    attends[0] = attend(parents, seg_lists[0], queries[0], all_kv)
    attn_low = in_groups([attends[0][0].astype(low), *returned])
    attn_low, o_zy, gate_z, up_weight = together(attn_low, o_zy, gate_z, up_weight)

    o_full = jnp.concatenate(o_zy, axis=1)
    attn_part = matmul(attn_low, o_full).astype(low)
    attn_mine = tensor_sum(attn_part, local_rows)
    up_z = exchanged(column_blocks(up_weight, z_size), "z")
    gate_zy = relative_pieces(gate_z.reshape(z_size * own_width, -1), "y")
    up_z, gate_zy, attn_mine, down_weight = together(up_z, gate_zy, attn_mine, down_weight)

    middle = inputs + branch_scale * attn_mine
    normed_two, inv_two = row_norm(middle)
    hidden_two = (normed_two * gain_two).astype(low)
    rows_two = lax.all_gather(hidden_two, ("z", "c"), axis=0, tiled=True)
    up_z = up_z.reshape(z_size * own_width, -1)
    up_zy = relative_pieces(up_z, "y")
    gate_zx = relative_pieces(gate_zy[0], "x")
    gate_zx, up_zy, up_z = together(gate_zx, up_zy, up_z)
    up_zx = relative_pieces(up_z, "x")
    gate_far = [relative_pieces(v, "y")[1:] for v in gate_zx[1:]]
    rows_two, up_zx, gate_far, down_weight = together(rows_two, up_zx, gate_far, down_weight)

    down_z = joined_columns(exchanged(down_weight.reshape(z_size, -1, own_width), "z"))
    half = own_width * z_size // 2
    upper = [[rotated(v[:half], "x", i) for i in range(1, x_size)] for v in up_zy[1:]]
    lower = [[rotated(v[half:], "y", k) for v in up_zx[1:]] for k in range(1, y_size)]
    down_z, upper, lower = together(down_z, upper, lower)
    up_far = [
        [jnp.concatenate(pair, axis=0) for pair in zip(*rows)] for rows in zip(upper, lower)
    ]
    gates = [gate_zx] + [
        [gate_zy[k], *[far[k - 1] for far in gate_far]] for k in range(1, y_size)
    ]
    ups = [up_zx] + [[up_zy[k], *up_far[k - 1]] for k in range(1, y_size)]

    grad_mlp = (branch_scale * own_grad).astype(low)
    grad_mlp_rows = lax.all_gather(grad_mlp, ("z", "c"), axis=0, tiled=True)
    down_zy = relative_pieces(down_z, "y")
    down_zx = relative_pieces(down_z, "x")
    activated, gate_slope, up_slope = gate_forward(rows_two, gates, ups)
    down_zy, down_zx, activated, gate_slope, up_slope = together(
        down_zy, down_zx, activated, gate_slope, up_slope
    )
    half = down_z.shape[0] // 2
    upper = [[rotated(v[:half], "x", i) for i in range(1, x_size)] for v in down_zy[1:]]
    lower = [[rotated(v[half:], "y", k) for v in down_zx[1:]] for k in range(1, y_size)]
    upper, lower, grad_mlp_rows = together(upper, lower, grad_mlp_rows)
    down_far = [
        [jnp.concatenate(pair, axis=0) for pair in zip(*rows)] for rows in zip(upper, lower)
    ]
    downs = [down_zx] + [[down_zy[k], *down_far[k - 1]] for k in range(1, y_size)]
    grad_mlp_parts = halves(grad_mlp_rows, y_size)
    mlp_part = down_forward(activated, downs)
    mlp_mine = lax.psum_scatter(mlp_part, ("z", "c"), scatter_dimension=0, tiled=True)
    acts = halves(activated, x_size)
    down_far = [
        summed_pieces([turned_matmul(act, grad) for grad in grad_mlp_parts], "y").astype(low)
        for act in acts[1:]
    ]
    grad_gate_act, grad_up_act = gate_backward(grad_mlp_parts, downs, gate_slope, up_slope)
    grad_gate_act, grad_up_act, down_far = together(grad_gate_act, grad_up_act, down_far)

    down_near = summed_pieces([turned_matmul(acts[0], grad) for grad in grad_mlp_parts], "y")
    grad_down_z = summed_pieces([down_near, *down_far], "x").astype(low)
    input_part = pair_product(grad_gate_act, grad_up_act, gates, ups)
    input_part, grad_down_z, rows_two = together(input_part, grad_down_z, rows_two)

    grad_rows_two = lax.psum_scatter(input_part, ("z", "c"), scatter_dimension=0, tiled=True)
    rows_parts = halves(rows_two, y_size)
    gate_parts, up_parts = halves(grad_gate_act, x_size), halves(grad_up_act, x_size)
    gate_far = [
        summed_pieces([turned_matmul(a, b) for a in rows_parts], "y").astype(low)
        for b in gate_parts[1:]
    ]
    up_far = [
        summed_pieces([turned_matmul(a, b) for b in up_parts], "x").astype(low)
        for a in rows_parts[1:]
    ]
    gate_far, up_far = together(gate_far, up_far)
    gate_near = summed_pieces([turned_matmul(a, gate_parts[0]) for a in rows_parts], "y")
    grad_gate_z = summed_pieces([gate_near, *gate_far], "x").astype(low)
    grad_rows_two, grad_gate_z, up_far, mlp_mine = together(
        grad_rows_two, grad_gate_z, up_far, mlp_mine
    )

    mixed = natural_columns((middle + branch_scale * mlp_mine.astype(jnp.float32)).astype(low))
    grad_rows_two = grad_rows_two.astype(jnp.float32)
    gain_two_part = jnp.sum(grad_rows_two * normed_two, axis=0)
    grad_middle = own_grad + norm_back(grad_rows_two, normed_two, inv_two, gain_two)
    grad_attn = (branch_scale * grad_middle).astype(low)
    grad_gate = exchanged(grad_gate_z.reshape(z_size, own_width, -1), "z")
    up_far = [rotated(v, "y", -1 - i) for i, v in enumerate(up_far)]
    grad_attn_rows = tensor_gather(grad_attn)
    grad_attn_rows, up_far, grad_down_z = together(grad_attn_rows, up_far, grad_down_z)

    grad_heads = sent_groups(matmul_turned(grad_attn_rows, o_full).astype(low))
    up_near = summed_pieces([turned_matmul(rows_parts[0], b) for b in up_parts], "x")
    grad_up_z = sum([v.astype(jnp.float32) for v in up_far], up_near).astype(low)
    grad_heads, grad_gate, grad_down_z, grad_attn_rows = together(
        grad_heads, grad_gate, grad_down_z, grad_attn_rows
    )
    grad_down = exchanged(column_blocks(grad_down_z, z_size), "z")
    grad_o_y = summed_pieces(
        [turned_matmul(attn_low, v) for v in halves(grad_attn_rows, y_size)], "y"
    ).astype(low)
    cosines, sines = jnp.split(cosine_lanes, y_size), jnp.split(sine_lanes, y_size)
    grad_queries, sums = [None] * y_size, None
    for k in range(y_size - 1, 0, -1):
        grad_queries[k], sums = attend_back(
            parents, seg_lists[k], queries[k], grad_heads[k], *attends[k], cosines[k], sines[k],
            all_kv, sums,
        )
    grad_queries[1:], sums, grad_o_y, grad_up_z = together(
        grad_queries[1:], sums, grad_o_y, grad_up_z
    )
    grad_o = lax.psum_scatter(
        column_blocks(grad_o_y, z_size), "z", scatter_dimension=0, tiled=True
    )[0]
    returned = [rotated(v, "y", -k) for k, v in enumerate(grad_queries[1:], 1)]
    grad_queries[0], grad_kv = attend_back(
        parents, seg_lists[0], queries[0], grad_heads[0], *attends[0], cosines[0], sines[0],
        all_kv, sums,
    )
    grad_queries = in_groups([grad_queries[0], *returned])
    grad_queries, grad_kv, grad_down, grad_up_z = together(
        grad_queries, grad_kv, grad_down, grad_up_z
    )

    def owned_rows(left, right):
        return summed_pieces([turned_matmul(v, right) for v in halves(left, y_size)], "y").astype(
            low
        )

    kv_mine = summed_blocks(grad_kv.reshape(z_size, y_size * seg_count, LANES, SEG), "z")
    grad_q_y = owned_rows(rows_one, grad_queries)
    q_full = jnp.concatenate(q_weights, axis=0)
    query_part = matmul_turned(grad_queries, q_full)
    kv_mine, query_part, grad_q_y, grad_up_z = together(kv_mine, query_part, grad_q_y, grad_up_z)

    grad_q = lax.psum_scatter(
        grad_q_y.reshape(z_size, own_width, -1), "z", scatter_dimension=0, tiled=True
    )[0]
    grad_up = exchanged(grad_up_z.reshape(z_size, own_width, -1), "z")
    kv_mine = kv_mine.transpose(0, 2, 1).reshape(y_size, group_rows, LANES)
    kv_mine = [lax.dynamic_index_in_dim(kv_mine, s, 0, keepdims=False) for s in sources]
    kv_mine = jnp.concatenate(kv_mine, axis=0)
    grad_keys = turned_back(kv_mine[:, :HEAD_SIZE], cosine_table, sine_table)
    grad_kv_rows = jnp.concatenate([grad_keys, kv_mine[:, HEAD_SIZE:]], axis=1).astype(low)
    grad_kv_rows = in_groups(
        [grad_kv_rows[:group_rows]]
        + [
            rotated(grad_kv_rows[k * group_rows : (k + 1) * group_rows], "y", -k)
            for k in range(1, y_size)
        ]
    )
    kv_full = jnp.concatenate(kv_weights, axis=0)
    input_one = (query_part + matmul_turned(grad_kv_rows, kv_full)).astype(low)
    grad_kv_y = owned_rows(rows_one, grad_kv_rows)
    grad_rows_one = tensor_sum(input_one, local_rows)
    grad_kv_y, grad_rows_one = together(grad_kv_y, grad_rows_one)
    grad_kv_weight = summed_blocks(grad_kv_y.reshape(z_size, own_width, -1), "z")
    grad_q, grad_o = grad_q.astype(jnp.float32), grad_o.astype(jnp.float32)
    gain_one_part = jnp.sum(grad_rows_one * normed_one, axis=0)
    grad_inputs = grad_middle + norm_back(grad_rows_one, normed_one, inv_one, gain_one)
    grad_tokens = natural_columns(grad_inputs.astype(low))
    grad_gate, grad_up = (joined_columns(v).astype(jnp.float32) for v in (grad_gate, grad_up))
    grad_down = grad_down.reshape(-1, own_width).astype(jnp.float32)

    gain_parts = jnp.stack([gain_one_part, gain_two_part], axis=0)
    gain_parts = natural_columns(gain_parts).reshape(2, z_size * y_size, 1, own_width)
    gain_parts = jnp.broadcast_to(
        gain_parts, (2, z_size * y_size, tensor_size, own_width)
    ).reshape(2, -1, own_width).transpose(1, 0, 2)
    gain_sums = jnp.sum(exchanged(gain_parts, ("z", "y", "x", "c")), axis=0)
    grad_heads = halves(grad_kv_weight, 2 * kv_local)
    return (
        mixed,
        grad_tokens,
        gain_sums[0],
        grad_q,
        jnp.concatenate(grad_heads[::2], axis=1),
        jnp.concatenate(grad_heads[1::2], axis=1),
        grad_o,
        gain_sums[1],
        grad_gate,
        grad_up,
        grad_down,
    )


def solution(mesh):
    dp_size, tensor_size = mesh.shape["dp"], mesh.shape["tensor"]
    fine = jax.sharding.Mesh(
        mesh.devices.reshape(dp_size // 2, 2, tensor_size // 2, 2), ("z", "y", "x", "c")
    )
    dp, tensor = ("z", "y"), ("x", "c")
    tokens = P(dp + tensor, None)
    rows = P(dp, tensor)
    columns = P(tensor, dp)
    in_specs = (
        tokens,
        P(dp),
        rows,
        rows,
        rows,
        columns,
        P(dp),
        rows,
        rows,
        columns,
        P(),
        tokens,
    )
    out_specs = (
        tokens,
        tokens,
        P(dp),
        rows,
        rows,
        rows,
        columns,
        P(dp),
        rows,
        rows,
        columns,
    )
    return jax.shard_map(local, mesh=fine, in_specs=in_specs, out_specs=out_specs, check_vma=False)
```

```python
import functools

import jax
import jax.numpy as jnp
from jax import lax
from jax.experimental import pallas as pl
from jax.experimental.pallas import tpu as pltpu
from jax.sharding import PartitionSpec as P

HEAD_SIZE = 64
SEG = 256
MAX_STEPS = 9
LANES = 2 * HEAD_SIZE
KERNEL_VMEM = 56 * 2**20
SMALL_COST = pl.CostEstimate(flops=2**28, bytes_accessed=2**18, transcendentals=0)


attn_scale = 0.015625
branch_scale = 0.22
norm_eps = 1e-05
rope_base = 10000000.0
masked_score = -1e30


def segment_depth(parents):
    seg_total = parents.shape[0]
    seg_ids = jnp.arange(seg_total, dtype=jnp.int32)
    reach = (parents[:, None] == seg_ids[None, :]) | (seg_ids[:, None] == seg_ids[None, :])
    reach = reach.astype(jnp.float32)
    for doubling in range(4):
        reach = jnp.minimum(jnp.dot(reach, reach, preferred_element_type=jnp.float32), 1.0)
    return jnp.sum(reach, axis=1).astype(jnp.int32) - 1


def rope_tables(position, head_dim):
    half_dim = head_dim // 2
    exponent = jnp.arange(half_dim, dtype=jnp.float32) * (2.0 / head_dim)
    inverse = jnp.power(rope_base, -exponent)
    angles = position.astype(jnp.float32)[:, None] * inverse[None, :]
    return (jnp.cos(angles), jnp.sin(angles))


def rotated(value, axis, step):
    size = lax.axis_size(axis)
    return lax.ppermute(value, axis, [(i, (i + step) % size) for i in range(size)])


def relative_pieces(value, axis):
    return [value] + [rotated(value, axis, k) for k in range(1, lax.axis_size(axis))]


def natural_pieces(pieces, axis):
    size = len(pieces)
    place = lax.axis_index(axis)
    return [
        lax.select_n(place, *[pieces[(i - j) % size] for i in range(size)]) for j in range(size)
    ]


def gathered(value, axis):
    size = lax.axis_size(axis)
    copies = jnp.broadcast_to(value[None], (size, *value.shape))
    return lax.all_to_all(copies, axis, 0, 0, tiled=True)


def exchanged(blocks, axis):
    return lax.all_to_all(blocks, axis, 0, 0, tiled=True)


def summed_pieces(pieces, axis):
    sent = [rotated(pieces[k].astype(jnp.bfloat16), axis, -k) for k in range(1, len(pieces))]
    total = pieces[0].astype(jnp.float32)
    for value in sent:
        total = total + value.astype(jnp.float32)
    return total


def summed_blocks(blocks, axis):
    return jnp.sum(exchanged(blocks.astype(jnp.bfloat16), axis).astype(jnp.float32), axis=0)


def column_blocks(value, count):
    return value.reshape(value.shape[0], count, -1).transpose(1, 0, 2)


def joined_columns(blocks):
    return blocks.transpose(1, 0, 2).reshape(blocks.shape[1], -1)


def relative_columns(value):
    size = lax.axis_size("y")
    place = lax.axis_index("y")
    rows = value.shape[0]
    split = value.reshape(rows, lax.axis_size("z"), size, -1)
    flat = [split[:, :, i].reshape(rows, -1) for i in range(size)]
    return jnp.concatenate(
        [
            lax.select_n(place, *[flat[(i - k) % size] for i in range(size)])
            for k in range(size)
        ],
        axis=1,
    )


def natural_columns(value):
    size = lax.axis_size("y")
    rows = value.shape[0]
    split = value.reshape(rows, size, lax.axis_size("z"), -1)
    parts = natural_pieces([split[:, k] for k in range(size)], "y")
    return jnp.stack(parts, axis=2).reshape(rows, -1)


def together(*values):
    return lax.optimization_barrier(values)


def after(value, *others):
    return lax.optimization_barrier((value, *others))[0]


def ancestor_count(parents, seg):
    def climb(step, state):
        current, count = state
        above = parents[current]
        return above, count + jnp.where(above != current, 1, 0)

    return lax.fori_loop(0, MAX_STEPS, climb, (seg, jnp.int32(1)))[1]


def left_lanes(shape):
    return lax.broadcasted_iota(jnp.int32, shape, 1) < HEAD_SIZE


def stacked_heads(pairs, to_left):
    left = left_lanes(pairs[0].shape)
    stack = []
    for pair in pairs:
        swapped = pltpu.roll(pair, HEAD_SIZE, 1)
        for head in (pair, swapped) if to_left else (swapped, pair):
            stack.append(jnp.where(left, head, 0.0) if to_left else jnp.where(left, 0.0, head))
    return jnp.concatenate(stack, axis=0)


def unstacked_heads(stack, from_left):
    left = left_lanes((SEG, 2 * HEAD_SIZE))
    pairs = []
    for first in range(0, stack.shape[0], 2 * SEG):
        even, odd = stack[first : first + SEG], stack[first + SEG : first + 2 * SEG]
        if from_left:
            odd = pltpu.roll(odd, HEAD_SIZE, 1)
        else:
            even = pltpu.roll(even, HEAD_SIZE, 1)
        pairs.append(jnp.where(left, even, odd))
    return pairs


def turned(value, cosine, sine, direction):
    half = HEAD_SIZE // 2
    lane = lax.broadcasted_iota(jnp.int32, value.shape, 1)
    first = lax.rem(lane, HEAD_SIZE) < half
    ahead = pltpu.roll(value, LANES - half, 1)
    behind = pltpu.roll(value, half, 1)
    signed = sine * direction
    return value * cosine + jnp.where(first, -ahead * signed, behind * signed)


def nt_dot(left, right):
    return lax.dot_general(
        left, right, (((1,), (1,)), ((), ())), preferred_element_type=jnp.float32
    )


def nn_dot(left, right):
    return lax.dot_general(
        left, right, (((1,), (0,)), ((), ())), preferred_element_type=jnp.float32
    )


def causal_tile(rows):
    query = lax.rem(lax.broadcasted_iota(jnp.int32, (rows, SEG), 0), SEG)
    return lax.broadcasted_iota(jnp.int32, (rows, SEG), 1) <= query


def lane_blocks(ref):
    return [ref[:, at : at + LANES] for at in range(0, ref.shape[1], LANES)]


def project_kernel(parts, rows, *refs):
    weights, (cosine, sine, out) = refs[:parts], refs[parts:]
    depth = weights[0].shape[0]
    product = sum(nn_dot(rows[:, i * depth : (i + 1) * depth], w[...]) for i, w in enumerate(weights))
    cos, sin = cosine[...], sine[...]
    for at in range(0, product.shape[1], LANES):
        block = turned(product[:, at : at + LANES], cos, sin, 1.0)
        out[:, at : at + LANES] = block.astype(jnp.bfloat16)


def project(rows, weights, cosine, sine):
    count, width = rows.shape
    depth, cols = weights[0].shape
    step = 2 * LANES
    table = pl.BlockSpec((count, LANES), lambda j: (0, 0))
    return pl.pallas_call(
        functools.partial(project_kernel, len(weights)),
        grid=(cols // step,),
        in_specs=[pl.BlockSpec((count, width), lambda j: (0, 0))]
        + [pl.BlockSpec((depth, step), lambda j: (0, j))] * len(weights)
        + [table, table],
        out_specs=pl.BlockSpec((count, step), lambda j: (0, j)),
        out_shape=jax.ShapeDtypeStruct((count, cols), jnp.bfloat16),
        compiler_params=pltpu.CompilerParams(vmem_limit_bytes=KERNEL_VMEM),
        cost_estimate=SMALL_COST,
    )(rows, *weights, cosine, sine)


def attend_kernel(parents, segs, queries, keys_values, out, stats, out_low, scores):
    seg = segs[pl.program_id(0)]
    count = ancestor_count(parents, seg)
    pairs = [block.astype(jnp.float32) * attn_scale for block in lane_blocks(queries)]
    stack = stacked_heads(pairs, True).astype(jnp.bfloat16)
    rows = stack.shape[0]

    first = jnp.where(causal_tile(rows), nt_dot(stack, keys_values[seg]), masked_score)
    scores[0] = first

    def folded(tile):
        return jnp.maximum(tile[:, :LANES], tile[:, LANES:])

    def measure(step, state):
        current, top = state
        current = parents[current]
        tile = nt_dot(stack, keys_values[current])
        scores[step] = tile
        return current, jnp.maximum(top, folded(tile))

    top = lax.fori_loop(1, count, measure, (seg, folded(first)))[1]
    row_max = jnp.max(top, axis=1, keepdims=True)
    left = left_lanes((SEG, LANES))

    def gather(step, state):
        current, mixed = state
        terms = jnp.exp(scores[step] - row_max).astype(jnp.bfloat16)
        tile = jnp.where(left, jnp.ones((SEG, LANES), jnp.bfloat16), keys_values[current])
        return parents[current], mixed + nn_dot(terms, tile)

    start = (seg, jnp.zeros((rows, LANES), jnp.float32))
    mixed = lax.fori_loop(0, count, gather, start)[1]
    total = mixed[:, :1]
    mixed = mixed / total
    stats[0] = row_max + jnp.log(total)
    for place, pair in enumerate(unstacked_heads(mixed, False)):
        out[:, place * LANES : (place + 1) * LANES] = pair
        out_low[:, place * LANES : (place + 1) * LANES] = pair.astype(jnp.bfloat16)


def attend_back_kernel(
    parents, segs, queries, grads, attended, stats, cosine, sine, keys_values, *refs
):
    earlier, (grad_queries, grad_kv, kv_sum) = refs[:-3], refs[-3:]
    seg = segs[pl.program_id(0)]
    count = ancestor_count(parents, seg)

    @pl.when(pl.program_id(0) == 0)
    def _():
        kv_sum[...] = earlier[0][...] if earlier else jnp.zeros_like(kv_sum)

    query_pairs = [block.astype(jnp.float32) * attn_scale for block in lane_blocks(queries)]
    grad_pairs = [block.astype(jnp.float32) for block in lane_blocks(grads)]
    left = left_lanes((SEG, LANES))
    deltas = []
    for pair, out in zip(grad_pairs, lane_blocks(attended)):
        product = pair * out
        deltas.append(jnp.sum(jnp.where(left, product, 0.0), axis=1, keepdims=True))
        deltas.append(jnp.sum(jnp.where(left, 0.0, product), axis=1, keepdims=True))
    delta = jnp.concatenate(deltas, axis=0)
    query_wide = stacked_heads(query_pairs, True)
    grad_wide = stacked_heads(grad_pairs, False)
    query_stack, grad_stack = query_wide.astype(jnp.bfloat16), grad_wide.astype(jnp.bfloat16)
    query_turned = query_wide.T.astype(jnp.bfloat16)
    grad_turned = grad_wide.T.astype(jnp.bfloat16)
    log_total = stats[0]
    rows = query_stack.shape[0]

    def visit(current, total, diagonal):
        tile_kv = keys_values[current]
        tile = nt_dot(query_stack, tile_kv)
        if diagonal:
            tile = jnp.where(causal_tile(rows), tile, masked_score)
        probs = jnp.exp(tile - log_total)
        grad_probs = nt_dot(grad_stack, tile_kv)
        grad_tile = (probs * (grad_probs - delta)).astype(jnp.bfloat16)
        kv_sum[current] += nn_dot(query_turned, grad_tile) + nn_dot(
            grad_turned, probs.astype(jnp.bfloat16)
        )
        return total + nn_dot(grad_tile, tile_kv)

    total = visit(seg, jnp.zeros((rows, LANES), jnp.float32), True)

    def climb(step, state):
        current, total = state
        current = parents[current]
        return current, visit(current, total, False)

    total = lax.fori_loop(1, count, climb, (seg, total))[1]
    cos, sin = cosine[...], sine[...]
    for place, pair in enumerate(unstacked_heads(total * attn_scale, True)):
        grad_queries[:, place * LANES : (place + 1) * LANES] = turned(
            pair, cos, sin, -1.0
        ).astype(jnp.bfloat16)

    @pl.when(pl.program_id(0) == pl.num_programs(0) - 1)
    def _():
        grad_kv[...] = kv_sum[...].astype(grad_kv.dtype)


def attention_specs(cols, seg_total):
    block = pl.BlockSpec((SEG, cols), lambda s: (s, 0))
    table = pl.BlockSpec((SEG, LANES), lambda s: (s, 0))
    whole = pl.BlockSpec((seg_total, SEG, LANES), lambda s: (0, 0, 0))
    rows = SEG * (cols // HEAD_SIZE)
    stat = pl.BlockSpec((1, rows, 1), lambda s: (s, 0, 0))
    return block, table, whole, rows, stat, pl.BlockSpec(memory_space=pltpu.SMEM)


def attend(parents, segs, queries, keys_values):
    count, cols = queries.shape
    block, table, whole, rows, stat, scalar = attention_specs(cols, keys_values.shape[0])
    steps = count // SEG
    return pl.pallas_call(
        attend_kernel,
        grid=(steps,),
        in_specs=[scalar, scalar, block, whole],
        out_specs=[block, stat, block],
        out_shape=[
            jax.ShapeDtypeStruct((count, cols), jnp.float32),
            jax.ShapeDtypeStruct((steps, rows, 1), jnp.float32),
            jax.ShapeDtypeStruct((count, cols), jnp.bfloat16),
        ],
        scratch_shapes=[pltpu.VMEM((MAX_STEPS + 1, rows, SEG), jnp.float32)],
        compiler_params=pltpu.CompilerParams(vmem_limit_bytes=KERNEL_VMEM),
        cost_estimate=SMALL_COST,
    )(parents, segs, queries, keys_values)


def attend_back(
    parents, segs, queries, grads, attended, stats, cosine, sine, keys_values, earlier=None
):
    count, cols = queries.shape
    seg_total = keys_values.shape[0]
    block, table, whole, rows, stat, scalar = attention_specs(cols, seg_total)
    sums = pl.BlockSpec((seg_total, LANES, SEG), lambda s: (0, 0, 0))
    last = earlier is not None
    sum_type = jnp.bfloat16 if last else jnp.float32
    return pl.pallas_call(
        attend_back_kernel,
        grid=(count // SEG,),
        in_specs=[scalar, scalar, block, block, block, stat, table, table, whole] + [sums] * last,
        out_specs=[block, sums],
        out_shape=[
            jax.ShapeDtypeStruct((count, cols), jnp.bfloat16),
            jax.ShapeDtypeStruct((seg_total, LANES, SEG), sum_type),
        ],
        scratch_shapes=[pltpu.VMEM((seg_total, LANES, SEG), jnp.float32)],
        compiler_params=pltpu.CompilerParams(vmem_limit_bytes=KERNEL_VMEM),
        cost_estimate=SMALL_COST,
    )(
        parents, segs, queries, grads, attended, stats, cosine, sine, keys_values,
        *([earlier] if last else []),
    )


def in_turn(per, count, step):
    for i in range(count):
        pl.when(pl.program_id(1) // per == i)(functools.partial(step, i))


def gate_kernel(per, parts, pieces, rows, *refs):
    gates, ups = refs[: parts * pieces], refs[parts * pieces : 2 * parts * pieces]
    activated, gate_slope, up_slope = refs[2 * parts * pieces :]
    depth = gates[0].shape[0]

    def product(weights, i):
        return sum(
            nn_dot(rows[:, k * depth : (k + 1) * depth], weights[k * pieces + i][...])
            for k in range(parts)
        )

    def step(i):
        gate, up = product(gates, i), product(ups, i)
        sigmoid = 1.0 / (1.0 + jnp.exp(-gate))
        silu = gate * sigmoid
        activated[...] = (silu * up).astype(jnp.bfloat16)
        gate_slope[...] = up * sigmoid * (1.0 + gate * (1.0 - sigmoid))
        up_slope[...] = silu

    in_turn(per, pieces, step)


def gate_back_kernel(per, parts, pieces, grads, *refs):
    weights, (gate_slope, up_slope, grad_gate, grad_up) = refs[:-4], refs[-4:]
    blocks, _, depth = weights[0].shape

    def step(i):
        grad = 0.0
        for k in range(parts):
            for z in range(blocks):
                at = (k * blocks + z) * depth
                grad = grad + nt_dot(grads[:, at : at + depth], weights[k * pieces + i][z])
        grad_gate[...] = (grad * gate_slope[...]).astype(jnp.bfloat16)
        grad_up[...] = (grad * up_slope[...]).astype(jnp.bfloat16)

    in_turn(per, pieces, step)


def down_kernel(per, parts, pieces, acts, *refs):
    weights, out = refs[:-1], refs[-1]
    depth = weights[0].shape[1]

    def step(k):
        total = sum(
            nn_dot(acts[:, i * depth : (i + 1) * depth], weights[k * pieces + i][0])
            for i in range(pieces)
        )
        out[...] = total.astype(jnp.bfloat16)

    in_turn(per, parts, step)


def turned_kernel(terms, per, parts, pieces, *refs):
    lefts, weights, out = refs[:terms], refs[terms:-1], refs[-1]
    depth = weights[0].shape[1]

    def step(k):
        total = 0.0
        for term, left in enumerate(lefts):
            for i in range(pieces):
                weight = weights[(term * parts + k) * pieces + i]
                total = total + nt_dot(left[:, i * depth : (i + 1) * depth], weight[...])
        out[...] = total.astype(jnp.bfloat16)

    in_turn(per, parts, step)


def wide_call(kernel, whole, weights, tiled, axis, by_piece, outs):
    parts, pieces = len(weights[0]), len(weights[0][0])
    shape = weights[0][0][0].shape
    groups = pieces if by_piece else parts
    if len(shape) == 3 and axis == 0:
        width, block, per = shape[0] * shape[2], (1, *shape[1:]), shape[0]
    else:
        width = shape[axis]
        per = width // min(width, 256)
        block = tuple(n // per if at == axis else n for at, n in enumerate(shape))
    tile = (min(whole[0].shape[0], 1024), width // per)
    count, cols = whole[0].shape[0], groups * width

    def piece_spec(k, i):
        group = i if by_piece else k

        def place(row, col):
            at = jnp.clip(col - group * per, 0, per - 1)
            return tuple(at if dim == axis else 0 for dim in range(len(shape)))

        return pl.BlockSpec(block, place)

    tile_spec = pl.BlockSpec(tile, lambda row, col: (row, col))
    flat = [v for weight in weights for row in weight for v in row]
    return pl.pallas_call(
        functools.partial(kernel, per, parts, pieces),
        grid=(count // tile[0], groups * per),
        in_specs=[pl.BlockSpec((tile[0], v.shape[1]), lambda row, col: (row, 0)) for v in whole]
        + [piece_spec(k, i) for _ in weights for k in range(parts) for i in range(pieces)]
        + [tile_spec] * len(tiled),
        out_specs=[tile_spec] * len(outs),
        out_shape=[jax.ShapeDtypeStruct((count, cols), t) for t in outs],
        compiler_params=pltpu.CompilerParams(vmem_limit_bytes=KERNEL_VMEM),
        cost_estimate=SMALL_COST,
    )(*whole, *flat, *tiled)


def gate_forward(rows, gates, ups):
    outs = (jnp.bfloat16, jnp.float32, jnp.float32)
    return wide_call(gate_kernel, [rows], [gates, ups], [], 1, True, outs)


def gate_backward(grads, downs, gate_slope, up_slope):
    outs = (jnp.bfloat16, jnp.bfloat16)
    return wide_call(gate_back_kernel, [grads], [downs], [gate_slope, up_slope], 1, True, outs)


def down_forward(acts, downs):
    if downs[0][0].shape[2] % LANES:
        rows = [jnp.concatenate([joined_columns(v) for v in row], axis=0) for row in downs]
        return nn_dot(acts, jnp.concatenate(rows, axis=1)).astype(jnp.bfloat16)
    return wide_call(down_kernel, [acts], [downs], [], 0, False, (jnp.bfloat16,))[0]


def turned_product(lefts, weights):
    kernel = functools.partial(turned_kernel, len(lefts))
    return wide_call(kernel, lefts, weights, [], 0, False, (jnp.bfloat16,))[0]


def o_kernel(parts, place, *refs):
    rows, weights, out = refs[:-1 - parts], refs[-1 - parts : -1], refs[-1]
    blocks = weights[0].shape[0]
    depth = rows[0].shape[1]
    at = lax.rem(pl.program_id(0), blocks)
    for k in range(parts):

        @pl.when(pl.program_id(0) // blocks == k)
        def _(k=k):
            total = 0.0
            for i, piece in enumerate(rows):
                group = lax.rem(place[0] + i, len(rows))
                start = pl.multiple_of(group * depth, depth)
                total = total + nn_dot(piece[...], weights[k][at, pl.ds(start, depth), :])
            out[...] = total.astype(jnp.bfloat16)


def o_forward(pieces, weights, place):
    count, depth = pieces[0].shape
    blocks, _, step = weights[0].shape
    if step % LANES:
        full = jnp.concatenate([joined_columns(v) for v in weights], axis=1)
        return nn_dot(in_groups(pieces), full).astype(jnp.bfloat16)
    whole = pl.BlockSpec(weights[0].shape, lambda j: (0, 0, 0))
    return pl.pallas_call(
        functools.partial(o_kernel, len(weights)),
        grid=(len(weights) * blocks,),
        in_specs=[pl.BlockSpec(memory_space=pltpu.SMEM)]
        + [pl.BlockSpec((count, depth), lambda j: (0, 0))] * len(pieces)
        + [whole] * len(weights),
        out_specs=pl.BlockSpec((count, step), lambda j: (0, j)),
        out_shape=jax.ShapeDtypeStruct((count, len(weights) * blocks * step), jnp.bfloat16),
        compiler_params=pltpu.CompilerParams(vmem_limit_bytes=KERNEL_VMEM),
        cost_estimate=SMALL_COST,
    )(place.astype(jnp.int32).reshape(1), *pieces, *weights)


def o_back_kernel(parts, rows, *refs):
    weights, out = refs[:parts], refs[parts]
    blocks, _, step = weights[0].shape
    total = 0.0
    for k in range(parts):
        for z in range(blocks):
            at = (k * blocks + z) * step
            total = total + nt_dot(rows[:, at : at + step], weights[k][z])
    out[...] = total.astype(jnp.bfloat16)


def o_backward(rows, weights):
    return pl.pallas_call(
        functools.partial(o_back_kernel, len(weights)),
        out_shape=jax.ShapeDtypeStruct((rows.shape[0], weights[0].shape[1]), jnp.bfloat16),
        compiler_params=pltpu.CompilerParams(vmem_limit_bytes=KERNEL_VMEM),
        cost_estimate=SMALL_COST,
    )(rows, *weights)


def split_kernel(*refs):
    values, out = refs[:-1], refs[-1]
    for i, value in enumerate(values):
        out[0, i] = value[...]


def split_columns(values, count):
    rows, cols = values[0].shape
    step = cols // count
    if step % LANES:
        return jnp.stack([column_blocks(v, count) for v in values], axis=1)
    return pl.pallas_call(
        split_kernel,
        grid=(count,),
        in_specs=[pl.BlockSpec((rows, step), lambda j: (0, j))] * len(values),
        out_specs=pl.BlockSpec((1, len(values), rows, step), lambda j: (j, 0, 0, 0)),
        out_shape=jax.ShapeDtypeStruct((count, len(values), rows, step), values[0].dtype),
        compiler_params=pltpu.CompilerParams(vmem_limit_bytes=KERNEL_VMEM),
        cost_estimate=SMALL_COST,
    )(*values)


def row_norm(value):
    inverse = lax.rsqrt(jnp.mean(value * value, axis=-1, keepdims=True) + norm_eps)
    return value * inverse, inverse


def norm_back(grad, normed, inverse, gain):
    scaled = grad * gain
    return inverse * (scaled - normed * jnp.mean(scaled * normed, axis=-1, keepdims=True))


def silu_parts(gate_pre):
    sigmoid = jax.nn.sigmoid(gate_pre)
    return sigmoid, gate_pre * sigmoid


def halves(value, count):
    part = value.shape[1] // count
    return [value[:, i * part : (i + 1) * part] for i in range(count)]


def crossed(by_x, by_y):
    half = by_x[0].shape[0] // 2
    upper = [[rotated(v[:half], "x", i) for i in range(1, len(by_x))] for v in by_y[1:]]
    lower = [[rotated(v[half:], "y", k) for v in by_x[1:]] for k in range(1, len(by_y))]
    return upper, lower


def quarters(by_x, by_y, upper, lower):
    far = [[jnp.concatenate(v, axis=0) for v in zip(*rows)] for rows in zip(upper, lower)]
    return [by_x] + [[by_y[k], *far[k - 1]] for k in range(1, len(by_y))]


def matmul(left, right):
    return jnp.dot(left, right, preferred_element_type=jnp.float32)


def matmul_turned(left, right):
    return nt_dot(left, right)


def turned_matmul(left, right):
    return lax.dot_general(
        left, right, (((0,), (0,)), ((), ())), preferred_element_type=jnp.float32
    )


def sent_groups(value):
    size = lax.axis_size("y")
    place = lax.axis_index("y")
    width = value.shape[1] // size
    pieces = []
    for k in range(size):
        start = lax.rem(place + k, size) * width
        piece = lax.dynamic_slice_in_dim(value, start, width, 1)
        pieces.append(rotated(piece, "y", k) if k else piece)
    return pieces


def in_groups(pieces):
    size = len(pieces)
    place = lax.axis_index("y")
    return jnp.concatenate(
        [
            lax.select_n(place, *[pieces[(j - i) % size] for i in range(size)])
            for j in range(size)
        ],
        axis=1,
    )


def in_order(pieces):
    return natural_pieces(pieces, "y")


def turned_sum_kernel(blocks, cosine, sine, out):
    total = sum(blocks[i, 0].astype(jnp.float32) for i in range(blocks.shape[0]))
    out[...] = turned(total.T, cosine[...], sine[...], -1.0).astype(jnp.bfloat16)


def turned_sum(blocks, cosine, sine):
    terms, segs, lanes, seg = blocks.shape
    table = pl.BlockSpec((seg, lanes), lambda s: (s, 0))
    return pl.pallas_call(
        turned_sum_kernel,
        grid=(segs,),
        in_specs=[pl.BlockSpec((terms, 1, lanes, seg), lambda s: (0, s, 0, 0)), table, table],
        out_specs=table,
        out_shape=jax.ShapeDtypeStruct((segs * seg, lanes), jnp.bfloat16),
        compiler_params=pltpu.CompilerParams(vmem_limit_bytes=KERNEL_VMEM),
        cost_estimate=SMALL_COST,
    )(blocks, cosine, sine)


def gathered_core(x_pieces):
    rows = jnp.stack(natural_pieces(x_pieces, "x"))
    rows = jnp.stack(natural_pieces(relative_pieces(rows, "c"), "c"), axis=1)
    return rows.reshape(-1, rows.shape[-1])


def own_first(value, axis):
    size = value.shape[0]
    place = lax.axis_index(axis)
    return [
        lax.dynamic_index_in_dim(value, lax.rem(place - k + size, size), 0, keepdims=False)
        for k in range(size)
    ]


def core_sum(part, rows):
    blocks = part.reshape(lax.axis_size("x"), lax.axis_size("c"), rows, -1)
    return summed_pieces(own_first(blocks.transpose(1, 0, 2, 3), "c"), "c").astype(jnp.bfloat16)


def x_blocks(value):
    return own_first(value, "x")


def tensor_sum(part, rows):
    return summed_pieces(x_blocks(core_sum(part, rows)), "x")


def local(
    tokens,
    norm_gain,
    q_weight,
    key_matrix,
    value_matrix,
    o_weight,
    mlp_gain,
    gate_weight,
    up_weight,
    down_weight,
    parents,
    out_grad,
):
    z_size, y_size, x_size = (lax.axis_size(name) for name in ("z", "y", "x"))
    tensor_size = x_size * lax.axis_size("c")
    low = jnp.bfloat16
    local_rows, width = tokens.shape
    group_rows = local_rows * tensor_size
    kv_cols = key_matrix.shape[1]
    kv_local = kv_cols // HEAD_SIZE
    q_cols = q_weight.shape[1]
    own_width = norm_gain.shape[0]

    own_tokens = relative_columns(tokens)
    own_grad = relative_columns(out_grad).astype(jnp.float32)
    both_gains = jnp.concatenate([norm_gain, mlp_gain])
    both_gains = jnp.pad(both_gains, (0, -both_gains.shape[0] % (2 * kv_cols)))
    key_heads, value_heads = halves(key_matrix, kv_local), halves(value_matrix, kv_local)
    kv_shard = jnp.concatenate(
        [
            jnp.concatenate([v for kv in zip(key_heads, value_heads) for v in kv], axis=1),
            both_gains.reshape(-1, 2 * kv_cols),
        ],
        axis=0,
    )
    kv_copies = jnp.broadcast_to(kv_shard[None], (z_size, *kv_shard.shape))
    kv_copies, q_weight = together(kv_copies, q_weight)
    kv_z = exchanged(kv_copies, "z")
    q_z = lax.all_gather(q_weight, "z", axis=0, tiled=True)
    group_tokens = gathered_core(relative_pieces(own_tokens, "x"))
    kv_z, o_weight = together(kv_z, o_weight)
    o_z = lax.all_gather(o_weight, "z", axis=0)

    depth = segment_depth(parents)
    seg_count = group_rows // SEG
    z_place, y_place = lax.axis_index("z"), lax.axis_index("y")
    sources = [lax.rem(y_place - k + y_size, y_size) for k in range(y_size)]
    segs = jnp.concatenate(
        [
            (z_place * y_size + source) * seg_count + jnp.arange(seg_count, dtype=jnp.int32)
            for source in sources
        ]
    )
    seg_ids = jnp.arange(depth.shape[0], dtype=jnp.int32)
    seg_depth = jnp.sum(jnp.where(segs[:, None] == seg_ids[None, :], depth[None, :], 0), axis=1)
    position = (seg_depth[:, None] * SEG + jnp.arange(SEG, dtype=jnp.int32)[None, :]).reshape(-1)
    cosine_table, sine_table = rope_tables(position, HEAD_SIZE)
    cosine_lanes = jnp.tile(cosine_table, (1, 4))
    sine_lanes = jnp.tile(sine_table, (1, 4))
    key_lanes = jnp.arange(LANES) < HEAD_SIZE
    cosine_keys = jnp.where(key_lanes, cosine_lanes[:group_rows], 1.0)
    sine_keys = jnp.where(key_lanes, sine_lanes[:group_rows], 0.0)

    kv_zy = relative_pieces(kv_z, "y")
    kv_weights = [v[:, :own_width].reshape(-1, 2 * kv_cols) for v in kv_zy]
    gains = [
        v[:, own_width:].reshape(z_size, -1)[:, : 2 * own_width].reshape(z_size, 2, own_width)
        for v in kv_zy
    ]
    gains = jnp.stack(gains).astype(jnp.float32)
    gain_one, gain_two = gains[:, :, 0].reshape(-1), gains[:, :, 1].reshape(-1)
    inputs = own_tokens.astype(jnp.float32)
    normed_one, inv_one = row_norm(inputs)
    group_normed, _ = row_norm(group_tokens.astype(jnp.float32))
    rows_one = (group_normed * gain_one).astype(low)
    rows_one, q_z = together(rows_one, q_z)
    q_weights = relative_pieces(q_z, "y")
    kv_rows = project(rows_one, kv_weights, cosine_keys, sine_keys)
    kv_swapped = jnp.stack(natural_pieces(sent_groups(kv_rows), "y"))
    all_kv = gathered(kv_swapped, "z").reshape(-1, SEG, LANES)
    wide_blocks = split_columns(after((gate_weight, up_weight), kv_z), z_size)
    q_weights, wide_blocks = together(q_weights, wide_blocks)
    query_rows = project(rows_one, q_weights, cosine_lanes[:group_rows], sine_lanes[:group_rows])
    queries = sent_groups(query_rows)
    tables = [jnp.split(v, y_size) for v in (cosine_lanes, sine_lanes)]
    key_tables = [
        jnp.concatenate(in_order(jnp.split(v, y_size)))
        for v in (jnp.where(key_lanes, cosine_lanes, 1.0), jnp.where(key_lanes, sine_lanes, 0.0))
    ]
    all_kv, queries, o_z, wide_blocks, tables, key_tables = together(
        all_kv, queries, o_z, wide_blocks, tables, key_tables
    )

    wide_z = exchanged(wide_blocks, "z")
    o_weights = relative_pieces(o_z, "y")
    seg_lists = jnp.split(segs, y_size)
    attends, lows = [None] * y_size, [None] * y_size
    for k in range(y_size - 1, 0, -1):
        *attends[k], lows[k] = attend(parents, seg_lists[k], queries[k], all_kv)
    queries[0], attends[1:], lows[1:] = together(queries[0], attends[1:], lows[1:])
    returned = [rotated(v, "y", -k) for k, v in enumerate(lows[1:], 1)]
    *attends[0], lows[0] = attend(parents, seg_lists[0], queries[0], all_kv)
    attn_pieces = [lows[0], *returned]
    attn_pieces, o_weights = together(attn_pieces, o_weights)
    attn_part = o_forward(attn_pieces, o_weights, y_place)
    attn_low = in_groups(attn_pieces)
    attn_core = core_sum(attn_part, local_rows)
    attn_core, wide_z = together(attn_core, wide_z)

    gate_z, up_z = (wide_z[:, i].reshape(z_size * own_width, -1) for i in range(2))
    gate_zy, up_zy = relative_pieces(gate_z, "y"), relative_pieces(up_z, "y")
    gate_zx = relative_pieces(gate_z, "x")
    attn_mine = summed_pieces(x_blocks(attn_core), "x")
    attn_mine, up_z, down_weight = together(attn_mine, up_z, down_weight)

    middle = inputs + branch_scale * attn_mine
    normed_two, inv_two = row_norm(middle)
    hidden_two = (normed_two * gain_two).astype(low)
    rows_two = lax.all_gather(hidden_two, ("z", "c"), axis=0, tiled=True)
    down_z = exchanged(down_weight.reshape(z_size, -1, own_width), "z")
    gate_zx, gate_zy, up_z = together(gate_zx, gate_zy, up_z)
    gate_far = [relative_pieces(v, "y")[1:] for v in gate_zx[1:]]
    up_zx = relative_pieces(up_z, "x")
    grad_mlp = (branch_scale * own_grad).astype(low)
    up_zx, up_zy, grad_mlp, down_z = together(up_zx, up_zy, grad_mlp, down_z)
    grad_mlp_rows = lax.all_gather(grad_mlp, ("z", "c"), axis=0, tiled=True)
    up_far = [relative_pieces(v, "x")[1:] for v in up_zy[1:]]
    rows_two, gate_far, up_far, down_z = together(rows_two, gate_far, up_far, down_z)
    down_zy, down_zx = relative_pieces(down_z, "y"), relative_pieces(down_z, "x")
    gates = [gate_zx] + [[gate_zy[k], *[v[k - 1] for v in gate_far]] for k in range(1, y_size)]
    ups = [up_zx] + [[up_zy[k], *up_far[k - 1]] for k in range(1, y_size)]
    activated, gate_slope, up_slope = gate_forward(rows_two, gates, ups)
    down_zy, down_zx, activated, gate_slope, up_slope = together(
        down_zy, down_zx, activated, gate_slope, up_slope
    )
    down_crossed = together(*crossed(down_zx, down_zy))
    downs = quarters(down_zx, down_zy, *down_crossed)
    mlp_part = down_forward(activated, downs)
    mlp_part, grad_mlp_rows = together(mlp_part, grad_mlp_rows)

    mlp_mine = lax.psum_scatter(mlp_part, ("z", "c"), scatter_dimension=0, tiled=True)
    grad_parts, rows_parts = halves(grad_mlp_rows, y_size), halves(rows_two, y_size)
    acts = halves(activated, x_size)
    down_far = [summed_pieces([turned_matmul(a, b) for a in grad_parts], "y").astype(low) for b in acts[1:]]
    grad_gate_act, grad_up_act = gate_backward(grad_mlp_rows, downs, gate_slope, up_slope)
    grad_gate_act, grad_up_act = together(grad_gate_act, grad_up_act)

    gate_parts, up_parts = halves(grad_gate_act, x_size), halves(grad_up_act, x_size)
    gate_dots = [[turned_matmul(a, b) for a in rows_parts] for b in gate_parts[1:]]
    up_dots = [[turned_matmul(a, b) for b in up_parts] for a in rows_parts[1:]]
    for dots in gate_dots + up_dots:
        dots[1:] = [v.astype(low) for v in dots[1:]]
    grad_gate_act, gate_dots, up_dots = together(grad_gate_act, gate_dots, up_dots)
    gate_far = [summed_pieces(v, "y").astype(low) for v in gate_dots]
    up_far = [summed_pieces(v, "x").astype(low) for v in up_dots]
    input_part = turned_product([grad_gate_act, grad_up_act], [gates, ups])
    input_part, down_far = together(input_part, down_far)

    grad_rows_two = lax.psum_scatter(input_part, ("z", "c"), scatter_dimension=0, tiled=True)
    gate_far, up_far, acts = together(gate_far, up_far, acts)
    down_near = summed_pieces([turned_matmul(a, acts[0]) for a in grad_parts], "y")
    down_far = [rotated(v, "x", -1 - i) for i, v in enumerate(down_far)]
    down_near, down_far, gate_parts = together(down_near, down_far, gate_parts)
    grad_down_z = sum([v.astype(jnp.float32) for v in down_far], down_near).astype(low)
    gate_near = summed_pieces([turned_matmul(a, gate_parts[0]) for a in rows_parts], "y")
    gate_far = [rotated(v, "x", -1 - i) for i, v in enumerate(gate_far)]
    up_near = [turned_matmul(rows_parts[0], b) for b in up_parts]
    up_near[1:] = [v.astype(low) for v in up_near[1:]]
    grad_rows_two, mlp_mine, up_far, up_near, grad_down_z = together(
        grad_rows_two, mlp_mine, up_far, up_near, grad_down_z
    )
    grad_rows_two = grad_rows_two.astype(jnp.float32)
    gain_two_part = jnp.sum(grad_rows_two * normed_two, axis=0)
    grad_middle = own_grad + norm_back(grad_rows_two, normed_two, inv_two, gain_two)
    grad_attn = (branch_scale * grad_middle).astype(low)
    attn_x = relative_pieces(grad_attn, "x")
    up_far = [rotated(v, "y", -1 - i) for i, v in enumerate(up_far)]
    grad_gate_z = sum([v.astype(jnp.float32) for v in gate_far], gate_near).astype(low)
    wide_z = jnp.stack([v.reshape(z_size, own_width, -1) for v in (grad_gate_z, grad_down_z)], 1)
    attn_x, wide_z, up_near = together(attn_x, wide_z, up_near)
    wide_z = exchanged(wide_z, "z")
    grad_attn_rows = gathered_core(attn_x)
    grad_heads = o_backward(grad_attn_rows, o_weights)
    grad_heads, grad_attn_rows, up_near = together(grad_heads, grad_attn_rows, up_near)

    grad_heads = sent_groups(grad_heads)
    o_dots = [turned_matmul(v, attn_low) for v in halves(grad_attn_rows, y_size)[1:]]
    o_dots = [v.astype(low) for v in o_dots]
    grad_heads, o_dots, up_near, grad_attn_rows = together(
        grad_heads, o_dots, up_near, grad_attn_rows
    )
    o_sent = [rotated(v, "y", -1 - i) for i, v in enumerate(o_dots)]
    up_mine = [rotated(v, "x", -1 - i) for i, v in enumerate(up_near[1:])]
    cosines, sines = tables
    grad_queries, sums = [None] * y_size, None
    for k in range(y_size - 1, 0, -1):
        grad_queries[k], sums = attend_back(
            parents, seg_lists[k], queries[k], grad_heads[k], *attends[k], cosines[k], sines[k],
            all_kv, sums,
        )
    grad_o_y = turned_matmul(halves(grad_attn_rows, y_size)[0], attn_low)
    grad_o_y = sum([v.astype(jnp.float32) for v in o_sent], grad_o_y).astype(low)
    grad_queries[1:], sums, grad_o_y = together(grad_queries[1:], sums, grad_o_y)
    grad_o = lax.psum_scatter(grad_o_y, "z", scatter_dimension=0, tiled=True)
    returned = [rotated(v, "y", -k) for k, v in enumerate(grad_queries[1:], 1)]
    grad_queries[0], grad_kv = attend_back(
        parents, seg_lists[0], queries[0], grad_heads[0], *attends[0], cosines[0], sines[0],
        all_kv, sums,
    )
    grad_queries[0], grad_kv, returned, up_far, up_mine, up_near, wide_z = together(
        grad_queries[0], grad_kv, returned, up_far, up_mine, up_near, wide_z
    )

    def owned_dots(left, right):
        dots = [turned_matmul(v, right) for v in halves(left, y_size)]
        return dots[:1] + [v.astype(low) for v in dots[1:]]

    def sent_back(dots):
        return [rotated(v, "y", -1 - i) for i, v in enumerate(dots[1:])]

    def total(own, sent):
        return sum([v.astype(jnp.float32) for v in sent], own).astype(low)

    kv_mine = exchanged(grad_kv.reshape(z_size, y_size * seg_count, LANES, SEG), "z")
    grad_queries = in_groups([grad_queries[0], *returned])
    query_dots = owned_dots(rows_one, grad_queries)
    query_sent = sent_back(query_dots)
    q_full = jnp.concatenate(q_weights, axis=0)
    query_part = matmul_turned(grad_queries, q_full)
    grad_up_z = total(up_near[0], up_far + up_mine)
    kv_mine, query_part, query_dots, query_sent, grad_up_z = together(
        kv_mine, query_part, query_dots, query_sent, grad_up_z
    )

    grad_up = exchanged(grad_up_z.reshape(z_size, own_width, -1), "z")
    kv_mine = turned_sum(kv_mine, *key_tables).reshape(y_size, group_rows, LANES)
    kv_mine = own_first(kv_mine, "y")
    grad_kv_rows = in_groups(
        [kv_mine[0]] + [rotated(v, "y", -k) for k, v in enumerate(kv_mine[1:], 1)]
    )
    kv_full = jnp.concatenate(kv_weights, axis=0)
    input_one = (query_part + matmul_turned(grad_kv_rows, kv_full)).astype(low)
    input_core = core_sum(input_one, local_rows)
    kv_dots = owned_dots(rows_one, grad_kv_rows)
    kv_sent = sent_back(kv_dots)
    input_core, query_sent, query_dots, grad_up = together(
        input_core, query_sent, query_dots, grad_up
    )
    grad_q_y = total(query_dots[0], query_sent)
    grad_q = lax.psum_scatter(grad_q_y, "z", scatter_dimension=0, tiled=True)
    input_x = x_blocks(input_core)
    input_sent = [rotated(v, "x", -1 - i) for i, v in enumerate(input_x[1:])]
    input_x[0], input_sent, kv_sent, kv_dots, mlp_mine = together(
        input_x[0], input_sent, kv_sent, kv_dots, mlp_mine
    )
    grad_rows_one = sum([v.astype(jnp.float32) for v in input_sent], input_x[0].astype(jnp.float32))
    kv_blocks = own_first(total(kv_dots[0], kv_sent).reshape(z_size, own_width, -1), "z")
    kv_sent = [rotated(v, "z", -1 - i) for i, v in enumerate(kv_blocks[1:])]
    gain_one_part = jnp.sum(grad_rows_one * normed_one, axis=0)
    grad_inputs = grad_middle + norm_back(grad_rows_one, normed_one, inv_one, gain_one)
    kv_sent, kv_blocks, grad_inputs, wide_z, grad_up, grad_q, grad_o, mlp_mine = together(
        kv_sent, kv_blocks, grad_inputs, wide_z, grad_up, grad_q, grad_o, mlp_mine
    )
    mixed = natural_columns((middle + branch_scale * mlp_mine.astype(jnp.float32)).astype(low))
    grad_tokens = natural_columns(grad_inputs.astype(low))
    grad_kv_weight = sum([v.astype(jnp.float32) for v in kv_sent], kv_blocks[0].astype(jnp.float32))
    grad_q, grad_o = grad_q.astype(jnp.float32), grad_o.astype(jnp.float32).T
    grad_gate, grad_down, grad_up = (
        joined_columns(v).astype(jnp.float32) for v in (wide_z[:, 0], wide_z[:, 1], grad_up)
    )
    grad_down = grad_down.T

    gain_parts = jnp.stack([gain_one_part, gain_two_part], axis=0)
    gain_parts = natural_columns(gain_parts).reshape(2, z_size * y_size, 1, own_width)
    gain_parts = jnp.broadcast_to(
        gain_parts, (2, z_size * y_size, tensor_size, own_width)
    ).reshape(2, -1, own_width).transpose(1, 0, 2)
    gain_sums = jnp.sum(exchanged(gain_parts, ("z", "y", "x", "c")), axis=0)
    grad_heads = halves(grad_kv_weight, 2 * kv_local)
    return (
        mixed,
        grad_tokens,
        gain_sums[0],
        grad_q,
        jnp.concatenate(grad_heads[::2], axis=1),
        jnp.concatenate(grad_heads[1::2], axis=1),
        grad_o,
        gain_sums[1],
        grad_gate,
        grad_up,
        grad_down,
    )


def solution(mesh):
    dp_size, tensor_size = mesh.shape["dp"], mesh.shape["tensor"]
    fine = jax.sharding.Mesh(
        mesh.devices.reshape(dp_size // 2, 2, tensor_size // 2, 2), ("z", "y", "x", "c")
    )
    dp, tensor = ("z", "y"), ("x", "c")
    tokens = P(dp + tensor, None)
    rows = P(dp, tensor)
    columns = P(tensor, dp)
    in_specs = (
        tokens,
        P(dp),
        rows,
        rows,
        rows,
        columns,
        P(dp),
        rows,
        rows,
        columns,
        P(),
        tokens,
    )
    out_specs = (
        tokens,
        tokens,
        P(dp),
        rows,
        rows,
        rows,
        columns,
        P(dp),
        rows,
        rows,
        columns,
    )
    return jax.shard_map(local, mesh=fine, in_specs=in_specs, out_specs=out_specs, check_vma=False)
```

```python
import functools

import jax
import jax.numpy as jnp
from jax import lax
from jax.experimental import pallas as pl
from jax.experimental.pallas import tpu as pltpu
from jax.sharding import PartitionSpec as P

HEAD_SIZE = 64
SEG = 256
MAX_STEPS = 9
LANES = 2 * HEAD_SIZE
KERNEL_VMEM = 56 * 2**20
SMALL_COST = pl.CostEstimate(flops=2**28, bytes_accessed=2**18, transcendentals=0)


attn_scale = 0.015625
branch_scale = 0.22
norm_eps = 1e-05
rope_base = 10000000.0
masked_score = -1e30


def segment_depth(parents):
    seg_total = parents.shape[0]
    seg_ids = jnp.arange(seg_total, dtype=jnp.int32)
    reach = (parents[:, None] == seg_ids[None, :]) | (seg_ids[:, None] == seg_ids[None, :])
    reach = reach.astype(jnp.float32)
    for doubling in range(4):
        reach = jnp.minimum(jnp.dot(reach, reach, preferred_element_type=jnp.float32), 1.0)
    return jnp.sum(reach, axis=1).astype(jnp.int32) - 1


def rope_tables(position, head_dim):
    half_dim = head_dim // 2
    exponent = jnp.arange(half_dim, dtype=jnp.float32) * (2.0 / head_dim)
    inverse = jnp.power(rope_base, -exponent)
    angles = position.astype(jnp.float32)[:, None] * inverse[None, :]
    return (jnp.cos(angles), jnp.sin(angles))


def rotated(value, axis, step):
    size = lax.axis_size(axis)
    return lax.ppermute(value, axis, [(i, (i + step) % size) for i in range(size)])


def relative_pieces(value, axis):
    return [value] + [rotated(value, axis, k) for k in range(1, lax.axis_size(axis))]


def natural_pieces(pieces, axis):
    size = len(pieces)
    place = lax.axis_index(axis)
    return [
        lax.select_n(place, *[pieces[(i - j) % size] for i in range(size)]) for j in range(size)
    ]


def gathered(value, axis):
    size = lax.axis_size(axis)
    copies = jnp.broadcast_to(value[None], (size, *value.shape))
    return lax.all_to_all(copies, axis, 0, 0, tiled=True)


def exchanged(blocks, axis):
    return lax.all_to_all(blocks, axis, 0, 0, tiled=True)


def summed_pieces(pieces, axis):
    sent = [rotated(pieces[k].astype(jnp.bfloat16), axis, -k) for k in range(1, len(pieces))]
    total = pieces[0].astype(jnp.float32)
    for value in sent:
        total = total + value.astype(jnp.float32)
    return total


def summed_blocks(blocks, axis):
    return jnp.sum(exchanged(blocks.astype(jnp.bfloat16), axis).astype(jnp.float32), axis=0)


def column_blocks(value, count):
    return value.reshape(value.shape[0], count, -1).transpose(1, 0, 2)


def joined_columns(blocks):
    return blocks.transpose(1, 0, 2).reshape(blocks.shape[1], -1)


def relative_columns(value):
    size = lax.axis_size("y")
    place = lax.axis_index("y")
    rows = value.shape[0]
    split = value.reshape(rows, lax.axis_size("z"), size, -1)
    flat = [split[:, :, i].reshape(rows, -1) for i in range(size)]
    return jnp.concatenate(
        [
            lax.select_n(place, *[flat[(i - k) % size] for i in range(size)])
            for k in range(size)
        ],
        axis=1,
    )


def natural_columns(value):
    size = lax.axis_size("y")
    rows = value.shape[0]
    split = value.reshape(rows, size, lax.axis_size("z"), -1)
    parts = natural_pieces([split[:, k] for k in range(size)], "y")
    return jnp.stack(parts, axis=2).reshape(rows, -1)


def together(*values):
    return lax.optimization_barrier(values)


def after(value, *others):
    return lax.optimization_barrier((value, *others))[0]


def ancestor_count(parents, seg):
    def climb(step, state):
        current, count = state
        above = parents[current]
        return above, count + jnp.where(above != current, 1, 0)

    return lax.fori_loop(0, MAX_STEPS, climb, (seg, jnp.int32(1)))[1]


def left_lanes(shape):
    return lax.broadcasted_iota(jnp.int32, shape, 1) < HEAD_SIZE


def stacked_heads(pairs, to_left):
    left = left_lanes(pairs[0].shape)
    stack = []
    for pair in pairs:
        swapped = pltpu.roll(pair, HEAD_SIZE, 1)
        for head in (pair, swapped) if to_left else (swapped, pair):
            stack.append(jnp.where(left, head, 0.0) if to_left else jnp.where(left, 0.0, head))
    return jnp.concatenate(stack, axis=0)


def unstacked_heads(stack, from_left):
    left = left_lanes((SEG, 2 * HEAD_SIZE))
    pairs = []
    for first in range(0, stack.shape[0], 2 * SEG):
        even, odd = stack[first : first + SEG], stack[first + SEG : first + 2 * SEG]
        if from_left:
            odd = pltpu.roll(odd, HEAD_SIZE, 1)
        else:
            even = pltpu.roll(even, HEAD_SIZE, 1)
        pairs.append(jnp.where(left, even, odd))
    return pairs


def turned(value, cosine, sine, direction):
    half = HEAD_SIZE // 2
    lane = lax.broadcasted_iota(jnp.int32, value.shape, 1)
    first = lax.rem(lane, HEAD_SIZE) < half
    ahead = pltpu.roll(value, LANES - half, 1)
    behind = pltpu.roll(value, half, 1)
    signed = sine * direction
    return value * cosine + jnp.where(first, -ahead * signed, behind * signed)


def nt_dot(left, right):
    return lax.dot_general(
        left, right, (((1,), (1,)), ((), ())), preferred_element_type=jnp.float32
    )


def nn_dot(left, right):
    return lax.dot_general(
        left, right, (((1,), (0,)), ((), ())), preferred_element_type=jnp.float32
    )


def causal_tile(rows):
    query = lax.rem(lax.broadcasted_iota(jnp.int32, (rows, SEG), 0), SEG)
    return lax.broadcasted_iota(jnp.int32, (rows, SEG), 1) <= query


def lane_blocks(ref):
    return [ref[:, at : at + LANES] for at in range(0, ref.shape[1], LANES)]


def key_tables(cosine, sine):
    left = left_lanes(cosine.shape)
    return jnp.where(left, cosine, 1.0), jnp.where(left, sine, 0.0)


def settle_kernel(*refs):
    count = len(refs) // 2
    for value, out in zip(refs[:count], refs[count:]):
        out[...] = value[...]


def settled(*values):
    return pl.pallas_call(
        settle_kernel,
        out_shape=[jax.ShapeDtypeStruct(v.shape, v.dtype) for v in values],
        compiler_params=pltpu.CompilerParams(vmem_limit_bytes=KERNEL_VMEM),
        cost_estimate=SMALL_COST,
    )(*values)


def project_kernel(parts, keys, rows, *refs):
    weights, (cosine, sine, out) = refs[:parts], refs[parts:]
    depth = weights[0].shape[0]
    product = sum(nn_dot(rows[:, i * depth : (i + 1) * depth], w[...]) for i, w in enumerate(weights))
    cos, sin = cosine[...], sine[...]
    if keys:
        cos, sin = key_tables(cos, sin)
    for at in range(0, product.shape[1], LANES):
        block = turned(product[:, at : at + LANES], cos, sin, 1.0)
        out[:, at : at + LANES] = block.astype(jnp.bfloat16)


def project(rows, weights, cosine, sine, keys=False):
    count, width = rows.shape
    depth, cols = weights[0].shape
    step = 2 * LANES
    table = pl.BlockSpec((count, LANES), lambda j: (0, 0))
    return pl.pallas_call(
        functools.partial(project_kernel, len(weights), keys),
        grid=(cols // step,),
        in_specs=[pl.BlockSpec((count, width), lambda j: (0, 0))]
        + [pl.BlockSpec((depth, step), lambda j: (0, j))] * len(weights)
        + [table, table],
        out_specs=pl.BlockSpec((count, step), lambda j: (0, j)),
        out_shape=jax.ShapeDtypeStruct((count, cols), jnp.bfloat16),
        compiler_params=pltpu.CompilerParams(vmem_limit_bytes=KERNEL_VMEM),
        cost_estimate=SMALL_COST,
    )(rows, *weights, cosine, sine)


def attend_kernel(parents, segs, queries, keys_values, out, stats, out_low, scores):
    seg = segs[pl.program_id(0)]
    count = ancestor_count(parents, seg)
    pairs = [block.astype(jnp.float32) * attn_scale for block in lane_blocks(queries)]
    stack = stacked_heads(pairs, True).astype(jnp.bfloat16)
    rows = stack.shape[0]

    first = jnp.where(causal_tile(rows), nt_dot(stack, keys_values[seg]), masked_score)
    scores[0] = first

    def folded(tile):
        return jnp.maximum(tile[:, :LANES], tile[:, LANES:])

    def measure(step, state):
        current, top = state
        current = parents[current]
        tile = nt_dot(stack, keys_values[current])
        scores[step] = tile
        return current, jnp.maximum(top, folded(tile))

    top = lax.fori_loop(1, count, measure, (seg, folded(first)))[1]
    row_max = jnp.max(top, axis=1, keepdims=True)
    left = left_lanes((SEG, LANES))

    def gather(step, state):
        current, mixed = state
        terms = jnp.exp(scores[step] - row_max).astype(jnp.bfloat16)
        tile = jnp.where(left, jnp.ones((SEG, LANES), jnp.bfloat16), keys_values[current])
        return parents[current], mixed + nn_dot(terms, tile)

    start = (seg, jnp.zeros((rows, LANES), jnp.float32))
    mixed = lax.fori_loop(0, count, gather, start)[1]
    total = mixed[:, :1]
    mixed = mixed / total
    stats[0] = row_max + jnp.log(total)
    for place, pair in enumerate(unstacked_heads(mixed, False)):
        out[:, place * LANES : (place + 1) * LANES] = pair
        out_low[:, place * LANES : (place + 1) * LANES] = pair.astype(jnp.bfloat16)


def attend_back_kernel(
    parents, segs, queries, grads, attended, stats, cosine, sine, keys_values, *refs
):
    earlier, (grad_queries, grad_kv, kv_sum) = refs[:-3], refs[-3:]
    seg = segs[pl.program_id(0)]
    count = ancestor_count(parents, seg)

    @pl.when(pl.program_id(0) == 0)
    def _():
        kv_sum[...] = earlier[0][...] if earlier else jnp.zeros_like(kv_sum)

    query_pairs = [block.astype(jnp.float32) * attn_scale for block in lane_blocks(queries)]
    grad_pairs = [block.astype(jnp.float32) for block in lane_blocks(grads)]
    left = left_lanes((SEG, LANES))
    deltas = []
    for pair, out in zip(grad_pairs, lane_blocks(attended)):
        product = pair * out
        deltas.append(jnp.sum(jnp.where(left, product, 0.0), axis=1, keepdims=True))
        deltas.append(jnp.sum(jnp.where(left, 0.0, product), axis=1, keepdims=True))
    delta = jnp.concatenate(deltas, axis=0)
    query_wide = stacked_heads(query_pairs, True)
    grad_wide = stacked_heads(grad_pairs, False)
    query_stack, grad_stack = query_wide.astype(jnp.bfloat16), grad_wide.astype(jnp.bfloat16)
    query_turned = query_wide.T.astype(jnp.bfloat16)
    grad_turned = grad_wide.T.astype(jnp.bfloat16)
    log_total = stats[0]
    rows = query_stack.shape[0]

    def visit(current, total, diagonal):
        tile_kv = keys_values[current]
        tile = nt_dot(query_stack, tile_kv)
        if diagonal:
            tile = jnp.where(causal_tile(rows), tile, masked_score)
        probs = jnp.exp(tile - log_total)
        grad_probs = nt_dot(grad_stack, tile_kv)
        grad_tile = (probs * (grad_probs - delta)).astype(jnp.bfloat16)
        kv_sum[current] += nn_dot(query_turned, grad_tile) + nn_dot(
            grad_turned, probs.astype(jnp.bfloat16)
        )
        return total + nn_dot(grad_tile, tile_kv)

    total = visit(seg, jnp.zeros((rows, LANES), jnp.float32), True)

    def climb(step, state):
        current, total = state
        current = parents[current]
        return current, visit(current, total, False)

    total = lax.fori_loop(1, count, climb, (seg, total))[1]
    cos, sin = cosine[...], sine[...]
    for place, pair in enumerate(unstacked_heads(total * attn_scale, True)):
        grad_queries[:, place * LANES : (place + 1) * LANES] = turned(
            pair, cos, sin, -1.0
        ).astype(jnp.bfloat16)

    @pl.when(pl.program_id(0) == pl.num_programs(0) - 1)
    def _():
        grad_kv[...] = kv_sum[...].astype(grad_kv.dtype)


def attention_specs(cols, seg_total):
    block = pl.BlockSpec((SEG, cols), lambda s: (s, 0))
    table = pl.BlockSpec((SEG, LANES), lambda s: (s, 0))
    whole = pl.BlockSpec((seg_total, SEG, LANES), lambda s: (0, 0, 0))
    rows = SEG * (cols // HEAD_SIZE)
    stat = pl.BlockSpec((1, rows, 1), lambda s: (s, 0, 0))
    return block, table, whole, rows, stat, pl.BlockSpec(memory_space=pltpu.SMEM)


def attend(parents, segs, queries, keys_values):
    count, cols = queries.shape
    block, table, whole, rows, stat, scalar = attention_specs(cols, keys_values.shape[0])
    steps = count // SEG
    return pl.pallas_call(
        attend_kernel,
        grid=(steps,),
        in_specs=[scalar, scalar, block, whole],
        out_specs=[block, stat, block],
        out_shape=[
            jax.ShapeDtypeStruct((count, cols), jnp.float32),
            jax.ShapeDtypeStruct((steps, rows, 1), jnp.float32),
            jax.ShapeDtypeStruct((count, cols), jnp.bfloat16),
        ],
        scratch_shapes=[pltpu.VMEM((MAX_STEPS + 1, rows, SEG), jnp.float32)],
        compiler_params=pltpu.CompilerParams(vmem_limit_bytes=KERNEL_VMEM),
        cost_estimate=SMALL_COST,
    )(parents, segs, queries, keys_values)


def attend_back(
    parents, segs, queries, grads, attended, stats, cosine, sine, place, keys_values, earlier=None
):
    count, cols = queries.shape
    first = place * (count // SEG)
    seg_total = keys_values.shape[0]
    block, table, whole, rows, stat, scalar = attention_specs(cols, seg_total)
    sums = pl.BlockSpec((seg_total, LANES, SEG), lambda s: (0, 0, 0))
    last = earlier is not None
    sum_type = jnp.bfloat16 if last else jnp.float32
    return pl.pallas_call(
        attend_back_kernel,
        grid=(count // SEG,),
        in_specs=[scalar, scalar, block, block, block, stat]
        + [pl.BlockSpec((SEG, LANES), lambda s: (first + s, 0))] * 2
        + [whole]
        + [sums] * last,
        out_specs=[block, sums],
        out_shape=[
            jax.ShapeDtypeStruct((count, cols), jnp.bfloat16),
            jax.ShapeDtypeStruct((seg_total, LANES, SEG), sum_type),
        ],
        scratch_shapes=[pltpu.VMEM((seg_total, LANES, SEG), jnp.float32)],
        compiler_params=pltpu.CompilerParams(vmem_limit_bytes=KERNEL_VMEM),
        cost_estimate=SMALL_COST,
    )(
        parents, segs, queries, grads, attended, stats, cosine, sine, keys_values,
        *([earlier] if last else []),
    )


def in_turn(per, count, step):
    for i in range(count):
        pl.when(pl.program_id(1) // per == i)(functools.partial(step, i))


def gate_kernel(per, parts, pieces, rows, *refs):
    gates, ups = refs[: parts * pieces], refs[parts * pieces : 2 * parts * pieces]
    activated, gate_slope, up_slope = refs[2 * parts * pieces :]
    depth = gates[0].shape[0]

    def product(weights, i):
        return sum(
            nn_dot(rows[:, k * depth : (k + 1) * depth], weights[k * pieces + i][...])
            for k in range(parts)
        )

    def step(i):
        gate, up = product(gates, i), product(ups, i)
        sigmoid = 1.0 / (1.0 + jnp.exp(-gate))
        silu = gate * sigmoid
        activated[...] = (silu * up).astype(jnp.bfloat16)
        gate_slope[...] = up * sigmoid * (1.0 + gate * (1.0 - sigmoid))
        up_slope[...] = silu

    in_turn(per, pieces, step)


def gate_back_kernel(per, parts, pieces, grads, *refs):
    weights, (gate_slope, up_slope, grad_gate, grad_up) = refs[:-4], refs[-4:]
    blocks, _, depth = weights[0].shape

    def step(i):
        grad = 0.0
        for k in range(parts):
            for z in range(blocks):
                at = (k * blocks + z) * depth
                grad = grad + nt_dot(grads[:, at : at + depth], weights[k * pieces + i][z])
        grad_gate[...] = (grad * gate_slope[...]).astype(jnp.bfloat16)
        grad_up[...] = (grad * up_slope[...]).astype(jnp.bfloat16)

    in_turn(per, pieces, step)


def down_kernel(per, parts, pieces, acts, *refs):
    weights, out = refs[:-1], refs[-1]
    depth = weights[0].shape[1]

    def step(k):
        total = sum(
            nn_dot(acts[:, i * depth : (i + 1) * depth], weights[k * pieces + i][0])
            for i in range(pieces)
        )
        out[...] = total.astype(jnp.bfloat16)

    in_turn(per, parts, step)


def turned_kernel(terms, per, parts, pieces, *refs):
    lefts, weights, out = refs[:terms], refs[terms:-1], refs[-1]
    depth = weights[0].shape[1]

    def step(k):
        total = 0.0
        for term, left in enumerate(lefts):
            for i in range(pieces):
                weight = weights[(term * parts + k) * pieces + i]
                total = total + nt_dot(left[:, i * depth : (i + 1) * depth], weight[...])
        out[...] = total.astype(jnp.bfloat16)

    in_turn(per, parts, step)


def wide_call(kernel, whole, weights, tiled, axis, by_piece, outs):
    parts, pieces = len(weights[0]), len(weights[0][0])
    shape = weights[0][0][0].shape
    groups = pieces if by_piece else parts
    if len(shape) == 3 and axis == 0:
        width, block, per = shape[0] * shape[2], (1, *shape[1:]), shape[0]
    else:
        width = shape[axis]
        per = width // min(width, 256)
        block = tuple(n // per if at == axis else n for at, n in enumerate(shape))
    tile = (min(whole[0].shape[0], 1024), width // per)
    count, cols = whole[0].shape[0], groups * width

    def piece_spec(k, i):
        group = i if by_piece else k

        def place(row, col):
            at = jnp.clip(col - group * per, 0, per - 1)
            return tuple(at if dim == axis else 0 for dim in range(len(shape)))

        return pl.BlockSpec(block, place)

    tile_spec = pl.BlockSpec(tile, lambda row, col: (row, col))
    flat = [v for weight in weights for row in weight for v in row]
    return pl.pallas_call(
        functools.partial(kernel, per, parts, pieces),
        grid=(count // tile[0], groups * per),
        in_specs=[pl.BlockSpec((tile[0], v.shape[1]), lambda row, col: (row, 0)) for v in whole]
        + [piece_spec(k, i) for _ in weights for k in range(parts) for i in range(pieces)]
        + [tile_spec] * len(tiled),
        out_specs=[tile_spec] * len(outs),
        out_shape=[jax.ShapeDtypeStruct((count, cols), t) for t in outs],
        compiler_params=pltpu.CompilerParams(vmem_limit_bytes=KERNEL_VMEM),
        cost_estimate=SMALL_COST,
    )(*whole, *flat, *tiled)


def gate_forward(rows, gates, ups):
    outs = (jnp.bfloat16, jnp.float32, jnp.float32)
    return wide_call(gate_kernel, [rows], [gates, ups], [], 1, True, outs)


def gate_backward(grads, downs, gate_slope, up_slope):
    outs = (jnp.bfloat16, jnp.bfloat16)
    return wide_call(gate_back_kernel, [grads], [downs], [gate_slope, up_slope], 1, True, outs)


def down_forward(acts, downs):
    if downs[0][0].shape[2] % LANES:
        rows = [jnp.concatenate([joined_columns(v) for v in row], axis=0) for row in downs]
        return nn_dot(acts, jnp.concatenate(rows, axis=1)).astype(jnp.bfloat16)
    return wide_call(down_kernel, [acts], [downs], [], 0, False, (jnp.bfloat16,))[0]


def turned_product(lefts, weights):
    kernel = functools.partial(turned_kernel, len(lefts))
    return wide_call(kernel, lefts, weights, [], 0, False, (jnp.bfloat16,))[0]


def o_kernel(parts, place, *refs):
    rows, weights, out = refs[:-1 - parts], refs[-1 - parts : -1], refs[-1]
    blocks = weights[0].shape[0]
    depth = rows[0].shape[1]
    at = lax.rem(pl.program_id(0), blocks)
    for k in range(parts):

        @pl.when(pl.program_id(0) // blocks == k)
        def _(k=k):
            total = 0.0
            for i, piece in enumerate(rows):
                group = lax.rem(place[0] + i, len(rows))
                start = pl.multiple_of(group * depth, depth)
                total = total + nn_dot(piece[...], weights[k][at, pl.ds(start, depth), :])
            out[...] = total.astype(jnp.bfloat16)


def o_forward(pieces, weights, place):
    count, depth = pieces[0].shape
    blocks, _, step = weights[0].shape
    if step % LANES:
        full = jnp.concatenate([joined_columns(v) for v in weights], axis=1)
        return nn_dot(in_groups(pieces), full).astype(jnp.bfloat16)
    whole = pl.BlockSpec(weights[0].shape, lambda j: (0, 0, 0))
    return pl.pallas_call(
        functools.partial(o_kernel, len(weights)),
        grid=(len(weights) * blocks,),
        in_specs=[pl.BlockSpec(memory_space=pltpu.SMEM)]
        + [pl.BlockSpec((count, depth), lambda j: (0, 0))] * len(pieces)
        + [whole] * len(weights),
        out_specs=pl.BlockSpec((count, step), lambda j: (0, j)),
        out_shape=jax.ShapeDtypeStruct((count, len(weights) * blocks * step), jnp.bfloat16),
        compiler_params=pltpu.CompilerParams(vmem_limit_bytes=KERNEL_VMEM),
        cost_estimate=SMALL_COST,
    )(place.astype(jnp.int32).reshape(1), *pieces, *weights)


def o_back_kernel(parts, rows, *refs):
    weights, out = refs[:parts], refs[parts]
    blocks, _, step = weights[0].shape
    total = 0.0
    for k in range(parts):
        for z in range(blocks):
            at = (k * blocks + z) * step
            total = total + nt_dot(rows[:, at : at + step], weights[k][z])
    out[...] = total.astype(jnp.bfloat16)


def o_backward(rows, weights):
    return pl.pallas_call(
        functools.partial(o_back_kernel, len(weights)),
        out_shape=jax.ShapeDtypeStruct((rows.shape[0], weights[0].shape[1]), jnp.bfloat16),
        compiler_params=pltpu.CompilerParams(vmem_limit_bytes=KERNEL_VMEM),
        cost_estimate=SMALL_COST,
    )(rows, *weights)


def split_kernel(*refs):
    values, out = refs[:-1], refs[-1]
    for i, value in enumerate(values):
        out[0, i] = value[...]


def split_columns(values, count):
    rows, cols = values[0].shape
    step = cols // count
    if step % LANES:
        return jnp.stack([column_blocks(v, count) for v in values], axis=1)
    return pl.pallas_call(
        split_kernel,
        grid=(count,),
        in_specs=[pl.BlockSpec((rows, step), lambda j: (0, j))] * len(values),
        out_specs=pl.BlockSpec((1, len(values), rows, step), lambda j: (j, 0, 0, 0)),
        out_shape=jax.ShapeDtypeStruct((count, len(values), rows, step), values[0].dtype),
        compiler_params=pltpu.CompilerParams(vmem_limit_bytes=KERNEL_VMEM),
        cost_estimate=SMALL_COST,
    )(*values)


def finish_kernel(pair, single, first, second, third):
    first[...] = pair[0, 0].astype(jnp.float32)
    second[...] = pair[0, 1].astype(jnp.float32).T
    third[...] = single[0].astype(jnp.float32)


def finished(pair, single):
    count, _, rows, cols = pair.shape
    if cols % LANES or rows % LANES:
        first, second, third = (joined_columns(v) for v in (pair[:, 0], pair[:, 1], single))
        return [v.astype(jnp.float32) for v in (first, second.T, third)]
    side = pl.BlockSpec((rows, cols), lambda z: (0, z))
    return pl.pallas_call(
        finish_kernel,
        grid=(count,),
        in_specs=[
            pl.BlockSpec((1, 2, rows, cols), lambda z: (z, 0, 0, 0)),
            pl.BlockSpec((1, rows, cols), lambda z: (z, 0, 0)),
        ],
        out_specs=[side, pl.BlockSpec((cols, rows), lambda z: (z, 0)), side],
        out_shape=[
            jax.ShapeDtypeStruct((rows, count * cols), jnp.float32),
            jax.ShapeDtypeStruct((count * cols, rows), jnp.float32),
            jax.ShapeDtypeStruct((rows, count * cols), jnp.float32),
        ],
        compiler_params=pltpu.CompilerParams(vmem_limit_bytes=KERNEL_VMEM),
        cost_estimate=SMALL_COST,
    )(pair, single)


def row_norm(value):
    inverse = lax.rsqrt(jnp.mean(value * value, axis=-1, keepdims=True) + norm_eps)
    return value * inverse, inverse


def norm_back(grad, normed, inverse, gain):
    scaled = grad * gain
    return inverse * (scaled - normed * jnp.mean(scaled * normed, axis=-1, keepdims=True))


def silu_parts(gate_pre):
    sigmoid = jax.nn.sigmoid(gate_pre)
    return sigmoid, gate_pre * sigmoid


def halves(value, count):
    part = value.shape[1] // count
    return [value[:, i * part : (i + 1) * part] for i in range(count)]


def crossed(by_x, by_y):
    half = by_x[0].shape[0] // 2
    upper = [[rotated(v[:half], "x", i) for i in range(1, len(by_x))] for v in by_y[1:]]
    lower = [[rotated(v[half:], "y", k) for v in by_x[1:]] for k in range(1, len(by_y))]
    return upper, lower


def quarters(by_x, by_y, upper, lower):
    far = [[jnp.concatenate(v, axis=0) for v in zip(*rows)] for rows in zip(upper, lower)]
    return [by_x] + [[by_y[k], *far[k - 1]] for k in range(1, len(by_y))]


def matmul(left, right):
    return jnp.dot(left, right, preferred_element_type=jnp.float32)


def matmul_turned(left, right):
    return nt_dot(left, right)


def turned_matmul(left, right):
    return lax.dot_general(
        left, right, (((0,), (0,)), ((), ())), preferred_element_type=jnp.float32
    )


def sent_groups(value):
    size = lax.axis_size("y")
    place = lax.axis_index("y")
    width = value.shape[1] // size
    pieces = []
    for k in range(size):
        start = lax.rem(place + k, size) * width
        piece = lax.dynamic_slice_in_dim(value, start, width, 1)
        pieces.append(rotated(piece, "y", k) if k else piece)
    return pieces


def in_groups(pieces):
    size = len(pieces)
    place = lax.axis_index("y")
    return jnp.concatenate(
        [
            lax.select_n(place, *[pieces[(j - i) % size] for i in range(size)])
            for j in range(size)
        ],
        axis=1,
    )


def in_order(pieces):
    return natural_pieces(pieces, "y")


def turned_sum_kernel(blocks, cosine, sine, out):
    total = sum(blocks[i, 0].astype(jnp.float32) for i in range(blocks.shape[0]))
    cos, sin = key_tables(cosine[...], sine[...])
    out[...] = turned(total.T, cos, sin, -1.0).astype(jnp.bfloat16)


def turned_sum(blocks, cosine, sine):
    terms, segs, lanes, seg = blocks.shape
    table = pl.BlockSpec((seg, lanes), lambda s: (s, 0))
    return pl.pallas_call(
        turned_sum_kernel,
        grid=(segs,),
        in_specs=[pl.BlockSpec((terms, 1, lanes, seg), lambda s: (0, s, 0, 0)), table, table],
        out_specs=table,
        out_shape=jax.ShapeDtypeStruct((segs * seg, lanes), jnp.bfloat16),
        compiler_params=pltpu.CompilerParams(vmem_limit_bytes=KERNEL_VMEM),
        cost_estimate=SMALL_COST,
    )(blocks, cosine, sine)


def gathered_core(x_pieces):
    rows = jnp.stack(natural_pieces(x_pieces, "x"))
    rows = jnp.stack(natural_pieces(relative_pieces(rows, "c"), "c"), axis=1)
    return rows.reshape(-1, rows.shape[-1])


def own_first(value, axis):
    size = value.shape[0]
    place = lax.axis_index(axis)
    return [
        lax.dynamic_index_in_dim(value, lax.rem(place - k + size, size), 0, keepdims=False)
        for k in range(size)
    ]


def core_sum(part, rows):
    blocks = part.reshape(lax.axis_size("x"), lax.axis_size("c"), rows, -1)
    return summed_pieces(own_first(blocks.transpose(1, 0, 2, 3), "c"), "c").astype(jnp.bfloat16)


def x_blocks(value):
    return own_first(value, "x")


def tensor_sum(part, rows):
    return summed_pieces(x_blocks(core_sum(part, rows)), "x")


def local(
    tokens,
    norm_gain,
    q_weight,
    key_matrix,
    value_matrix,
    o_weight,
    mlp_gain,
    gate_weight,
    up_weight,
    down_weight,
    parents,
    out_grad,
):
    z_size, y_size, x_size = (lax.axis_size(name) for name in ("z", "y", "x"))
    tensor_size = x_size * lax.axis_size("c")
    low = jnp.bfloat16
    local_rows, width = tokens.shape
    group_rows = local_rows * tensor_size
    kv_cols = key_matrix.shape[1]
    kv_local = kv_cols // HEAD_SIZE
    q_cols = q_weight.shape[1]
    own_width = norm_gain.shape[0]

    own_tokens = relative_columns(tokens)
    own_grad = relative_columns(out_grad).astype(jnp.float32)
    both_gains = jnp.concatenate([norm_gain, mlp_gain])
    both_gains = jnp.pad(both_gains, (0, -both_gains.shape[0] % (2 * kv_cols)))
    key_heads, value_heads = halves(key_matrix, kv_local), halves(value_matrix, kv_local)
    kv_shard = jnp.concatenate(
        [
            jnp.concatenate([v for kv in zip(key_heads, value_heads) for v in kv], axis=1),
            both_gains.reshape(-1, 2 * kv_cols),
        ],
        axis=0,
    )
    kv_copies = jnp.broadcast_to(kv_shard[None], (z_size, *kv_shard.shape))
    kv_copies, q_weight = together(kv_copies, q_weight)
    kv_z = exchanged(kv_copies, "z")
    q_z = lax.all_gather(q_weight, "z", axis=0, tiled=True)
    group_tokens = gathered_core(relative_pieces(own_tokens, "x"))
    kv_z, o_weight = together(kv_z, o_weight)
    o_z = lax.all_gather(o_weight, "z", axis=0)

    depth = segment_depth(parents)
    seg_count = group_rows // SEG
    z_place, y_place = lax.axis_index("z"), lax.axis_index("y")
    sources = [lax.rem(y_place - k + y_size, y_size) for k in range(y_size)]
    segs = jnp.concatenate(
        [
            (z_place * y_size + source) * seg_count + jnp.arange(seg_count, dtype=jnp.int32)
            for source in sources
        ]
    )
    seg_ids = jnp.arange(depth.shape[0], dtype=jnp.int32)
    seg_depth = jnp.sum(jnp.where(segs[:, None] == seg_ids[None, :], depth[None, :], 0), axis=1)
    position = (seg_depth[:, None] * SEG + jnp.arange(SEG, dtype=jnp.int32)[None, :]).reshape(-1)
    cosine_table, sine_table = rope_tables(position, HEAD_SIZE)
    cosine_lanes = jnp.tile(cosine_table, (1, 4))
    sine_lanes = jnp.tile(sine_table, (1, 4))
    ordered = [jnp.concatenate(in_order(jnp.split(v, y_size))) for v in (cosine_lanes, sine_lanes)]
    cosine_lanes, sine_lanes, *ordered = settled(cosine_lanes, sine_lanes, *ordered)

    kv_zy = relative_pieces(kv_z, "y")
    kv_zy, cosine_lanes, sine_lanes, ordered = together(kv_zy, cosine_lanes, sine_lanes, ordered)
    kv_weights = [v[:, :own_width].reshape(-1, 2 * kv_cols) for v in kv_zy]
    gains = [
        v[:, own_width:].reshape(z_size, -1)[:, : 2 * own_width].reshape(z_size, 2, own_width)
        for v in kv_zy
    ]
    gains = jnp.stack(gains).astype(jnp.float32)
    gain_one, gain_two = gains[:, :, 0].reshape(-1), gains[:, :, 1].reshape(-1)
    inputs = own_tokens.astype(jnp.float32)
    normed_one, inv_one = row_norm(inputs)
    group_normed, _ = row_norm(group_tokens.astype(jnp.float32))
    rows_one = (group_normed * gain_one).astype(low)
    rows_one, q_z = together(rows_one, q_z)
    q_weights = relative_pieces(q_z, "y")
    kv_rows = project(rows_one, kv_weights, cosine_lanes, sine_lanes, keys=True)
    kv_swapped = jnp.stack(natural_pieces(sent_groups(kv_rows), "y"))
    all_kv = gathered(kv_swapped, "z").reshape(-1, SEG, LANES)
    wide_blocks = split_columns(after((gate_weight, up_weight), kv_z), z_size)
    q_weights, wide_blocks = together(q_weights, wide_blocks)
    query_rows = project(rows_one, q_weights, cosine_lanes, sine_lanes)
    queries = sent_groups(query_rows)
    all_kv, queries, o_z, wide_blocks = together(all_kv, queries, o_z, wide_blocks)

    wide_z = exchanged(wide_blocks, "z")
    o_weights = relative_pieces(o_z, "y")
    seg_lists = jnp.split(segs, y_size)
    attends, lows = [None] * y_size, [None] * y_size
    for k in range(y_size - 1, 0, -1):
        *attends[k], lows[k] = attend(parents, seg_lists[k], queries[k], all_kv)
    queries[0], attends[1:], lows[1:] = together(queries[0], attends[1:], lows[1:])
    returned = [rotated(v, "y", -k) for k, v in enumerate(lows[1:], 1)]
    *attends[0], lows[0] = attend(parents, seg_lists[0], queries[0], all_kv)
    attn_pieces = [lows[0], *returned]
    attn_pieces, o_weights = together(attn_pieces, o_weights)
    attn_part = o_forward(attn_pieces, o_weights, y_place)
    attn_low = in_groups(attn_pieces)
    attn_core = core_sum(attn_part, local_rows)
    attn_core, wide_z = together(attn_core, wide_z)

    gate_z, up_z = (wide_z[:, i].reshape(z_size * own_width, -1) for i in range(2))
    gate_zy, up_zy = relative_pieces(gate_z, "y"), relative_pieces(up_z, "y")
    gate_zx = relative_pieces(gate_z, "x")
    attn_mine = summed_pieces(x_blocks(attn_core), "x")
    attn_mine, up_z, down_weight = together(attn_mine, up_z, down_weight)

    middle = inputs + branch_scale * attn_mine
    normed_two, inv_two = row_norm(middle)
    hidden_two = (normed_two * gain_two).astype(low)
    rows_two = lax.all_gather(hidden_two, ("z", "c"), axis=0, tiled=True)
    down_z = exchanged(down_weight.reshape(z_size, -1, own_width), "z")
    gate_zx, gate_zy, up_z = together(gate_zx, gate_zy, up_z)
    gate_far = [relative_pieces(v, "y")[1:] for v in gate_zx[1:]]
    up_zx = relative_pieces(up_z, "x")
    grad_mlp = (branch_scale * own_grad).astype(low)
    up_zx, up_zy, grad_mlp, down_z = together(up_zx, up_zy, grad_mlp, down_z)
    grad_mlp_rows = lax.all_gather(grad_mlp, ("z", "c"), axis=0, tiled=True)
    up_far = [relative_pieces(v, "x")[1:] for v in up_zy[1:]]
    rows_two, gate_far, up_far, down_z = together(rows_two, gate_far, up_far, down_z)
    down_zy, down_zx = relative_pieces(down_z, "y"), relative_pieces(down_z, "x")
    gates = [gate_zx] + [[gate_zy[k], *[v[k - 1] for v in gate_far]] for k in range(1, y_size)]
    ups = [up_zx] + [[up_zy[k], *up_far[k - 1]] for k in range(1, y_size)]
    activated, gate_slope, up_slope = gate_forward(rows_two, gates, ups)
    down_zy, down_zx, activated, gate_slope, up_slope = together(
        down_zy, down_zx, activated, gate_slope, up_slope
    )
    down_crossed = together(*crossed(down_zx, down_zy))
    downs = quarters(down_zx, down_zy, *down_crossed)
    mlp_part = down_forward(activated, downs)
    mlp_part, grad_mlp_rows = together(mlp_part, grad_mlp_rows)

    mlp_mine = lax.psum_scatter(mlp_part, ("z", "c"), scatter_dimension=0, tiled=True)
    grad_parts, rows_parts = halves(grad_mlp_rows, y_size), halves(rows_two, y_size)
    acts = halves(activated, x_size)
    down_far = [summed_pieces([turned_matmul(a, b) for a in grad_parts], "y").astype(low) for b in acts[1:]]
    grad_gate_act, grad_up_act = gate_backward(grad_mlp_rows, downs, gate_slope, up_slope)
    grad_gate_act, grad_up_act = together(grad_gate_act, grad_up_act)

    gate_parts, up_parts = halves(grad_gate_act, x_size), halves(grad_up_act, x_size)
    gate_dots = [[turned_matmul(a, b) for a in rows_parts] for b in gate_parts[1:]]
    up_dots = [[turned_matmul(a, b) for b in up_parts] for a in rows_parts[1:]]
    for dots in gate_dots + up_dots:
        dots[1:] = [v.astype(low) for v in dots[1:]]
    grad_gate_act, gate_dots, up_dots = together(grad_gate_act, gate_dots, up_dots)
    gate_far = [summed_pieces(v, "y").astype(low) for v in gate_dots]
    up_far = [summed_pieces(v, "x").astype(low) for v in up_dots]
    input_part = turned_product([grad_gate_act, grad_up_act], [gates, ups])
    input_part, down_far = together(input_part, down_far)

    grad_rows_two = lax.psum_scatter(input_part, ("z", "c"), scatter_dimension=0, tiled=True)
    gate_far, up_far, acts = together(gate_far, up_far, acts)
    down_near = summed_pieces([turned_matmul(a, acts[0]) for a in grad_parts], "y")
    down_far = [rotated(v, "x", -1 - i) for i, v in enumerate(down_far)]
    down_near, down_far, mlp_mine = together(down_near, down_far, mlp_mine)
    mixed = natural_columns((middle + branch_scale * mlp_mine.astype(jnp.float32)).astype(low))
    grad_down_z = sum([v.astype(jnp.float32) for v in down_far], down_near).astype(low)
    gate_near = summed_pieces([turned_matmul(a, gate_parts[0]) for a in rows_parts], "y")
    gate_far = [rotated(v, "x", -1 - i) for i, v in enumerate(gate_far)]
    up_near = [turned_matmul(rows_parts[0], b) for b in up_parts]
    up_near[1:] = [v.astype(low) for v in up_near[1:]]
    grad_rows_two, mixed, up_far, up_near, grad_down_z = together(
        grad_rows_two, mixed, up_far, up_near, grad_down_z
    )
    grad_rows_two = grad_rows_two.astype(jnp.float32)
    gain_two_part = jnp.sum(grad_rows_two * normed_two, axis=0)
    grad_middle = own_grad + norm_back(grad_rows_two, normed_two, inv_two, gain_two)
    grad_attn = (branch_scale * grad_middle).astype(low)
    attn_x = relative_pieces(grad_attn, "x")
    up_far = [rotated(v, "y", -1 - i) for i, v in enumerate(up_far)]
    grad_gate_z = sum([v.astype(jnp.float32) for v in gate_far], gate_near).astype(low)
    wide_z = jnp.stack([v.reshape(z_size, own_width, -1) for v in (grad_gate_z, grad_down_z)], 1)
    attn_x, wide_z, up_near = together(attn_x, wide_z, up_near)
    grad_attn_rows = gathered_core(attn_x)
    grad_heads = o_backward(grad_attn_rows, o_weights)
    grad_heads, grad_attn_rows, up_near, wide_z = together(
        grad_heads, grad_attn_rows, up_near, wide_z
    )
    wide_z = exchanged(wide_z, "z")

    grad_heads = sent_groups(grad_heads)
    o_dots = [turned_matmul(v, attn_low) for v in halves(grad_attn_rows, y_size)[1:]]
    o_dots = [v.astype(low) for v in o_dots]
    grad_heads, o_dots, up_near, grad_attn_rows = together(
        grad_heads, o_dots, up_near, grad_attn_rows
    )
    o_sent = [rotated(v, "y", -1 - i) for i, v in enumerate(o_dots)]
    up_mine = [rotated(v, "x", -1 - i) for i, v in enumerate(up_near[1:])]
    grad_queries, sums = [None] * y_size, None
    for k in range(y_size - 1, 0, -1):
        grad_queries[k], sums = attend_back(
            parents, seg_lists[k], queries[k], grad_heads[k], *attends[k], cosine_lanes,
            sine_lanes, k, all_kv, sums,
        )
    grad_o_y = turned_matmul(halves(grad_attn_rows, y_size)[0], attn_low)
    grad_o_y = sum([v.astype(jnp.float32) for v in o_sent], grad_o_y).astype(low)
    grad_queries[1:], sums, grad_o_y = together(grad_queries[1:], sums, grad_o_y)
    grad_o = lax.psum_scatter(grad_o_y, "z", scatter_dimension=0, tiled=True)
    returned = [rotated(v, "y", -k) for k, v in enumerate(grad_queries[1:], 1)]
    grad_queries[0], grad_kv = attend_back(
        parents, seg_lists[0], queries[0], grad_heads[0], *attends[0], cosine_lanes, sine_lanes,
        0, all_kv, sums,
    )
    grad_kv, wide_z = together(grad_kv, wide_z)
    grad_queries[0], returned, up_far, up_mine, up_near = after(
        (grad_queries[0], returned, up_far, up_mine, up_near), grad_kv
    )

    def owned_dots(left, right):
        dots = [turned_matmul(v, right) for v in halves(left, y_size)]
        return dots[:1] + [v.astype(low) for v in dots[1:]]

    def sent_back(dots):
        return [rotated(v, "y", -1 - i) for i, v in enumerate(dots[1:])]

    def total(own, sent):
        return sum([v.astype(jnp.float32) for v in sent], own).astype(low)

    kv_mine = exchanged(grad_kv.reshape(z_size, y_size * seg_count, LANES, SEG), "z")
    grad_queries = in_groups([grad_queries[0], *returned])
    query_dots = owned_dots(rows_one, grad_queries)
    query_sent = sent_back(query_dots)
    q_full = jnp.concatenate(q_weights, axis=0)
    query_part = matmul_turned(grad_queries, q_full)
    grad_up_z = total(up_near[0], up_far + up_mine)
    kv_mine, query_part, query_dots, query_sent, grad_up_z, grad_o = together(
        kv_mine, query_part, query_dots, query_sent, grad_up_z, grad_o
    )

    grad_up = exchanged(grad_up_z.reshape(z_size, own_width, -1), "z")
    kv_mine = turned_sum(kv_mine, *ordered).reshape(y_size, group_rows, LANES)
    kv_mine = own_first(kv_mine, "y")
    grad_kv_rows = in_groups(
        [kv_mine[0]] + [rotated(v, "y", -k) for k, v in enumerate(kv_mine[1:], 1)]
    )
    kv_full = jnp.concatenate(kv_weights, axis=0)
    input_one = (query_part + matmul_turned(grad_kv_rows, kv_full)).astype(low)
    input_core = core_sum(input_one, local_rows)
    grad_q_y = total(query_dots[0], query_sent)
    kv_dots = owned_dots(rows_one, grad_kv_rows)
    kv_sent = sent_back(kv_dots)
    input_core, grad_q_y, grad_up, wide_z, grad_o = together(
        input_core, grad_q_y, grad_up, wide_z, grad_o
    )
    grad_q = lax.psum_scatter(grad_q_y, "z", scatter_dimension=0, tiled=True)
    input_x = x_blocks(input_core)
    input_sent = [rotated(v, "x", -1 - i) for i, v in enumerate(input_x[1:])]
    input_x[0], input_sent, kv_sent, kv_dots, wide_z, grad_up, grad_o = together(
        input_x[0], input_sent, kv_sent, kv_dots, wide_z, grad_up, grad_o
    )
    grad_rows_one = sum([v.astype(jnp.float32) for v in input_sent], input_x[0].astype(jnp.float32))
    kv_blocks = own_first(total(kv_dots[0], kv_sent).reshape(z_size, own_width, -1), "z")
    kv_sent = [rotated(v, "z", -1 - i) for i, v in enumerate(kv_blocks[1:])]
    gain_one_part = jnp.sum(grad_rows_one * normed_one, axis=0)
    grad_inputs = grad_middle + norm_back(grad_rows_one, normed_one, inv_one, gain_one)
    gain_parts = jnp.stack([gain_one_part, gain_two_part], axis=0)
    gain_parts = natural_columns(gain_parts).reshape(2, z_size * y_size, 1, own_width)
    gain_parts = jnp.broadcast_to(
        gain_parts, (2, z_size * y_size, tensor_size, own_width)
    ).reshape(2, -1, own_width).transpose(1, 0, 2)
    gain_parts = exchanged(gain_parts, ("z", "y", "x", "c"))
    grad_tokens = natural_columns(grad_inputs.astype(low))
    gain_parts, kv_sent, kv_blocks, wide_z, grad_up, grad_o, grad_tokens = together(
        gain_parts, kv_sent, kv_blocks, wide_z, grad_up, grad_o, grad_tokens
    )
    gain_sums = jnp.sum(gain_parts, axis=0)
    grad_gate, grad_down, grad_up = finished(wide_z, grad_up)
    grad_o = grad_o.astype(jnp.float32).T
    grad_kv_weight = sum([v.astype(jnp.float32) for v in kv_sent], kv_blocks[0].astype(jnp.float32))
    grad_q = grad_q.astype(jnp.float32)
    grad_heads = halves(grad_kv_weight, 2 * kv_local)
    return (
        mixed,
        grad_tokens,
        gain_sums[0],
        grad_q,
        jnp.concatenate(grad_heads[::2], axis=1),
        jnp.concatenate(grad_heads[1::2], axis=1),
        grad_o,
        gain_sums[1],
        grad_gate,
        grad_up,
        grad_down,
    )


def solution(mesh):
    dp_size, tensor_size = mesh.shape["dp"], mesh.shape["tensor"]
    fine = jax.sharding.Mesh(
        mesh.devices.reshape(dp_size // 2, 2, tensor_size // 2, 2), ("z", "y", "x", "c")
    )
    dp, tensor = ("z", "y"), ("x", "c")
    tokens = P(dp + tensor, None)
    rows = P(dp, tensor)
    columns = P(tensor, dp)
    in_specs = (
        tokens,
        P(dp),
        rows,
        rows,
        rows,
        columns,
        P(dp),
        rows,
        rows,
        columns,
        P(),
        tokens,
    )
    out_specs = (
        tokens,
        tokens,
        P(dp),
        rows,
        rows,
        rows,
        columns,
        P(dp),
        rows,
        rows,
        columns,
    )
    return jax.shard_map(local, mesh=fine, in_specs=in_specs, out_specs=out_specs, check_vma=False)
```

```python
import functools

import jax
import jax.numpy as jnp
from jax import lax
from jax.experimental import pallas as pl
from jax.experimental.pallas import tpu as pltpu
from jax.sharding import PartitionSpec as P

HEAD_SIZE = 64
SEG = 256
MAX_STEPS = 9
LANES = 2 * HEAD_SIZE
KERNEL_VMEM = 32 * 2**20
SMALL_COST = pl.CostEstimate(flops=2**28, bytes_accessed=2**18, transcendentals=0)


attn_scale = 0.015625
branch_scale = 0.22
norm_eps = 1e-05
rope_base = 10000000.0
masked_score = -1e30


def segment_depth(parents):
    seg_total = parents.shape[0]
    seg_ids = jnp.arange(seg_total, dtype=jnp.int32)
    reach = (parents[:, None] == seg_ids[None, :]) | (seg_ids[:, None] == seg_ids[None, :])
    reach = reach.astype(jnp.float32)
    for doubling in range(4):
        reach = jnp.minimum(jnp.dot(reach, reach, preferred_element_type=jnp.float32), 1.0)
    return jnp.sum(reach, axis=1).astype(jnp.int32) - 1


def rope_tables(position, head_dim):
    half_dim = head_dim // 2
    exponent = jnp.arange(half_dim, dtype=jnp.float32) * (2.0 / head_dim)
    inverse = jnp.power(rope_base, -exponent)
    angles = position.astype(jnp.float32)[:, None] * inverse[None, :]
    return (jnp.cos(angles), jnp.sin(angles))


def rotated(value, axis, step):
    size = lax.axis_size(axis)
    return lax.ppermute(value, axis, [(i, (i + step) % size) for i in range(size)])


def relative_pieces(value, axis):
    return [value] + [rotated(value, axis, k) for k in range(1, lax.axis_size(axis))]


def natural_pieces(pieces, axis):
    size = len(pieces)
    place = lax.axis_index(axis)
    return [
        lax.select_n(place, *[pieces[(i - j) % size] for i in range(size)]) for j in range(size)
    ]


def gathered(value, axis):
    size = lax.axis_size(axis)
    copies = jnp.broadcast_to(value[None], (size, *value.shape))
    return lax.all_to_all(copies, axis, 0, 0, tiled=True)


def exchanged(blocks, axis):
    return lax.all_to_all(blocks, axis, 0, 0, tiled=True)


def summed_pieces(pieces, axis):
    sent = [rotated(pieces[k].astype(jnp.bfloat16), axis, -k) for k in range(1, len(pieces))]
    total = pieces[0].astype(jnp.float32)
    for value in sent:
        total = total + value.astype(jnp.float32)
    return total


def summed_blocks(blocks, axis):
    return jnp.sum(exchanged(blocks.astype(jnp.bfloat16), axis).astype(jnp.float32), axis=0)


def column_blocks(value, count):
    return value.reshape(value.shape[0], count, -1).transpose(1, 0, 2)


def joined_columns(blocks):
    return blocks.transpose(1, 0, 2).reshape(blocks.shape[1], -1)


def relative_columns(value):
    size = lax.axis_size("y")
    place = lax.axis_index("y")
    rows = value.shape[0]
    split = value.reshape(rows, lax.axis_size("z"), size, -1)
    flat = [split[:, :, i].reshape(rows, -1) for i in range(size)]
    return jnp.concatenate(
        [
            lax.select_n(place, *[flat[(i - k) % size] for i in range(size)])
            for k in range(size)
        ],
        axis=1,
    )


def natural_columns(value):
    size = lax.axis_size("y")
    rows = value.shape[0]
    split = value.reshape(rows, size, lax.axis_size("z"), -1)
    parts = natural_pieces([split[:, k] for k in range(size)], "y")
    return jnp.stack(parts, axis=2).reshape(rows, -1)


def together(*values):
    return lax.optimization_barrier(values)


def after(value, *others):
    return lax.optimization_barrier((value, *others))[0]


def ancestor_count(parents, seg):
    def climb(step, state):
        current, count = state
        above = parents[current]
        return above, count + jnp.where(above != current, 1, 0)

    return lax.fori_loop(0, MAX_STEPS, climb, (seg, jnp.int32(1)))[1]


def left_lanes(shape):
    return lax.broadcasted_iota(jnp.int32, shape, 1) < HEAD_SIZE


def stacked_heads(pairs, to_left):
    left = left_lanes(pairs[0].shape)
    stack = []
    for pair in pairs:
        swapped = pltpu.roll(pair, HEAD_SIZE, 1)
        for head in (pair, swapped) if to_left else (swapped, pair):
            stack.append(jnp.where(left, head, 0.0) if to_left else jnp.where(left, 0.0, head))
    return jnp.concatenate(stack, axis=0)


def unstacked_heads(stack, from_left):
    left = left_lanes((SEG, 2 * HEAD_SIZE))
    pairs = []
    for first in range(0, stack.shape[0], 2 * SEG):
        even, odd = stack[first : first + SEG], stack[first + SEG : first + 2 * SEG]
        if from_left:
            odd = pltpu.roll(odd, HEAD_SIZE, 1)
        else:
            even = pltpu.roll(even, HEAD_SIZE, 1)
        pairs.append(jnp.where(left, even, odd))
    return pairs


def turned(value, cosine, sine, direction):
    half = HEAD_SIZE // 2
    lane = lax.broadcasted_iota(jnp.int32, value.shape, 1)
    first = lax.rem(lane, HEAD_SIZE) < half
    ahead = pltpu.roll(value, LANES - half, 1)
    behind = pltpu.roll(value, half, 1)
    signed = sine * direction
    return value * cosine + jnp.where(first, -ahead * signed, behind * signed)


def nt_dot(left, right):
    return lax.dot_general(
        left, right, (((1,), (1,)), ((), ())), preferred_element_type=jnp.float32
    )


def nn_dot(left, right):
    return lax.dot_general(
        left, right, (((1,), (0,)), ((), ())), preferred_element_type=jnp.float32
    )


def causal_tile(rows):
    query = lax.rem(lax.broadcasted_iota(jnp.int32, (rows, SEG), 0), SEG)
    return lax.broadcasted_iota(jnp.int32, (rows, SEG), 1) <= query


def lane_blocks(ref):
    return [ref[:, at : at + LANES] for at in range(0, ref.shape[1], LANES)]


def key_tables(cosine, sine):
    left = left_lanes(cosine.shape)
    return jnp.where(left, cosine, 1.0), jnp.where(left, sine, 0.0)


def settle_kernel(*refs):
    count = len(refs) // 2
    for value, out in zip(refs[:count], refs[count:]):
        out[...] = value[...]


def settled(*values):
    return pl.pallas_call(
        settle_kernel,
        out_shape=[jax.ShapeDtypeStruct(v.shape, v.dtype) for v in values],
        compiler_params=pltpu.CompilerParams(vmem_limit_bytes=KERNEL_VMEM),
        cost_estimate=SMALL_COST,
    )(*values)


def project_kernel(parts, keys, rows, *refs):
    weights, (cosine, sine, out) = refs[:parts], refs[parts:]
    depth = weights[0].shape[0]
    product = sum(nn_dot(rows[:, i * depth : (i + 1) * depth], w[...]) for i, w in enumerate(weights))
    cos, sin = cosine[...], sine[...]
    if keys:
        cos, sin = key_tables(cos, sin)
    for at in range(0, product.shape[1], LANES):
        block = turned(product[:, at : at + LANES], cos, sin, 1.0)
        out[:, at : at + LANES] = block.astype(jnp.bfloat16)


def project(rows, weights, cosine, sine, keys=False):
    count, width = rows.shape
    depth, cols = weights[0].shape
    step = 2 * LANES
    table = pl.BlockSpec((count, LANES), lambda j: (0, 0))
    return pl.pallas_call(
        functools.partial(project_kernel, len(weights), keys),
        grid=(cols // step,),
        in_specs=[pl.BlockSpec((count, width), lambda j: (0, 0))]
        + [pl.BlockSpec((depth, step), lambda j: (0, j))] * len(weights)
        + [table, table],
        out_specs=pl.BlockSpec((count, step), lambda j: (0, j)),
        out_shape=jax.ShapeDtypeStruct((count, cols), jnp.bfloat16),
        compiler_params=pltpu.CompilerParams(vmem_limit_bytes=KERNEL_VMEM),
        cost_estimate=SMALL_COST,
    )(rows, *weights, cosine, sine)


def attend_kernel(parents, segs, queries, keys_values, out, stats, out_low, scores):
    seg = segs[pl.program_id(0)]
    count = ancestor_count(parents, seg)
    pairs = [block.astype(jnp.float32) * attn_scale for block in lane_blocks(queries)]
    stack = stacked_heads(pairs, True).astype(jnp.bfloat16)
    rows = stack.shape[0]

    first = jnp.where(causal_tile(rows), nt_dot(stack, keys_values[seg]), masked_score)
    scores[0] = first

    def folded(tile):
        return jnp.maximum(tile[:, :LANES], tile[:, LANES:])

    def measure(step, state):
        current, top = state
        current = parents[current]
        tile = nt_dot(stack, keys_values[current])
        scores[step] = tile
        return current, jnp.maximum(top, folded(tile))

    top = lax.fori_loop(1, count, measure, (seg, folded(first)))[1]
    row_max = jnp.max(top, axis=1, keepdims=True)
    left = left_lanes((SEG, LANES))

    def gather(step, state):
        current, mixed = state
        terms = jnp.exp(scores[step] - row_max).astype(jnp.bfloat16)
        tile = jnp.where(left, jnp.ones((SEG, LANES), jnp.bfloat16), keys_values[current])
        return parents[current], mixed + nn_dot(terms, tile)

    start = (seg, jnp.zeros((rows, LANES), jnp.float32))
    mixed = lax.fori_loop(0, count, gather, start)[1]
    total = mixed[:, :1]
    mixed = mixed / total
    stats[0] = row_max + jnp.log(total)
    for place, pair in enumerate(unstacked_heads(mixed, False)):
        out[:, place * LANES : (place + 1) * LANES] = pair
        out_low[:, place * LANES : (place + 1) * LANES] = pair.astype(jnp.bfloat16)


def attend_back_kernel(
    parents, segs, queries, grads, attended, stats, cosine, sine, keys_values, *refs
):
    earlier, (grad_queries, grad_kv, kv_sum) = refs[:-3], refs[-3:]
    seg = segs[pl.program_id(0)]
    count = ancestor_count(parents, seg)

    @pl.when(pl.program_id(0) == 0)
    def _():
        kv_sum[...] = earlier[0][...] if earlier else jnp.zeros_like(kv_sum)

    query_pairs = [block.astype(jnp.float32) * attn_scale for block in lane_blocks(queries)]
    grad_pairs = [block.astype(jnp.float32) for block in lane_blocks(grads)]
    left = left_lanes((SEG, LANES))
    deltas = []
    for pair, out in zip(grad_pairs, lane_blocks(attended)):
        product = pair * out
        deltas.append(jnp.sum(jnp.where(left, product, 0.0), axis=1, keepdims=True))
        deltas.append(jnp.sum(jnp.where(left, 0.0, product), axis=1, keepdims=True))
    delta = jnp.concatenate(deltas, axis=0)
    query_wide = stacked_heads(query_pairs, True)
    grad_wide = stacked_heads(grad_pairs, False)
    query_stack, grad_stack = query_wide.astype(jnp.bfloat16), grad_wide.astype(jnp.bfloat16)
    query_turned = query_wide.T.astype(jnp.bfloat16)
    grad_turned = grad_wide.T.astype(jnp.bfloat16)
    log_total = stats[0]
    rows = query_stack.shape[0]

    def visit(current, total, diagonal):
        tile_kv = keys_values[current]
        tile = nt_dot(query_stack, tile_kv)
        if diagonal:
            tile = jnp.where(causal_tile(rows), tile, masked_score)
        probs = jnp.exp(tile - log_total)
        grad_probs = nt_dot(grad_stack, tile_kv)
        grad_tile = (probs * (grad_probs - delta)).astype(jnp.bfloat16)
        kv_sum[current] += nn_dot(query_turned, grad_tile) + nn_dot(
            grad_turned, probs.astype(jnp.bfloat16)
        )
        return total + nn_dot(grad_tile, tile_kv)

    total = visit(seg, jnp.zeros((rows, LANES), jnp.float32), True)

    def climb(step, state):
        current, total = state
        current = parents[current]
        return current, visit(current, total, False)

    total = lax.fori_loop(1, count, climb, (seg, total))[1]
    cos, sin = cosine[...], sine[...]
    for place, pair in enumerate(unstacked_heads(total * attn_scale, True)):
        grad_queries[:, place * LANES : (place + 1) * LANES] = turned(
            pair, cos, sin, -1.0
        ).astype(jnp.bfloat16)

    @pl.when(pl.program_id(0) == pl.num_programs(0) - 1)
    def _():
        grad_kv[...] = kv_sum[...].astype(grad_kv.dtype)


def attention_specs(cols, seg_total):
    block = pl.BlockSpec((SEG, cols), lambda s: (s, 0))
    table = pl.BlockSpec((SEG, LANES), lambda s: (s, 0))
    whole = pl.BlockSpec((seg_total, SEG, LANES), lambda s: (0, 0, 0))
    rows = SEG * (cols // HEAD_SIZE)
    stat = pl.BlockSpec((1, rows, 1), lambda s: (s, 0, 0))
    return block, table, whole, rows, stat, pl.BlockSpec(memory_space=pltpu.SMEM)


def attend(parents, segs, queries, keys_values):
    count, cols = queries.shape
    block, table, whole, rows, stat, scalar = attention_specs(cols, keys_values.shape[0])
    steps = count // SEG
    return pl.pallas_call(
        attend_kernel,
        grid=(steps,),
        in_specs=[scalar, scalar, block, whole],
        out_specs=[block, stat, block],
        out_shape=[
            jax.ShapeDtypeStruct((count, cols), jnp.float32),
            jax.ShapeDtypeStruct((steps, rows, 1), jnp.float32),
            jax.ShapeDtypeStruct((count, cols), jnp.bfloat16),
        ],
        scratch_shapes=[pltpu.VMEM((MAX_STEPS + 1, rows, SEG), jnp.float32)],
        compiler_params=pltpu.CompilerParams(vmem_limit_bytes=KERNEL_VMEM),
        cost_estimate=SMALL_COST,
    )(parents, segs, queries, keys_values)


def attend_back(
    parents, segs, queries, grads, attended, stats, cosine, sine, place, keys_values, earlier=None
):
    count, cols = queries.shape
    first = place * (count // SEG)
    seg_total = keys_values.shape[0]
    block, table, whole, rows, stat, scalar = attention_specs(cols, seg_total)
    sums = pl.BlockSpec((seg_total, LANES, SEG), lambda s: (0, 0, 0))
    last = earlier is not None
    sum_type = jnp.bfloat16 if last else jnp.float32
    return pl.pallas_call(
        attend_back_kernel,
        grid=(count // SEG,),
        in_specs=[scalar, scalar, block, block, block, stat]
        + [pl.BlockSpec((SEG, LANES), lambda s: (first + s, 0))] * 2
        + [whole]
        + [sums] * last,
        out_specs=[block, sums],
        out_shape=[
            jax.ShapeDtypeStruct((count, cols), jnp.bfloat16),
            jax.ShapeDtypeStruct((seg_total, LANES, SEG), sum_type),
        ],
        scratch_shapes=[pltpu.VMEM((seg_total, LANES, SEG), jnp.float32)],
        compiler_params=pltpu.CompilerParams(vmem_limit_bytes=56 * 2**20),
        cost_estimate=SMALL_COST,
    )(
        parents, segs, queries, grads, attended, stats, cosine, sine, keys_values,
        *([earlier] if last else []),
    )


def in_turn(per, count, step):
    for i in range(count):
        pl.when(pl.program_id(1) // per == i)(functools.partial(step, i))


def gate_kernel(per, parts, pieces, rows, *refs):
    gates, ups = refs[: parts * pieces], refs[parts * pieces : 2 * parts * pieces]
    activated, gate_slope, up_slope = refs[2 * parts * pieces :]
    depth = gates[0].shape[0]

    def product(weights, i):
        return sum(
            nn_dot(rows[:, k * depth : (k + 1) * depth], weights[k * pieces + i][...])
            for k in range(parts)
        )

    def step(i):
        gate, up = product(gates, i), product(ups, i)
        sigmoid = 1.0 / (1.0 + jnp.exp(-gate))
        silu = gate * sigmoid
        activated[...] = (silu * up).astype(jnp.bfloat16)
        gate_slope[...] = up * sigmoid * (1.0 + gate * (1.0 - sigmoid))
        up_slope[...] = silu

    in_turn(per, pieces, step)


def gate_back_kernel(per, parts, pieces, grads, *refs):
    weights, (gate_slope, up_slope, grad_gate, grad_up) = refs[:-4], refs[-4:]
    blocks, _, depth = weights[0].shape

    def step(i):
        grad = 0.0
        for k in range(parts):
            for z in range(blocks):
                at = (k * blocks + z) * depth
                grad = grad + nt_dot(grads[:, at : at + depth], weights[k * pieces + i][z])
        grad_gate[...] = (grad * gate_slope[...]).astype(jnp.bfloat16)
        grad_up[...] = (grad * up_slope[...]).astype(jnp.bfloat16)

    in_turn(per, pieces, step)


def down_kernel(per, parts, pieces, acts, *refs):
    weights, out = refs[:-1], refs[-1]
    depth = weights[0].shape[1]

    def step(k):
        total = sum(
            nn_dot(acts[:, i * depth : (i + 1) * depth], weights[k * pieces + i][0])
            for i in range(pieces)
        )
        out[...] = total.astype(jnp.bfloat16)

    in_turn(per, parts, step)


def turned_kernel(terms, per, parts, pieces, *refs):
    lefts, weights, out = refs[:terms], refs[terms:-1], refs[-1]
    depth = weights[0].shape[1]

    def step(k):
        total = 0.0
        for term, left in enumerate(lefts):
            for i in range(pieces):
                weight = weights[(term * parts + k) * pieces + i]
                total = total + nt_dot(left[:, i * depth : (i + 1) * depth], weight[...])
        out[...] = total.astype(jnp.bfloat16)

    in_turn(per, parts, step)


def wide_call(kernel, whole, weights, tiled, axis, by_piece, outs):
    parts, pieces = len(weights[0]), len(weights[0][0])
    shape = weights[0][0][0].shape
    groups = pieces if by_piece else parts
    if len(shape) == 3 and axis == 0:
        width, block, per = shape[0] * shape[2], (1, *shape[1:]), shape[0]
    else:
        width = shape[axis]
        per = width // min(width, 256)
        block = tuple(n // per if at == axis else n for at, n in enumerate(shape))
    tile = (min(whole[0].shape[0], 1024), width // per)
    count, cols = whole[0].shape[0], groups * width

    def piece_spec(k, i):
        group = i if by_piece else k

        def place(row, col):
            at = jnp.clip(col - group * per, 0, per - 1)
            return tuple(at if dim == axis else 0 for dim in range(len(shape)))

        return pl.BlockSpec(block, place)

    tile_spec = pl.BlockSpec(tile, lambda row, col: (row, col))
    flat = [v for weight in weights for row in weight for v in row]
    return pl.pallas_call(
        functools.partial(kernel, per, parts, pieces),
        grid=(count // tile[0], groups * per),
        in_specs=[pl.BlockSpec((tile[0], v.shape[1]), lambda row, col: (row, 0)) for v in whole]
        + [piece_spec(k, i) for _ in weights for k in range(parts) for i in range(pieces)]
        + [tile_spec] * len(tiled),
        out_specs=[tile_spec] * len(outs),
        out_shape=[jax.ShapeDtypeStruct((count, cols), t) for t in outs],
        compiler_params=pltpu.CompilerParams(vmem_limit_bytes=KERNEL_VMEM),
        cost_estimate=SMALL_COST,
    )(*whole, *flat, *tiled)


def gate_forward(rows, gates, ups):
    outs = (jnp.bfloat16, jnp.float32, jnp.float32)
    return wide_call(gate_kernel, [rows], [gates, ups], [], 1, True, outs)


def gate_backward(grads, downs, gate_slope, up_slope):
    outs = (jnp.bfloat16, jnp.bfloat16)
    return wide_call(gate_back_kernel, [grads], [downs], [gate_slope, up_slope], 1, True, outs)


def down_forward(acts, downs):
    if downs[0][0].shape[2] % LANES:
        rows = [jnp.concatenate([joined_columns(v) for v in row], axis=0) for row in downs]
        return nn_dot(acts, jnp.concatenate(rows, axis=1)).astype(jnp.bfloat16)
    return wide_call(down_kernel, [acts], [downs], [], 0, False, (jnp.bfloat16,))[0]


def turned_product(lefts, weights):
    kernel = functools.partial(turned_kernel, len(lefts))
    return wide_call(kernel, lefts, weights, [], 0, False, (jnp.bfloat16,))[0]


def o_kernel(parts, place, *refs):
    rows, weights, out = refs[:-1 - parts], refs[-1 - parts : -1], refs[-1]
    blocks = weights[0].shape[0]
    depth = rows[0].shape[1]
    at = lax.rem(pl.program_id(0), blocks)
    for k in range(parts):

        @pl.when(pl.program_id(0) // blocks == k)
        def _(k=k):
            total = 0.0
            for i, piece in enumerate(rows):
                group = lax.rem(place[0] + i, len(rows))
                start = pl.multiple_of(group * depth, depth)
                total = total + nn_dot(piece[...], weights[k][at, pl.ds(start, depth), :])
            out[...] = total.astype(jnp.bfloat16)


def o_forward(pieces, weights, place):
    count, depth = pieces[0].shape
    blocks, _, step = weights[0].shape
    if step % LANES:
        full = jnp.concatenate([joined_columns(v) for v in weights], axis=1)
        return nn_dot(in_groups(pieces), full).astype(jnp.bfloat16)
    whole = pl.BlockSpec(weights[0].shape, lambda j: (0, 0, 0))
    return pl.pallas_call(
        functools.partial(o_kernel, len(weights)),
        grid=(len(weights) * blocks,),
        in_specs=[pl.BlockSpec(memory_space=pltpu.SMEM)]
        + [pl.BlockSpec((count, depth), lambda j: (0, 0))] * len(pieces)
        + [whole] * len(weights),
        out_specs=pl.BlockSpec((count, step), lambda j: (0, j)),
        out_shape=jax.ShapeDtypeStruct((count, len(weights) * blocks * step), jnp.bfloat16),
        compiler_params=pltpu.CompilerParams(vmem_limit_bytes=KERNEL_VMEM),
        cost_estimate=SMALL_COST,
    )(place.astype(jnp.int32).reshape(1), *pieces, *weights)


def o_back_kernel(parts, rows, *refs):
    weights, out = refs[:parts], refs[parts]
    blocks, _, step = weights[0].shape
    total = 0.0
    for k in range(parts):
        for z in range(blocks):
            at = (k * blocks + z) * step
            total = total + nt_dot(rows[:, at : at + step], weights[k][z])
    out[...] = total.astype(jnp.bfloat16)


def o_backward(rows, weights):
    return pl.pallas_call(
        functools.partial(o_back_kernel, len(weights)),
        out_shape=jax.ShapeDtypeStruct((rows.shape[0], weights[0].shape[1]), jnp.bfloat16),
        compiler_params=pltpu.CompilerParams(vmem_limit_bytes=KERNEL_VMEM),
        cost_estimate=SMALL_COST,
    )(rows, *weights)


def split_kernel(*refs):
    values, out = refs[:-1], refs[-1]
    for i, value in enumerate(values):
        out[0, i] = value[...]


def split_columns(values, count):
    rows, cols = values[0].shape
    step = cols // count
    if step % LANES:
        return jnp.stack([column_blocks(v, count) for v in values], axis=1)
    return pl.pallas_call(
        split_kernel,
        grid=(count,),
        in_specs=[pl.BlockSpec((rows, step), lambda j: (0, j))] * len(values),
        out_specs=pl.BlockSpec((1, len(values), rows, step), lambda j: (j, 0, 0, 0)),
        out_shape=jax.ShapeDtypeStruct((count, len(values), rows, step), values[0].dtype),
        compiler_params=pltpu.CompilerParams(vmem_limit_bytes=KERNEL_VMEM),
        cost_estimate=SMALL_COST,
    )(*values)


def finish_kernel(pair, single, first, second, third):
    first[...] = pair[0, 0].astype(jnp.float32)
    second[...] = pair[0, 1].astype(jnp.float32).T
    third[...] = single[0].astype(jnp.float32)


def finished(pair, single):
    count, _, rows, cols = pair.shape
    if cols % LANES or rows % LANES:
        first, second, third = (joined_columns(v) for v in (pair[:, 0], pair[:, 1], single))
        return [v.astype(jnp.float32) for v in (first, second.T, third)]
    side = pl.BlockSpec((rows, cols), lambda z: (0, z))
    return pl.pallas_call(
        finish_kernel,
        grid=(count,),
        in_specs=[
            pl.BlockSpec((1, 2, rows, cols), lambda z: (z, 0, 0, 0)),
            pl.BlockSpec((1, rows, cols), lambda z: (z, 0, 0)),
        ],
        out_specs=[side, pl.BlockSpec((cols, rows), lambda z: (z, 0)), side],
        out_shape=[
            jax.ShapeDtypeStruct((rows, count * cols), jnp.float32),
            jax.ShapeDtypeStruct((count * cols, rows), jnp.float32),
            jax.ShapeDtypeStruct((rows, count * cols), jnp.float32),
        ],
        compiler_params=pltpu.CompilerParams(vmem_limit_bytes=KERNEL_VMEM),
        cost_estimate=SMALL_COST,
    )(pair, single)


def row_norm(value):
    inverse = lax.rsqrt(jnp.mean(value * value, axis=-1, keepdims=True) + norm_eps)
    return value * inverse, inverse


def norm_back(grad, normed, inverse, gain):
    scaled = grad * gain
    return inverse * (scaled - normed * jnp.mean(scaled * normed, axis=-1, keepdims=True))


def silu_parts(gate_pre):
    sigmoid = jax.nn.sigmoid(gate_pre)
    return sigmoid, gate_pre * sigmoid


def halves(value, count):
    part = value.shape[1] // count
    return [value[:, i * part : (i + 1) * part] for i in range(count)]


def crossed(by_x, by_y):
    half = by_x[0].shape[0] // 2
    upper = [[rotated(v[:half], "x", i) for i in range(1, len(by_x))] for v in by_y[1:]]
    lower = [[rotated(v[half:], "y", k) for v in by_x[1:]] for k in range(1, len(by_y))]
    return upper, lower


def quarters(by_x, by_y, upper, lower):
    far = [[jnp.concatenate(v, axis=0) for v in zip(*rows)] for rows in zip(upper, lower)]
    return [by_x] + [[by_y[k], *far[k - 1]] for k in range(1, len(by_y))]


def matmul(left, right):
    return jnp.dot(left, right, preferred_element_type=jnp.float32)


def matmul_turned(left, right):
    return nt_dot(left, right)


def turned_matmul(left, right):
    return lax.dot_general(
        left, right, (((0,), (0,)), ((), ())), preferred_element_type=jnp.float32
    )


def sent_groups(value):
    size = lax.axis_size("y")
    place = lax.axis_index("y")
    width = value.shape[1] // size
    pieces = []
    for k in range(size):
        start = lax.rem(place + k, size) * width
        piece = lax.dynamic_slice_in_dim(value, start, width, 1)
        pieces.append(rotated(piece, "y", k) if k else piece)
    return pieces


def in_groups(pieces):
    size = len(pieces)
    place = lax.axis_index("y")
    return jnp.concatenate(
        [
            lax.select_n(place, *[pieces[(j - i) % size] for i in range(size)])
            for j in range(size)
        ],
        axis=1,
    )


def in_order(pieces):
    return natural_pieces(pieces, "y")


def turned_sum_kernel(blocks, cosine, sine, out):
    total = sum(blocks[i, 0].astype(jnp.float32) for i in range(blocks.shape[0]))
    cos, sin = key_tables(cosine[...], sine[...])
    out[...] = turned(total.T, cos, sin, -1.0).astype(jnp.bfloat16)


def turned_sum(blocks, cosine, sine):
    terms, segs, lanes, seg = blocks.shape
    table = pl.BlockSpec((seg, lanes), lambda s: (s, 0))
    return pl.pallas_call(
        turned_sum_kernel,
        grid=(segs,),
        in_specs=[pl.BlockSpec((terms, 1, lanes, seg), lambda s: (0, s, 0, 0)), table, table],
        out_specs=table,
        out_shape=jax.ShapeDtypeStruct((segs * seg, lanes), jnp.bfloat16),
        compiler_params=pltpu.CompilerParams(vmem_limit_bytes=KERNEL_VMEM),
        cost_estimate=SMALL_COST,
    )(blocks, cosine, sine)


def gathered_core(x_pieces):
    rows = jnp.stack(natural_pieces(x_pieces, "x"))
    rows = jnp.stack(natural_pieces(relative_pieces(rows, "c"), "c"), axis=1)
    return rows.reshape(-1, rows.shape[-1])


def own_first(value, axis):
    size = value.shape[0]
    place = lax.axis_index(axis)
    return [
        lax.dynamic_index_in_dim(value, lax.rem(place - k + size, size), 0, keepdims=False)
        for k in range(size)
    ]


def core_sum(part, rows):
    blocks = part.reshape(lax.axis_size("x"), lax.axis_size("c"), rows, -1)
    return summed_pieces(own_first(blocks.transpose(1, 0, 2, 3), "c"), "c").astype(jnp.bfloat16)


def x_blocks(value):
    return own_first(value, "x")


def tensor_sum(part, rows):
    return summed_pieces(x_blocks(core_sum(part, rows)), "x")


def local(
    tokens,
    norm_gain,
    q_weight,
    key_matrix,
    value_matrix,
    o_weight,
    mlp_gain,
    gate_weight,
    up_weight,
    down_weight,
    parents,
    out_grad,
):
    z_size, y_size, x_size = (lax.axis_size(name) for name in ("z", "y", "x"))
    tensor_size = x_size * lax.axis_size("c")
    low = jnp.bfloat16
    local_rows, width = tokens.shape
    group_rows = local_rows * tensor_size
    kv_cols = key_matrix.shape[1]
    kv_local = kv_cols // HEAD_SIZE
    q_cols = q_weight.shape[1]
    own_width = norm_gain.shape[0]

    own_tokens = relative_columns(tokens)
    own_grad = relative_columns(out_grad).astype(jnp.float32)
    both_gains = jnp.concatenate([norm_gain, mlp_gain])
    both_gains = jnp.pad(both_gains, (0, -both_gains.shape[0] % (2 * kv_cols)))
    key_heads, value_heads = halves(key_matrix, kv_local), halves(value_matrix, kv_local)
    kv_shard = jnp.concatenate(
        [
            jnp.concatenate([v for kv in zip(key_heads, value_heads) for v in kv], axis=1),
            both_gains.reshape(-1, 2 * kv_cols),
        ],
        axis=0,
    )
    kv_copies = jnp.broadcast_to(kv_shard[None], (z_size, *kv_shard.shape))
    kv_copies, q_weight = together(kv_copies, q_weight)
    kv_z = exchanged(kv_copies, "z")
    q_z = lax.all_gather(q_weight, "z", axis=0, tiled=True)
    group_tokens = gathered_core(relative_pieces(own_tokens, "x"))
    kv_z, o_weight = together(kv_z, o_weight)
    o_z = lax.all_gather(o_weight, "z", axis=0)

    depth = segment_depth(parents)
    seg_count = group_rows // SEG
    z_place, y_place = lax.axis_index("z"), lax.axis_index("y")
    sources = [lax.rem(y_place - k + y_size, y_size) for k in range(y_size)]
    segs = jnp.concatenate(
        [
            (z_place * y_size + source) * seg_count + jnp.arange(seg_count, dtype=jnp.int32)
            for source in sources
        ]
    )
    seg_ids = jnp.arange(depth.shape[0], dtype=jnp.int32)
    seg_depth = jnp.sum(jnp.where(segs[:, None] == seg_ids[None, :], depth[None, :], 0), axis=1)
    position = (seg_depth[:, None] * SEG + jnp.arange(SEG, dtype=jnp.int32)[None, :]).reshape(-1)
    cosine_table, sine_table = rope_tables(position, HEAD_SIZE)
    cosine_lanes = jnp.tile(cosine_table, (1, 4))
    sine_lanes = jnp.tile(sine_table, (1, 4))
    ordered = [jnp.concatenate(in_order(jnp.split(v, y_size))) for v in (cosine_lanes, sine_lanes)]
    cosine_lanes, sine_lanes, *ordered = settled(cosine_lanes, sine_lanes, *ordered)

    kv_zy = relative_pieces(kv_z, "y")
    kv_zy, cosine_lanes, sine_lanes, ordered = together(kv_zy, cosine_lanes, sine_lanes, ordered)
    kv_weights = [v[:, :own_width].reshape(-1, 2 * kv_cols) for v in kv_zy]
    gains = [
        v[:, own_width:].reshape(z_size, -1)[:, : 2 * own_width].reshape(z_size, 2, own_width)
        for v in kv_zy
    ]
    gains = jnp.stack(gains).astype(jnp.float32)
    gain_one, gain_two = gains[:, :, 0].reshape(-1), gains[:, :, 1].reshape(-1)
    inputs = own_tokens.astype(jnp.float32)
    normed_one, inv_one = row_norm(inputs)
    group_normed, _ = row_norm(group_tokens.astype(jnp.float32))
    rows_one = (group_normed * gain_one).astype(low)
    rows_one, q_z = together(rows_one, q_z)
    q_weights = relative_pieces(q_z, "y")
    kv_rows = project(rows_one, kv_weights, cosine_lanes, sine_lanes, keys=True)
    kv_swapped = jnp.stack(natural_pieces(sent_groups(kv_rows), "y"))
    all_kv = gathered(kv_swapped, "z").reshape(-1, SEG, LANES)
    wide_blocks = split_columns(after((gate_weight, up_weight), kv_z), z_size)
    q_weights, wide_blocks = together(q_weights, wide_blocks)
    query_rows = project(rows_one, q_weights, cosine_lanes, sine_lanes)
    queries = sent_groups(query_rows)
    all_kv, queries, o_z, wide_blocks = together(all_kv, queries, o_z, wide_blocks)

    wide_z = exchanged(wide_blocks, "z")
    o_weights = relative_pieces(o_z, "y")
    seg_lists = jnp.split(segs, y_size)
    attends, lows = [None] * y_size, [None] * y_size
    for k in range(y_size - 1, 0, -1):
        *attends[k], lows[k] = attend(parents, seg_lists[k], queries[k], all_kv)
    queries[0], attends[1:], lows[1:] = together(queries[0], attends[1:], lows[1:])
    returned = [rotated(v, "y", -k) for k, v in enumerate(lows[1:], 1)]
    *attends[0], lows[0] = attend(parents, seg_lists[0], queries[0], all_kv)
    attn_pieces = [lows[0], *returned]
    attn_pieces, o_weights = together(attn_pieces, o_weights)
    attn_part = o_forward(attn_pieces, o_weights, y_place)
    attn_low = in_groups(attn_pieces)
    attn_core = core_sum(attn_part, local_rows)
    attn_core, wide_z = together(attn_core, wide_z)

    gate_z, up_z = (wide_z[:, i].reshape(z_size * own_width, -1) for i in range(2))
    gate_zy, up_zy = relative_pieces(gate_z, "y"), relative_pieces(up_z, "y")
    gate_zx = relative_pieces(gate_z, "x")
    attn_mine = summed_pieces(x_blocks(attn_core), "x")
    attn_mine, up_z, down_weight = together(attn_mine, up_z, down_weight)

    middle = inputs + branch_scale * attn_mine
    normed_two, inv_two = row_norm(middle)
    hidden_two = (normed_two * gain_two).astype(low)
    rows_two = lax.all_gather(hidden_two, ("z", "c"), axis=0, tiled=True)
    down_z = exchanged(down_weight.reshape(z_size, -1, own_width), "z")
    gate_zx, gate_zy, up_z = together(gate_zx, gate_zy, up_z)
    gate_far = [relative_pieces(v, "y")[1:] for v in gate_zx[1:]]
    up_zx = relative_pieces(up_z, "x")
    grad_mlp = (branch_scale * own_grad).astype(low)
    up_zx, up_zy, grad_mlp, down_z = together(up_zx, up_zy, grad_mlp, down_z)
    grad_mlp_rows = lax.all_gather(grad_mlp, ("z", "c"), axis=0, tiled=True)
    up_far = [relative_pieces(v, "x")[1:] for v in up_zy[1:]]
    rows_two, gate_far, up_far, down_z = together(rows_two, gate_far, up_far, down_z)
    down_zy, down_zx = relative_pieces(down_z, "y"), relative_pieces(down_z, "x")
    gates = [gate_zx] + [[gate_zy[k], *[v[k - 1] for v in gate_far]] for k in range(1, y_size)]
    ups = [up_zx] + [[up_zy[k], *up_far[k - 1]] for k in range(1, y_size)]
    activated, gate_slope, up_slope = gate_forward(rows_two, gates, ups)
    down_zy, down_zx, activated, gate_slope, up_slope = together(
        down_zy, down_zx, activated, gate_slope, up_slope
    )
    down_crossed = together(*crossed(down_zx, down_zy))
    downs = quarters(down_zx, down_zy, *down_crossed)
    mlp_part = down_forward(activated, downs)
    mlp_part, grad_mlp_rows = together(mlp_part, grad_mlp_rows)

    mlp_mine = lax.psum_scatter(mlp_part, ("z", "c"), scatter_dimension=0, tiled=True)
    grad_parts, rows_parts = halves(grad_mlp_rows, y_size), halves(rows_two, y_size)
    acts = halves(activated, x_size)
    down_far = [summed_pieces([turned_matmul(a, b) for a in grad_parts], "y").astype(low) for b in acts[1:]]
    grad_gate_act, grad_up_act = gate_backward(grad_mlp_rows, downs, gate_slope, up_slope)
    grad_gate_act, grad_up_act = together(grad_gate_act, grad_up_act)

    gate_parts, up_parts = halves(grad_gate_act, x_size), halves(grad_up_act, x_size)
    gate_dots = [[turned_matmul(a, b) for a in rows_parts] for b in gate_parts[1:]]
    up_dots = [[turned_matmul(a, b) for b in up_parts] for a in rows_parts[1:]]
    for dots in gate_dots + up_dots:
        dots[1:] = [v.astype(low) for v in dots[1:]]
    grad_gate_act, gate_dots, up_dots = together(grad_gate_act, gate_dots, up_dots)
    gate_far = [summed_pieces(v, "y").astype(low) for v in gate_dots]
    up_far = [summed_pieces(v, "x").astype(low) for v in up_dots]
    input_part = turned_product([grad_gate_act, grad_up_act], [gates, ups])
    input_part, down_far = together(input_part, down_far)

    grad_rows_two = lax.psum_scatter(input_part, ("z", "c"), scatter_dimension=0, tiled=True)
    gate_far, up_far, acts = together(gate_far, up_far, acts)
    down_near = summed_pieces([turned_matmul(a, acts[0]) for a in grad_parts], "y")
    down_far = [rotated(v, "x", -1 - i) for i, v in enumerate(down_far)]
    down_near, down_far, mlp_mine = together(down_near, down_far, mlp_mine)
    grad_down_z = sum([v.astype(jnp.float32) for v in down_far], down_near).astype(low)
    gate_near = summed_pieces([turned_matmul(a, gate_parts[0]) for a in rows_parts], "y")
    gate_far = [rotated(v, "x", -1 - i) for i, v in enumerate(gate_far)]
    up_near = [turned_matmul(rows_parts[0], b) for b in up_parts]
    up_near[1:] = [v.astype(low) for v in up_near[1:]]
    grad_rows_two, mlp_mine, up_far, up_near, grad_down_z = together(
        grad_rows_two, mlp_mine, up_far, up_near, grad_down_z
    )
    grad_rows_two = grad_rows_two.astype(jnp.float32)
    gain_two_part = jnp.sum(grad_rows_two * normed_two, axis=0)
    grad_middle = own_grad + norm_back(grad_rows_two, normed_two, inv_two, gain_two)
    grad_attn = (branch_scale * grad_middle).astype(low)
    attn_x = relative_pieces(grad_attn, "x")
    up_far = [rotated(v, "y", -1 - i) for i, v in enumerate(up_far)]
    grad_gate_z = sum([v.astype(jnp.float32) for v in gate_far], gate_near).astype(low)
    wide_z = jnp.stack([v.reshape(z_size, own_width, -1) for v in (grad_gate_z, grad_down_z)], 1)
    attn_x, wide_z, up_near = together(attn_x, wide_z, up_near)
    grad_attn_rows = gathered_core(attn_x)
    grad_heads = o_backward(grad_attn_rows, o_weights)
    grad_heads, grad_attn_rows, up_near, wide_z = together(
        grad_heads, grad_attn_rows, up_near, wide_z
    )
    wide_z = exchanged(wide_z, "z")

    grad_heads = sent_groups(grad_heads)
    o_dots = [turned_matmul(v, attn_low) for v in halves(grad_attn_rows, y_size)[1:]]
    o_dots = [v.astype(low) for v in o_dots]
    grad_heads, o_dots, up_near, grad_attn_rows = together(
        grad_heads, o_dots, up_near, grad_attn_rows
    )
    o_sent = [rotated(v, "y", -1 - i) for i, v in enumerate(o_dots)]
    up_mine = [rotated(v, "x", -1 - i) for i, v in enumerate(up_near[1:])]
    grad_queries, sums = [None] * y_size, None
    for k in range(y_size - 1, 0, -1):
        grad_queries[k], sums = attend_back(
            parents, seg_lists[k], queries[k], grad_heads[k], *attends[k], cosine_lanes,
            sine_lanes, k, all_kv, sums,
        )
    grad_o_y = turned_matmul(halves(grad_attn_rows, y_size)[0], attn_low)
    grad_o_y = sum([v.astype(jnp.float32) for v in o_sent], grad_o_y).astype(low)
    grad_queries[1:], sums, grad_o_y = together(grad_queries[1:], sums, grad_o_y)
    grad_o = lax.psum_scatter(grad_o_y, "z", scatter_dimension=0, tiled=True)
    returned = [rotated(v, "y", -k) for k, v in enumerate(grad_queries[1:], 1)]
    grad_queries[0], grad_kv = attend_back(
        parents, seg_lists[0], queries[0], grad_heads[0], *attends[0], cosine_lanes, sine_lanes,
        0, all_kv, sums,
    )
    grad_kv, wide_z = together(grad_kv, wide_z)
    grad_queries[0], returned, up_far, up_mine, up_near = after(
        (grad_queries[0], returned, up_far, up_mine, up_near), grad_kv
    )

    def owned_dots(left, right):
        dots = [turned_matmul(v, right) for v in halves(left, y_size)]
        return dots[:1] + [v.astype(low) for v in dots[1:]]

    def sent_back(dots):
        return [rotated(v, "y", -1 - i) for i, v in enumerate(dots[1:])]

    def total(own, sent):
        return sum([v.astype(jnp.float32) for v in sent], own).astype(low)

    kv_mine = exchanged(grad_kv.reshape(z_size, y_size * seg_count, LANES, SEG), "z")
    grad_queries = in_groups([grad_queries[0], *returned])
    query_dots = owned_dots(rows_one, grad_queries)
    query_sent = sent_back(query_dots)
    q_full = jnp.concatenate(q_weights, axis=0)
    query_part = matmul_turned(grad_queries, q_full)
    grad_up_z = total(up_near[0], up_far + up_mine)
    kv_mine, query_part, query_dots, query_sent, grad_up_z, grad_o = together(
        kv_mine, query_part, query_dots, query_sent, grad_up_z, grad_o
    )

    grad_up = exchanged(grad_up_z.reshape(z_size, own_width, -1), "z")
    kv_mine = turned_sum(kv_mine, *ordered).reshape(y_size, group_rows, LANES)
    kv_mine = own_first(kv_mine, "y")
    grad_kv_rows = in_groups(
        [kv_mine[0]] + [rotated(v, "y", -k) for k, v in enumerate(kv_mine[1:], 1)]
    )
    kv_full = jnp.concatenate(kv_weights, axis=0)
    input_one = (query_part + matmul_turned(grad_kv_rows, kv_full)).astype(low)
    input_core = core_sum(input_one, local_rows)
    grad_q_y = total(query_dots[0], query_sent)
    kv_dots = owned_dots(rows_one, grad_kv_rows)
    kv_sent = sent_back(kv_dots)
    input_core, grad_q_y, grad_up, wide_z, grad_o = together(
        input_core, grad_q_y, grad_up, wide_z, grad_o
    )
    grad_q = lax.psum_scatter(grad_q_y, "z", scatter_dimension=0, tiled=True)
    input_x = x_blocks(input_core)
    input_sent = [rotated(v, "x", -1 - i) for i, v in enumerate(input_x[1:])]
    grad_gate, grad_down, grad_up = finished(wide_z, grad_up)
    input_x[0], input_sent, kv_sent, kv_dots, grad_gate, grad_down, grad_up, grad_o = together(
        input_x[0], input_sent, kv_sent, kv_dots, grad_gate, grad_down, grad_up, grad_o
    )
    grad_rows_one = sum([v.astype(jnp.float32) for v in input_sent], input_x[0].astype(jnp.float32))
    kv_blocks = own_first(total(kv_dots[0], kv_sent).reshape(z_size, own_width, -1), "z")
    kv_sent = [rotated(v, "z", -1 - i) for i, v in enumerate(kv_blocks[1:])]
    gain_one_part = jnp.sum(grad_rows_one * normed_one, axis=0)
    grad_inputs = grad_middle + norm_back(grad_rows_one, normed_one, inv_one, gain_one)
    gain_parts = jnp.stack([gain_one_part, gain_two_part], axis=0)
    gain_parts = natural_columns(gain_parts).reshape(2, z_size * y_size, 1, own_width)
    gain_parts = jnp.broadcast_to(
        gain_parts, (2, z_size * y_size, tensor_size, own_width)
    ).reshape(2, -1, own_width).transpose(1, 0, 2)
    gain_parts = exchanged(gain_parts, ("z", "y", "x", "c"))
    mlp_mine = after(mlp_mine, grad_inputs)
    mixed = natural_columns((middle + branch_scale * mlp_mine.astype(jnp.float32)).astype(low))
    grad_tokens = natural_columns(grad_inputs.astype(low))
    grad_o = after(grad_o, grad_inputs).astype(jnp.float32).T
    gain_parts, kv_sent, kv_blocks, grad_q, grad_o, grad_tokens, mixed = together(
        gain_parts, kv_sent, kv_blocks, grad_q.astype(jnp.float32), grad_o, grad_tokens, mixed
    )
    gain_sums = jnp.sum(gain_parts, axis=0)
    grad_kv_weight = sum([v.astype(jnp.float32) for v in kv_sent], kv_blocks[0].astype(jnp.float32))
    grad_heads = halves(grad_kv_weight, 2 * kv_local)
    return (
        mixed,
        grad_tokens,
        gain_sums[0],
        grad_q,
        jnp.concatenate(grad_heads[::2], axis=1),
        jnp.concatenate(grad_heads[1::2], axis=1),
        grad_o,
        gain_sums[1],
        grad_gate,
        grad_up,
        grad_down,
    )


def solution(mesh):
    dp_size, tensor_size = mesh.shape["dp"], mesh.shape["tensor"]
    fine = jax.sharding.Mesh(
        mesh.devices.reshape(dp_size // 2, 2, tensor_size // 2, 2), ("z", "y", "x", "c")
    )
    dp, tensor = ("z", "y"), ("x", "c")
    tokens = P(dp + tensor, None)
    rows = P(dp, tensor)
    columns = P(tensor, dp)
    in_specs = (
        tokens,
        P(dp),
        rows,
        rows,
        rows,
        columns,
        P(dp),
        rows,
        rows,
        columns,
        P(),
        tokens,
    )
    out_specs = (
        tokens,
        tokens,
        P(dp),
        rows,
        rows,
        rows,
        columns,
        P(dp),
        rows,
        rows,
        columns,
    )
    return jax.shard_map(local, mesh=fine, in_specs=in_specs, out_specs=out_specs, check_vma=False)
```

```python
import functools

import jax
import jax.numpy as jnp
from jax import lax
from jax.experimental import pallas as pl
from jax.experimental.pallas import tpu as pltpu
from jax.sharding import PartitionSpec as P

HEAD_SIZE = 64
SEG = 256
MAX_STEPS = 9
LANES = 2 * HEAD_SIZE
KERNEL_VMEM = 32 * 2**20
SMALL_COST = pl.CostEstimate(flops=2**28, bytes_accessed=2**18, transcendentals=0)


attn_scale = 0.015625
branch_scale = 0.22
norm_eps = 1e-05
rope_base = 10000000.0
masked_score = -1e30


def segment_depth(parents):
    seg_total = parents.shape[0]
    seg_ids = jnp.arange(seg_total, dtype=jnp.int32)
    reach = (parents[:, None] == seg_ids[None, :]) | (seg_ids[:, None] == seg_ids[None, :])
    reach = reach.astype(jnp.float32)
    for doubling in range(4):
        reach = jnp.minimum(jnp.dot(reach, reach, preferred_element_type=jnp.float32), 1.0)
    return jnp.sum(reach, axis=1).astype(jnp.int32) - 1


def rope_tables(position, head_dim):
    half_dim = head_dim // 2
    exponent = jnp.arange(half_dim, dtype=jnp.float32) * (2.0 / head_dim)
    inverse = jnp.power(rope_base, -exponent)
    angles = position.astype(jnp.float32)[:, None] * inverse[None, :]
    return (jnp.cos(angles), jnp.sin(angles))


def rotated(value, axis, step):
    size = lax.axis_size(axis)
    return lax.ppermute(value, axis, [(i, (i + step) % size) for i in range(size)])


def relative_pieces(value, axis):
    return [value] + [rotated(value, axis, k) for k in range(1, lax.axis_size(axis))]


def natural_pieces(pieces, axis):
    size = len(pieces)
    place = lax.axis_index(axis)
    return [
        lax.select_n(place, *[pieces[(i - j) % size] for i in range(size)]) for j in range(size)
    ]


def gathered(value, axis):
    size = lax.axis_size(axis)
    copies = jnp.broadcast_to(value[None], (size, *value.shape))
    return lax.all_to_all(copies, axis, 0, 0, tiled=True)


def exchanged(blocks, axis):
    return lax.all_to_all(blocks, axis, 0, 0, tiled=True)


def summed_pieces(pieces, axis):
    sent = [rotated(pieces[k].astype(jnp.bfloat16), axis, -k) for k in range(1, len(pieces))]
    total = pieces[0].astype(jnp.float32)
    for value in sent:
        total = total + value.astype(jnp.float32)
    return total


def summed_blocks(blocks, axis):
    return jnp.sum(exchanged(blocks.astype(jnp.bfloat16), axis).astype(jnp.float32), axis=0)


def column_blocks(value, count):
    return value.reshape(value.shape[0], count, -1).transpose(1, 0, 2)


def joined_columns(blocks):
    return blocks.transpose(1, 0, 2).reshape(blocks.shape[1], -1)


def relative_columns(value):
    size = lax.axis_size("y")
    place = lax.axis_index("y")
    rows = value.shape[0]
    split = value.reshape(rows, lax.axis_size("z"), size, -1)
    flat = [split[:, :, i].reshape(rows, -1) for i in range(size)]
    return jnp.concatenate(
        [
            lax.select_n(place, *[flat[(i - k) % size] for i in range(size)])
            for k in range(size)
        ],
        axis=1,
    )


def natural_columns(value):
    size = lax.axis_size("y")
    rows = value.shape[0]
    split = value.reshape(rows, size, lax.axis_size("z"), -1)
    parts = natural_pieces([split[:, k] for k in range(size)], "y")
    return jnp.stack(parts, axis=2).reshape(rows, -1)


def together(*values):
    return lax.optimization_barrier(values)


def after(value, *others):
    return lax.optimization_barrier((value, *others))[0]


def ancestor_count(parents, seg):
    def climb(step, state):
        current, count = state
        above = parents[current]
        return above, count + jnp.where(above != current, 1, 0)

    return lax.fori_loop(0, MAX_STEPS, climb, (seg, jnp.int32(1)))[1]


def left_lanes(shape):
    return lax.broadcasted_iota(jnp.int32, shape, 1) < HEAD_SIZE


def stacked_heads(pairs, to_left):
    left = left_lanes(pairs[0].shape)
    stack = []
    for pair in pairs:
        swapped = pltpu.roll(pair, HEAD_SIZE, 1)
        for head in (pair, swapped) if to_left else (swapped, pair):
            stack.append(jnp.where(left, head, 0.0) if to_left else jnp.where(left, 0.0, head))
    return jnp.concatenate(stack, axis=0)


def unstacked_heads(stack, from_left):
    left = left_lanes((SEG, 2 * HEAD_SIZE))
    pairs = []
    for first in range(0, stack.shape[0], 2 * SEG):
        even, odd = stack[first : first + SEG], stack[first + SEG : first + 2 * SEG]
        if from_left:
            odd = pltpu.roll(odd, HEAD_SIZE, 1)
        else:
            even = pltpu.roll(even, HEAD_SIZE, 1)
        pairs.append(jnp.where(left, even, odd))
    return pairs


def turned(value, cosine, sine, direction):
    half = HEAD_SIZE // 2
    lane = lax.broadcasted_iota(jnp.int32, value.shape, 1)
    first = lax.rem(lane, HEAD_SIZE) < half
    ahead = pltpu.roll(value, LANES - half, 1)
    behind = pltpu.roll(value, half, 1)
    signed = sine * direction
    return value * cosine + jnp.where(first, -ahead * signed, behind * signed)


def nt_dot(left, right):
    return lax.dot_general(
        left, right, (((1,), (1,)), ((), ())), preferred_element_type=jnp.float32
    )


def nn_dot(left, right):
    return lax.dot_general(
        left, right, (((1,), (0,)), ((), ())), preferred_element_type=jnp.float32
    )


def causal_tile(rows):
    query = lax.rem(lax.broadcasted_iota(jnp.int32, (rows, SEG), 0), SEG)
    return lax.broadcasted_iota(jnp.int32, (rows, SEG), 1) <= query


def lane_blocks(ref):
    return [ref[:, at : at + LANES] for at in range(0, ref.shape[1], LANES)]


def key_tables(cosine, sine):
    left = left_lanes(cosine.shape)
    return jnp.where(left, cosine, 1.0), jnp.where(left, sine, 0.0)


def settle_kernel(*refs):
    count = len(refs) // 2
    for value, out in zip(refs[:count], refs[count:]):
        out[...] = value[...]


def settled(*values):
    return pl.pallas_call(
        settle_kernel,
        out_shape=[jax.ShapeDtypeStruct(v.shape, v.dtype) for v in values],
        compiler_params=pltpu.CompilerParams(vmem_limit_bytes=KERNEL_VMEM),
        cost_estimate=SMALL_COST,
    )(*values)


def project_kernel(parts, keys, rows, *refs):
    weights, (cosine, sine, out) = refs[:parts], refs[parts:]
    depth = weights[0].shape[0]
    product = sum(nn_dot(rows[:, i * depth : (i + 1) * depth], w[...]) for i, w in enumerate(weights))
    cos, sin = cosine[...], sine[...]
    if keys:
        cos, sin = key_tables(cos, sin)
    for at in range(0, product.shape[1], LANES):
        block = turned(product[:, at : at + LANES], cos, sin, 1.0)
        out[:, at : at + LANES] = block.astype(jnp.bfloat16)


def project(rows, weights, cosine, sine, keys=False):
    count, width = rows.shape
    depth, cols = weights[0].shape
    step = 2 * LANES
    table = pl.BlockSpec((count, LANES), lambda j: (0, 0))
    return pl.pallas_call(
        functools.partial(project_kernel, len(weights), keys),
        grid=(cols // step,),
        in_specs=[pl.BlockSpec((count, width), lambda j: (0, 0))]
        + [pl.BlockSpec((depth, step), lambda j: (0, j))] * len(weights)
        + [table, table],
        out_specs=pl.BlockSpec((count, step), lambda j: (0, j)),
        out_shape=jax.ShapeDtypeStruct((count, cols), jnp.bfloat16),
        compiler_params=pltpu.CompilerParams(vmem_limit_bytes=KERNEL_VMEM),
        cost_estimate=SMALL_COST,
    )(rows, *weights, cosine, sine)


def attend_kernel(parents, segs, queries, keys_values, out, stats, out_low, scores):
    seg = segs[pl.program_id(0)]
    count = ancestor_count(parents, seg)
    pairs = [block.astype(jnp.float32) * attn_scale for block in lane_blocks(queries)]
    stack = stacked_heads(pairs, True).astype(jnp.bfloat16)
    rows = stack.shape[0]

    first = jnp.where(causal_tile(rows), nt_dot(stack, keys_values[seg]), masked_score)
    scores[0] = first

    def folded(tile):
        return jnp.maximum(tile[:, :LANES], tile[:, LANES:])

    def measure(step, state):
        current, top = state
        current = parents[current]
        tile = nt_dot(stack, keys_values[current])
        scores[step] = tile
        return current, jnp.maximum(top, folded(tile))

    top = lax.fori_loop(1, count, measure, (seg, folded(first)))[1]
    row_max = jnp.max(top, axis=1, keepdims=True)
    left = left_lanes((SEG, LANES))

    def gather(step, state):
        current, mixed = state
        terms = jnp.exp(scores[step] - row_max).astype(jnp.bfloat16)
        tile = jnp.where(left, jnp.ones((SEG, LANES), jnp.bfloat16), keys_values[current])
        return parents[current], mixed + nn_dot(terms, tile)

    start = (seg, jnp.zeros((rows, LANES), jnp.float32))
    mixed = lax.fori_loop(0, count, gather, start)[1]
    total = mixed[:, :1]
    mixed = mixed / total
    stats[0] = row_max + jnp.log(total)
    for place, pair in enumerate(unstacked_heads(mixed, False)):
        out[:, place * LANES : (place + 1) * LANES] = pair
        out_low[:, place * LANES : (place + 1) * LANES] = pair.astype(jnp.bfloat16)


def attend_back_kernel(
    parents, segs, queries, grads, attended, stats, cosine, sine, keys_values, *refs
):
    earlier, (grad_queries, grad_kv, kv_sum) = refs[:-3], refs[-3:]
    seg = segs[pl.program_id(0)]
    count = ancestor_count(parents, seg)

    @pl.when(pl.program_id(0) == 0)
    def _():
        kv_sum[...] = earlier[0][...] if earlier else jnp.zeros_like(kv_sum)

    query_pairs = [block.astype(jnp.float32) * attn_scale for block in lane_blocks(queries)]
    grad_pairs = [block.astype(jnp.float32) for block in lane_blocks(grads)]
    left = left_lanes((SEG, LANES))
    deltas = []
    for pair, out in zip(grad_pairs, lane_blocks(attended)):
        product = pair * out
        deltas.append(jnp.sum(jnp.where(left, product, 0.0), axis=1, keepdims=True))
        deltas.append(jnp.sum(jnp.where(left, 0.0, product), axis=1, keepdims=True))
    delta = jnp.concatenate(deltas, axis=0)
    query_wide = stacked_heads(query_pairs, True)
    grad_wide = stacked_heads(grad_pairs, False)
    query_stack, grad_stack = query_wide.astype(jnp.bfloat16), grad_wide.astype(jnp.bfloat16)
    query_turned = query_wide.T.astype(jnp.bfloat16)
    grad_turned = grad_wide.T.astype(jnp.bfloat16)
    log_total = stats[0]
    rows = query_stack.shape[0]

    def visit(current, total, diagonal):
        tile_kv = keys_values[current]
        tile = nt_dot(query_stack, tile_kv)
        if diagonal:
            tile = jnp.where(causal_tile(rows), tile, masked_score)
        probs = jnp.exp(tile - log_total)
        grad_probs = nt_dot(grad_stack, tile_kv)
        grad_tile = (probs * (grad_probs - delta)).astype(jnp.bfloat16)
        kv_sum[current] += nn_dot(query_turned, grad_tile) + nn_dot(
            grad_turned, probs.astype(jnp.bfloat16)
        )
        return total + nn_dot(grad_tile, tile_kv)

    total = visit(seg, jnp.zeros((rows, LANES), jnp.float32), True)

    def climb(step, state):
        current, total = state
        current = parents[current]
        return current, visit(current, total, False)

    total = lax.fori_loop(1, count, climb, (seg, total))[1]
    cos, sin = cosine[...], sine[...]
    for place, pair in enumerate(unstacked_heads(total * attn_scale, True)):
        grad_queries[:, place * LANES : (place + 1) * LANES] = turned(
            pair, cos, sin, -1.0
        ).astype(jnp.bfloat16)

    @pl.when(pl.program_id(0) == pl.num_programs(0) - 1)
    def _():
        grad_kv[...] = kv_sum[...].astype(grad_kv.dtype)


def attention_specs(cols, seg_total):
    block = pl.BlockSpec((SEG, cols), lambda s: (s, 0))
    table = pl.BlockSpec((SEG, LANES), lambda s: (s, 0))
    whole = pl.BlockSpec((seg_total, SEG, LANES), lambda s: (0, 0, 0))
    rows = SEG * (cols // HEAD_SIZE)
    stat = pl.BlockSpec((1, rows, 1), lambda s: (s, 0, 0))
    return block, table, whole, rows, stat, pl.BlockSpec(memory_space=pltpu.SMEM)


def attend(parents, segs, queries, keys_values):
    count, cols = queries.shape
    block, table, whole, rows, stat, scalar = attention_specs(cols, keys_values.shape[0])
    steps = count // SEG
    return pl.pallas_call(
        attend_kernel,
        grid=(steps,),
        in_specs=[scalar, scalar, block, whole],
        out_specs=[block, stat, block],
        out_shape=[
            jax.ShapeDtypeStruct((count, cols), jnp.float32),
            jax.ShapeDtypeStruct((steps, rows, 1), jnp.float32),
            jax.ShapeDtypeStruct((count, cols), jnp.bfloat16),
        ],
        scratch_shapes=[pltpu.VMEM((MAX_STEPS + 1, rows, SEG), jnp.float32)],
        compiler_params=pltpu.CompilerParams(vmem_limit_bytes=KERNEL_VMEM),
        cost_estimate=SMALL_COST,
    )(parents, segs, queries, keys_values)


def attend_back(
    parents, segs, queries, grads, attended, stats, cosine, sine, place, keys_values, earlier=None
):
    count, cols = queries.shape
    first = place * (count // SEG)
    seg_total = keys_values.shape[0]
    block, table, whole, rows, stat, scalar = attention_specs(cols, seg_total)
    sums = pl.BlockSpec((seg_total, LANES, SEG), lambda s: (0, 0, 0))
    last = earlier is not None
    sum_type = jnp.bfloat16 if last else jnp.float32
    return pl.pallas_call(
        attend_back_kernel,
        grid=(count // SEG,),
        in_specs=[scalar, scalar, block, block, block, stat]
        + [pl.BlockSpec((SEG, LANES), lambda s: (first + s, 0))] * 2
        + [whole]
        + [sums] * last,
        out_specs=[block, sums],
        out_shape=[
            jax.ShapeDtypeStruct((count, cols), jnp.bfloat16),
            jax.ShapeDtypeStruct((seg_total, LANES, SEG), sum_type),
        ],
        scratch_shapes=[pltpu.VMEM((seg_total, LANES, SEG), jnp.float32)],
        compiler_params=pltpu.CompilerParams(vmem_limit_bytes=56 * 2**20),
        cost_estimate=SMALL_COST,
    )(
        parents, segs, queries, grads, attended, stats, cosine, sine, keys_values,
        *([earlier] if last else []),
    )


def in_turn(per, count, step):
    for i in range(count):
        pl.when(pl.program_id(1) // per == i)(functools.partial(step, i))


def gate_kernel(per, parts, pieces, rows, *refs):
    gates, ups = refs[: parts * pieces], refs[parts * pieces : 2 * parts * pieces]
    activated, gate_slope, up_slope = refs[2 * parts * pieces :]
    depth = gates[0].shape[0]

    def product(weights, i):
        return sum(
            nn_dot(rows[:, k * depth : (k + 1) * depth], weights[k * pieces + i][...])
            for k in range(parts)
        )

    def step(i):
        gate, up = product(gates, i), product(ups, i)
        sigmoid = 1.0 / (1.0 + jnp.exp(-gate))
        silu = gate * sigmoid
        activated[...] = (silu * up).astype(jnp.bfloat16)
        gate_slope[...] = up * sigmoid * (1.0 + gate * (1.0 - sigmoid))
        up_slope[...] = silu

    in_turn(per, pieces, step)


def gate_back_kernel(per, parts, pieces, grads, *refs):
    weights, (gate_slope, up_slope, grad_gate, grad_up) = refs[:-4], refs[-4:]
    blocks, _, depth = weights[0].shape

    def step(i):
        grad = 0.0
        for k in range(parts):
            for z in range(blocks):
                at = (k * blocks + z) * depth
                grad = grad + nt_dot(grads[:, at : at + depth], weights[k * pieces + i][z])
        grad_gate[...] = (grad * gate_slope[...]).astype(jnp.bfloat16)
        grad_up[...] = (grad * up_slope[...]).astype(jnp.bfloat16)

    in_turn(per, pieces, step)


def down_kernel(per, parts, pieces, acts, *refs):
    weights, out = refs[:-1], refs[-1]
    depth = weights[0].shape[1]

    def step(k):
        total = sum(
            nn_dot(acts[:, i * depth : (i + 1) * depth], weights[k * pieces + i][0])
            for i in range(pieces)
        )
        out[...] = total.astype(jnp.bfloat16)

    in_turn(per, parts, step)


def turned_kernel(terms, per, parts, pieces, *refs):
    lefts, weights, out = refs[:terms], refs[terms:-1], refs[-1]
    depth = weights[0].shape[1]

    def step(k):
        total = 0.0
        for term, left in enumerate(lefts):
            for i in range(pieces):
                weight = weights[(term * parts + k) * pieces + i]
                total = total + nt_dot(left[:, i * depth : (i + 1) * depth], weight[...])
        out[...] = total.astype(jnp.bfloat16)

    in_turn(per, parts, step)


def wide_call(kernel, whole, weights, tiled, axis, by_piece, outs):
    parts, pieces = len(weights[0]), len(weights[0][0])
    shape = weights[0][0][0].shape
    groups = pieces if by_piece else parts
    if len(shape) == 3 and axis == 0:
        width, block, per = shape[0] * shape[2], (1, *shape[1:]), shape[0]
    else:
        width = shape[axis]
        per = width // min(width, 256)
        block = tuple(n // per if at == axis else n for at, n in enumerate(shape))
    tile = (min(whole[0].shape[0], 1024), width // per)
    count, cols = whole[0].shape[0], groups * width

    def piece_spec(k, i):
        group = i if by_piece else k

        def place(row, col):
            at = jnp.clip(col - group * per, 0, per - 1)
            return tuple(at if dim == axis else 0 for dim in range(len(shape)))

        return pl.BlockSpec(block, place)

    tile_spec = pl.BlockSpec(tile, lambda row, col: (row, col))
    flat = [v for weight in weights for row in weight for v in row]
    return pl.pallas_call(
        functools.partial(kernel, per, parts, pieces),
        grid=(count // tile[0], groups * per),
        in_specs=[pl.BlockSpec((tile[0], v.shape[1]), lambda row, col: (row, 0)) for v in whole]
        + [piece_spec(k, i) for _ in weights for k in range(parts) for i in range(pieces)]
        + [tile_spec] * len(tiled),
        out_specs=[tile_spec] * len(outs),
        out_shape=[jax.ShapeDtypeStruct((count, cols), t) for t in outs],
        compiler_params=pltpu.CompilerParams(vmem_limit_bytes=KERNEL_VMEM),
        cost_estimate=SMALL_COST,
    )(*whole, *flat, *tiled)


def gate_forward(rows, gates, ups):
    outs = (jnp.bfloat16, jnp.float32, jnp.float32)
    return wide_call(gate_kernel, [rows], [gates, ups], [], 1, True, outs)


def gate_backward(grads, downs, gate_slope, up_slope):
    outs = (jnp.bfloat16, jnp.bfloat16)
    return wide_call(gate_back_kernel, [grads], [downs], [gate_slope, up_slope], 1, True, outs)


def down_forward(acts, downs):
    if downs[0][0].shape[2] % LANES:
        rows = [jnp.concatenate([joined_columns(v) for v in row], axis=0) for row in downs]
        return nn_dot(acts, jnp.concatenate(rows, axis=1)).astype(jnp.bfloat16)
    return wide_call(down_kernel, [acts], [downs], [], 0, False, (jnp.bfloat16,))[0]


def turned_product(lefts, weights):
    kernel = functools.partial(turned_kernel, len(lefts))
    return wide_call(kernel, lefts, weights, [], 0, False, (jnp.bfloat16,))[0]


def o_kernel(parts, place, *refs):
    rows, weights, out = refs[:-1 - parts], refs[-1 - parts : -1], refs[-1]
    blocks = weights[0].shape[0]
    depth = rows[0].shape[1]
    at = lax.rem(pl.program_id(0), blocks)
    for k in range(parts):

        @pl.when(pl.program_id(0) // blocks == k)
        def _(k=k):
            total = 0.0
            for i, piece in enumerate(rows):
                group = lax.rem(place[0] + i, len(rows))
                start = pl.multiple_of(group * depth, depth)
                total = total + nn_dot(piece[...], weights[k][at, pl.ds(start, depth), :])
            out[...] = total.astype(jnp.bfloat16)


def o_forward(pieces, weights, place):
    count, depth = pieces[0].shape
    blocks, _, step = weights[0].shape
    if step % LANES:
        full = jnp.concatenate([joined_columns(v) for v in weights], axis=1)
        return nn_dot(in_groups(pieces), full).astype(jnp.bfloat16)
    whole = pl.BlockSpec(weights[0].shape, lambda j: (0, 0, 0))
    return pl.pallas_call(
        functools.partial(o_kernel, len(weights)),
        grid=(len(weights) * blocks,),
        in_specs=[pl.BlockSpec(memory_space=pltpu.SMEM)]
        + [pl.BlockSpec((count, depth), lambda j: (0, 0))] * len(pieces)
        + [whole] * len(weights),
        out_specs=pl.BlockSpec((count, step), lambda j: (0, j)),
        out_shape=jax.ShapeDtypeStruct((count, len(weights) * blocks * step), jnp.bfloat16),
        compiler_params=pltpu.CompilerParams(vmem_limit_bytes=KERNEL_VMEM),
        cost_estimate=SMALL_COST,
    )(place.astype(jnp.int32).reshape(1), *pieces, *weights)


def o_back_kernel(parts, rows, *refs):
    weights, out = refs[:parts], refs[parts]
    blocks, _, step = weights[0].shape
    total = 0.0
    for k in range(parts):
        for z in range(blocks):
            at = (k * blocks + z) * step
            total = total + nt_dot(rows[:, at : at + step], weights[k][z])
    out[...] = total.astype(jnp.bfloat16)


def o_backward(rows, weights):
    return pl.pallas_call(
        functools.partial(o_back_kernel, len(weights)),
        out_shape=jax.ShapeDtypeStruct((rows.shape[0], weights[0].shape[1]), jnp.bfloat16),
        compiler_params=pltpu.CompilerParams(vmem_limit_bytes=KERNEL_VMEM),
        cost_estimate=SMALL_COST,
    )(rows, *weights)


def split_kernel(*refs):
    values, out = refs[:-1], refs[-1]
    for i, value in enumerate(values):
        out[0, i] = value[...]


def split_columns(values, count):
    rows, cols = values[0].shape
    step = cols // count
    if step % LANES:
        return jnp.stack([column_blocks(v, count) for v in values], axis=1)
    return pl.pallas_call(
        split_kernel,
        grid=(count,),
        in_specs=[pl.BlockSpec((rows, step), lambda j: (0, j))] * len(values),
        out_specs=pl.BlockSpec((1, len(values), rows, step), lambda j: (j, 0, 0, 0)),
        out_shape=jax.ShapeDtypeStruct((count, len(values), rows, step), values[0].dtype),
        compiler_params=pltpu.CompilerParams(vmem_limit_bytes=KERNEL_VMEM),
        cost_estimate=SMALL_COST,
    )(*values)


def finish_kernel(pair, single, first, second, third):
    first[...] = pair[0, 0].astype(jnp.float32)
    second[...] = pair[0, 1].astype(jnp.float32).T
    third[...] = single[0].astype(jnp.float32)


def finished(pair, single):
    count, _, rows, cols = pair.shape
    if cols % LANES or rows % LANES:
        first, second, third = (joined_columns(v) for v in (pair[:, 0], pair[:, 1], single))
        return [v.astype(jnp.float32) for v in (first, second.T, third)]
    side = pl.BlockSpec((rows, cols), lambda z: (0, z))
    return pl.pallas_call(
        finish_kernel,
        grid=(count,),
        in_specs=[
            pl.BlockSpec((1, 2, rows, cols), lambda z: (z, 0, 0, 0)),
            pl.BlockSpec((1, rows, cols), lambda z: (z, 0, 0)),
        ],
        out_specs=[side, pl.BlockSpec((cols, rows), lambda z: (z, 0)), side],
        out_shape=[
            jax.ShapeDtypeStruct((rows, count * cols), jnp.float32),
            jax.ShapeDtypeStruct((count * cols, rows), jnp.float32),
            jax.ShapeDtypeStruct((rows, count * cols), jnp.float32),
        ],
        compiler_params=pltpu.CompilerParams(vmem_limit_bytes=KERNEL_VMEM),
        cost_estimate=SMALL_COST,
    )(pair, single)


def row_norm(value):
    inverse = lax.rsqrt(jnp.mean(value * value, axis=-1, keepdims=True) + norm_eps)
    return value * inverse, inverse


def norm_back(grad, normed, inverse, gain):
    scaled = grad * gain
    return inverse * (scaled - normed * jnp.mean(scaled * normed, axis=-1, keepdims=True))


def silu_parts(gate_pre):
    sigmoid = jax.nn.sigmoid(gate_pre)
    return sigmoid, gate_pre * sigmoid


def halves(value, count):
    part = value.shape[1] // count
    return [value[:, i * part : (i + 1) * part] for i in range(count)]


def crossed(by_x, by_y):
    half = by_x[0].shape[0] // 2
    upper = [[rotated(v[:half], "x", i) for i in range(1, len(by_x))] for v in by_y[1:]]
    lower = [[rotated(v[half:], "y", k) for v in by_x[1:]] for k in range(1, len(by_y))]
    return upper, lower


def quarters(by_x, by_y, upper, lower):
    far = [[jnp.concatenate(v, axis=0) for v in zip(*rows)] for rows in zip(upper, lower)]
    return [by_x] + [[by_y[k], *far[k - 1]] for k in range(1, len(by_y))]


def matmul(left, right):
    return jnp.dot(left, right, preferred_element_type=jnp.float32)


def matmul_turned(left, right):
    return nt_dot(left, right)


def turned_matmul(left, right):
    return lax.dot_general(
        left, right, (((0,), (0,)), ((), ())), preferred_element_type=jnp.float32
    )


def sent_groups(value):
    size = lax.axis_size("y")
    place = lax.axis_index("y")
    width = value.shape[1] // size
    pieces = []
    for k in range(size):
        start = lax.rem(place + k, size) * width
        piece = lax.dynamic_slice_in_dim(value, start, width, 1)
        pieces.append(rotated(piece, "y", k) if k else piece)
    return pieces


def in_groups(pieces):
    size = len(pieces)
    place = lax.axis_index("y")
    return jnp.concatenate(
        [
            lax.select_n(place, *[pieces[(j - i) % size] for i in range(size)])
            for j in range(size)
        ],
        axis=1,
    )


def in_order(pieces):
    return natural_pieces(pieces, "y")


def turned_sum_kernel(blocks, cosine, sine, out):
    total = sum(blocks[i, 0].astype(jnp.float32) for i in range(blocks.shape[0]))
    cos, sin = key_tables(cosine[...], sine[...])
    out[...] = turned(total.T, cos, sin, -1.0).astype(jnp.bfloat16)


def turned_sum(blocks, cosine, sine):
    terms, segs, lanes, seg = blocks.shape
    table = pl.BlockSpec((seg, lanes), lambda s: (s, 0))
    return pl.pallas_call(
        turned_sum_kernel,
        grid=(segs,),
        in_specs=[pl.BlockSpec((terms, 1, lanes, seg), lambda s: (0, s, 0, 0)), table, table],
        out_specs=table,
        out_shape=jax.ShapeDtypeStruct((segs * seg, lanes), jnp.bfloat16),
        compiler_params=pltpu.CompilerParams(vmem_limit_bytes=KERNEL_VMEM),
        cost_estimate=SMALL_COST,
    )(blocks, cosine, sine)


def gathered_core(x_pieces):
    rows = jnp.stack(natural_pieces(x_pieces, "x"))
    rows = jnp.stack(natural_pieces(relative_pieces(rows, "c"), "c"), axis=1)
    return rows.reshape(-1, rows.shape[-1])


def own_first(value, axis):
    size = value.shape[0]
    place = lax.axis_index(axis)
    return [
        lax.dynamic_index_in_dim(value, lax.rem(place - k + size, size), 0, keepdims=False)
        for k in range(size)
    ]


def core_sum(part, rows):
    blocks = part.reshape(lax.axis_size("x"), lax.axis_size("c"), rows, -1)
    return summed_pieces(own_first(blocks.transpose(1, 0, 2, 3), "c"), "c").astype(jnp.bfloat16)


def x_blocks(value):
    return own_first(value, "x")


def tensor_sum(part, rows):
    return summed_pieces(x_blocks(core_sum(part, rows)), "x")


def local(
    tokens,
    norm_gain,
    q_weight,
    key_matrix,
    value_matrix,
    o_weight,
    mlp_gain,
    gate_weight,
    up_weight,
    down_weight,
    parents,
    out_grad,
):
    z_size, y_size, x_size = (lax.axis_size(name) for name in ("z", "y", "x"))
    tensor_size = x_size * lax.axis_size("c")
    low = jnp.bfloat16
    local_rows, width = tokens.shape
    group_rows = local_rows * tensor_size
    kv_cols = key_matrix.shape[1]
    kv_local = kv_cols // HEAD_SIZE
    q_cols = q_weight.shape[1]
    own_width = norm_gain.shape[0]

    own_tokens = relative_columns(tokens)
    own_grad = relative_columns(out_grad).astype(jnp.float32)
    both_gains = jnp.concatenate([norm_gain, mlp_gain])
    both_gains = jnp.pad(both_gains, (0, -both_gains.shape[0] % (2 * kv_cols)))
    key_heads, value_heads = halves(key_matrix, kv_local), halves(value_matrix, kv_local)
    kv_shard = jnp.concatenate(
        [
            jnp.concatenate([v for kv in zip(key_heads, value_heads) for v in kv], axis=1),
            both_gains.reshape(-1, 2 * kv_cols),
        ],
        axis=0,
    )
    kv_copies = jnp.broadcast_to(kv_shard[None], (z_size, *kv_shard.shape))
    kv_copies, q_weight = together(kv_copies, q_weight)
    kv_z = exchanged(kv_copies, "z")
    q_z = lax.all_gather(q_weight, "z", axis=0, tiled=True)
    group_tokens = gathered_core(relative_pieces(own_tokens, "x"))
    kv_z, o_weight = together(kv_z, o_weight)
    o_z = lax.all_gather(o_weight, "z", axis=0)

    depth = segment_depth(parents)
    seg_count = group_rows // SEG
    z_place, y_place = lax.axis_index("z"), lax.axis_index("y")
    sources = [lax.rem(y_place - k + y_size, y_size) for k in range(y_size)]
    segs = jnp.concatenate(
        [
            (z_place * y_size + source) * seg_count + jnp.arange(seg_count, dtype=jnp.int32)
            for source in sources
        ]
    )
    seg_ids = jnp.arange(depth.shape[0], dtype=jnp.int32)
    seg_depth = jnp.sum(jnp.where(segs[:, None] == seg_ids[None, :], depth[None, :], 0), axis=1)
    position = (seg_depth[:, None] * SEG + jnp.arange(SEG, dtype=jnp.int32)[None, :]).reshape(-1)
    cosine_table, sine_table = rope_tables(position, HEAD_SIZE)
    cosine_lanes = jnp.tile(cosine_table, (1, 4))
    sine_lanes = jnp.tile(sine_table, (1, 4))
    ordered = [jnp.concatenate(in_order(jnp.split(v, y_size))) for v in (cosine_lanes, sine_lanes)]
    cosine_lanes, sine_lanes, *ordered = settled(cosine_lanes, sine_lanes, *ordered)

    kv_zy = relative_pieces(kv_z, "y")
    kv_zy, cosine_lanes, sine_lanes, ordered = together(kv_zy, cosine_lanes, sine_lanes, ordered)
    kv_weights = [v[:, :own_width].reshape(-1, 2 * kv_cols) for v in kv_zy]
    gains = [
        v[:, own_width:].reshape(z_size, -1)[:, : 2 * own_width].reshape(z_size, 2, own_width)
        for v in kv_zy
    ]
    gains = jnp.stack(gains).astype(jnp.float32)
    gain_one, gain_two = gains[:, :, 0].reshape(-1), gains[:, :, 1].reshape(-1)
    inputs = own_tokens.astype(jnp.float32)
    normed_one, inv_one = row_norm(inputs)
    group_normed, _ = row_norm(group_tokens.astype(jnp.float32))
    rows_one = (group_normed * gain_one).astype(low)
    rows_one, q_z = together(rows_one, q_z)
    q_weights = relative_pieces(q_z, "y")
    kv_rows = project(rows_one, kv_weights, cosine_lanes, sine_lanes, keys=True)
    kv_swapped = jnp.stack(natural_pieces(sent_groups(kv_rows), "y"))
    all_kv = gathered(kv_swapped, "z").reshape(-1, SEG, LANES)
    wide_blocks = split_columns(after((gate_weight, up_weight), kv_z), z_size)
    q_weights, wide_blocks = together(q_weights, wide_blocks)
    query_rows = project(rows_one, q_weights, cosine_lanes, sine_lanes)
    queries = sent_groups(query_rows)
    all_kv, queries, o_z, wide_blocks = together(all_kv, queries, o_z, wide_blocks)

    wide_z = exchanged(wide_blocks, "z")
    o_weights = relative_pieces(o_z, "y")
    seg_lists = jnp.split(segs, y_size)
    attends, lows = [None] * y_size, [None] * y_size
    for k in range(y_size - 1, 0, -1):
        *attends[k], lows[k] = attend(parents, seg_lists[k], queries[k], all_kv)
    queries[0], attends[1:], lows[1:] = together(queries[0], attends[1:], lows[1:])
    returned = [rotated(v, "y", -k) for k, v in enumerate(lows[1:], 1)]
    *attends[0], lows[0] = attend(parents, seg_lists[0], queries[0], all_kv)
    attn_pieces = [lows[0], *returned]
    attn_pieces, o_weights = together(attn_pieces, o_weights)
    attn_part = o_forward(attn_pieces, o_weights, y_place)
    attn_low = in_groups(attn_pieces)
    attn_core = core_sum(attn_part, local_rows)
    attn_core, wide_z = together(attn_core, wide_z)

    gate_z, up_z = (wide_z[:, i].reshape(z_size * own_width, -1) for i in range(2))
    gate_zy, up_zy = relative_pieces(gate_z, "y"), relative_pieces(up_z, "y")
    gate_zx = relative_pieces(gate_z, "x")
    attn_mine = summed_pieces(x_blocks(attn_core), "x")
    attn_mine, up_z, down_weight = together(attn_mine, up_z, down_weight)

    middle = inputs + branch_scale * attn_mine
    normed_two, inv_two = row_norm(middle)
    hidden_two = (normed_two * gain_two).astype(low)
    rows_two = lax.all_gather(hidden_two, ("z", "c"), axis=0, tiled=True)
    down_z = exchanged(down_weight.reshape(z_size, -1, own_width), "z")
    gate_zx, gate_zy, up_z = together(gate_zx, gate_zy, up_z)
    gate_far = [relative_pieces(v, "y")[1:] for v in gate_zx[1:]]
    up_zx = relative_pieces(up_z, "x")
    grad_mlp = (branch_scale * own_grad).astype(low)
    up_zx, up_zy, grad_mlp, down_z = together(up_zx, up_zy, grad_mlp, down_z)
    grad_mlp_rows = lax.all_gather(grad_mlp, ("z", "c"), axis=0, tiled=True)
    up_far = [relative_pieces(v, "x")[1:] for v in up_zy[1:]]
    rows_two, gate_far, up_far, down_z = together(rows_two, gate_far, up_far, down_z)
    down_zy, down_zx = relative_pieces(down_z, "y"), relative_pieces(down_z, "x")
    gates = [gate_zx] + [[gate_zy[k], *[v[k - 1] for v in gate_far]] for k in range(1, y_size)]
    ups = [up_zx] + [[up_zy[k], *up_far[k - 1]] for k in range(1, y_size)]
    activated, gate_slope, up_slope = gate_forward(rows_two, gates, ups)
    down_zy, down_zx, activated, gate_slope, up_slope = together(
        down_zy, down_zx, activated, gate_slope, up_slope
    )
    down_crossed = together(*crossed(down_zx, down_zy))
    downs = quarters(down_zx, down_zy, *down_crossed)
    mlp_part = down_forward(activated, downs)
    mlp_part, grad_mlp_rows = together(mlp_part, grad_mlp_rows)

    mlp_mine = lax.psum_scatter(mlp_part, ("z", "c"), scatter_dimension=0, tiled=True)
    grad_parts, rows_parts = halves(grad_mlp_rows, y_size), halves(rows_two, y_size)
    acts = halves(activated, x_size)
    down_far = [summed_pieces([turned_matmul(a, b) for a in grad_parts], "y").astype(low) for b in acts[1:]]
    grad_gate_act, grad_up_act = gate_backward(grad_mlp_rows, downs, gate_slope, up_slope)
    grad_gate_act, grad_up_act = together(grad_gate_act, grad_up_act)

    gate_parts, up_parts = halves(grad_gate_act, x_size), halves(grad_up_act, x_size)
    gate_dots = [[turned_matmul(a, b) for a in rows_parts] for b in gate_parts[1:]]
    up_dots = [[turned_matmul(a, b) for b in up_parts] for a in rows_parts[1:]]
    for dots in gate_dots + up_dots:
        dots[1:] = [v.astype(low) for v in dots[1:]]
    grad_gate_act, gate_dots, up_dots = together(grad_gate_act, gate_dots, up_dots)
    gate_far = [summed_pieces(v, "y").astype(low) for v in gate_dots]
    up_far = [summed_pieces(v, "x").astype(low) for v in up_dots]
    input_part = turned_product([grad_gate_act, grad_up_act], [gates, ups])
    input_part, down_far = together(input_part, down_far)

    grad_rows_two = lax.psum_scatter(input_part, ("z", "c"), scatter_dimension=0, tiled=True)
    gate_far, up_far, acts = together(gate_far, up_far, acts)
    down_near = summed_pieces([turned_matmul(a, acts[0]) for a in grad_parts], "y")
    down_far = [rotated(v, "x", -1 - i) for i, v in enumerate(down_far)]
    down_near, down_far, mlp_mine = together(down_near, down_far, mlp_mine)
    grad_down_z = sum([v.astype(jnp.float32) for v in down_far], down_near).astype(low)
    gate_near = summed_pieces([turned_matmul(a, gate_parts[0]) for a in rows_parts], "y")
    gate_far = [rotated(v, "x", -1 - i) for i, v in enumerate(gate_far)]
    up_near = [turned_matmul(rows_parts[0], b) for b in up_parts]
    up_near[1:] = [v.astype(low) for v in up_near[1:]]
    grad_rows_two, mlp_mine, up_far, up_near, grad_down_z = together(
        grad_rows_two, mlp_mine, up_far, up_near, grad_down_z
    )
    grad_rows_two = grad_rows_two.astype(jnp.float32)
    gain_two_part = jnp.sum(grad_rows_two * normed_two, axis=0)
    grad_middle = own_grad + norm_back(grad_rows_two, normed_two, inv_two, gain_two)
    grad_attn = (branch_scale * grad_middle).astype(low)
    attn_x = relative_pieces(grad_attn, "x")
    up_far = [rotated(v, "y", -1 - i) for i, v in enumerate(up_far)]
    grad_gate_z = sum([v.astype(jnp.float32) for v in gate_far], gate_near).astype(low)
    wide_z = jnp.stack([v.reshape(z_size, own_width, -1) for v in (grad_gate_z, grad_down_z)], 1)
    attn_x, wide_z, up_near = together(attn_x, wide_z, up_near)
    grad_attn_rows = gathered_core(attn_x)
    grad_heads = o_backward(grad_attn_rows, o_weights)
    grad_heads, grad_attn_rows, up_near, wide_z = together(
        grad_heads, grad_attn_rows, up_near, wide_z
    )
    wide_z = exchanged(wide_z, "z")

    grad_heads = sent_groups(grad_heads)
    o_dots = [turned_matmul(v, attn_low) for v in halves(grad_attn_rows, y_size)[1:]]
    o_dots = [v.astype(low) for v in o_dots]
    grad_heads, o_dots, up_near, grad_attn_rows = together(
        grad_heads, o_dots, up_near, grad_attn_rows
    )
    o_sent = [rotated(v, "y", -1 - i) for i, v in enumerate(o_dots)]
    up_mine = [rotated(v, "x", -1 - i) for i, v in enumerate(up_near[1:])]
    grad_queries, sums = [None] * y_size, None
    for k in range(y_size - 1, 0, -1):
        grad_queries[k], sums = attend_back(
            parents, seg_lists[k], queries[k], grad_heads[k], *attends[k], cosine_lanes,
            sine_lanes, k, all_kv, sums,
        )
    grad_o_y = turned_matmul(halves(grad_attn_rows, y_size)[0], attn_low)
    grad_o_y = sum([v.astype(jnp.float32) for v in o_sent], grad_o_y).astype(low)
    grad_queries[1:], sums, grad_o_y = together(grad_queries[1:], sums, grad_o_y)
    grad_o = lax.psum_scatter(grad_o_y, "z", scatter_dimension=0, tiled=True)
    returned = [rotated(v, "y", -k) for k, v in enumerate(grad_queries[1:], 1)]
    grad_queries[0], grad_kv = attend_back(
        parents, seg_lists[0], queries[0], grad_heads[0], *attends[0], cosine_lanes, sine_lanes,
        0, all_kv, sums,
    )
    grad_kv, wide_z = together(grad_kv, wide_z)
    grad_queries[0], returned, up_far, up_mine, up_near = after(
        (grad_queries[0], returned, up_far, up_mine, up_near), grad_kv
    )

    def owned_dots(left, right):
        dots = [turned_matmul(v, right) for v in halves(left, y_size)]
        return dots[:1] + [v.astype(low) for v in dots[1:]]

    def sent_back(dots):
        return [rotated(v, "y", -1 - i) for i, v in enumerate(dots[1:])]

    def total(own, sent):
        return sum([v.astype(jnp.float32) for v in sent], own).astype(low)

    kv_mine = exchanged(grad_kv.reshape(z_size, y_size * seg_count, LANES, SEG), "z")
    grad_queries = in_groups([grad_queries[0], *returned])
    query_dots = owned_dots(rows_one, grad_queries)
    query_sent = sent_back(query_dots)
    q_full = jnp.concatenate(q_weights, axis=0)
    query_part = matmul_turned(grad_queries, q_full)
    grad_up_z = total(up_near[0], up_far + up_mine)
    kv_mine, query_part, query_dots, query_sent, grad_up_z, grad_o = together(
        kv_mine, query_part, query_dots, query_sent, grad_up_z, grad_o
    )

    grad_up = exchanged(grad_up_z.reshape(z_size, own_width, -1), "z")
    kv_mine = turned_sum(kv_mine, *ordered).reshape(y_size, group_rows, LANES)
    kv_mine = own_first(kv_mine, "y")
    grad_kv_rows = in_groups(
        [kv_mine[0]] + [rotated(v, "y", -k) for k, v in enumerate(kv_mine[1:], 1)]
    )
    kv_full = jnp.concatenate(kv_weights, axis=0)
    input_one = (query_part + matmul_turned(grad_kv_rows, kv_full)).astype(low)
    input_core = core_sum(input_one, local_rows)
    grad_q_y = total(query_dots[0], query_sent)
    kv_dots = owned_dots(rows_one, grad_kv_rows)
    kv_sent = sent_back(kv_dots)
    input_core, grad_q_y, grad_up, wide_z, grad_o = together(
        input_core, grad_q_y, grad_up, wide_z, grad_o
    )
    grad_q = lax.psum_scatter(grad_q_y, "z", scatter_dimension=0, tiled=True)
    input_x = x_blocks(input_core)
    input_sent = [rotated(v, "x", -1 - i) for i, v in enumerate(input_x[1:])]
    grad_gate, grad_down, grad_up = finished(wide_z, grad_up)
    input_x[0], input_sent, kv_sent, kv_dots, grad_gate, grad_down, grad_up, grad_o = together(
        input_x[0], input_sent, kv_sent, kv_dots, grad_gate, grad_down, grad_up, grad_o
    )
    grad_rows_one = sum([v.astype(jnp.float32) for v in input_sent], input_x[0].astype(jnp.float32))
    kv_blocks = own_first(total(kv_dots[0], kv_sent).reshape(z_size, own_width, -1), "z")
    kv_sent = [rotated(v, "z", -1 - i) for i, v in enumerate(kv_blocks[1:])]
    gain_one_part = jnp.sum(grad_rows_one * normed_one, axis=0)
    grad_inputs = grad_middle + norm_back(grad_rows_one, normed_one, inv_one, gain_one)
    gain_parts = jnp.stack([gain_one_part, gain_two_part], axis=0)
    gain_parts = natural_columns(gain_parts).reshape(2, z_size * y_size, 1, own_width)
    gain_parts = jnp.broadcast_to(
        gain_parts, (2, z_size * y_size, tensor_size, own_width)
    ).reshape(2, -1, own_width).transpose(1, 0, 2)
    gain_parts, grad_inputs, mlp_mine = together(gain_parts, grad_inputs, mlp_mine)
    gain_parts = exchanged(gain_parts, ("z", "y", "x", "c"))
    mixed = natural_columns((middle + branch_scale * mlp_mine.astype(jnp.float32)).astype(low))
    grad_tokens = natural_columns(grad_inputs.astype(low))
    grad_o = after(grad_o, grad_inputs).astype(jnp.float32).T
    gain_parts, kv_sent, kv_blocks, grad_q, grad_o, grad_tokens, mixed = together(
        gain_parts, kv_sent, kv_blocks, grad_q.astype(jnp.float32), grad_o, grad_tokens, mixed
    )
    gain_sums = jnp.sum(gain_parts, axis=0)
    grad_kv_weight = sum([v.astype(jnp.float32) for v in kv_sent], kv_blocks[0].astype(jnp.float32))
    grad_heads = halves(grad_kv_weight, 2 * kv_local)
    return (
        mixed,
        grad_tokens,
        gain_sums[0],
        grad_q,
        jnp.concatenate(grad_heads[::2], axis=1),
        jnp.concatenate(grad_heads[1::2], axis=1),
        grad_o,
        gain_sums[1],
        grad_gate,
        grad_up,
        grad_down,
    )


def solution(mesh):
    dp_size, tensor_size = mesh.shape["dp"], mesh.shape["tensor"]
    fine = jax.sharding.Mesh(
        mesh.devices.reshape(dp_size // 2, 2, tensor_size // 2, 2), ("z", "y", "x", "c")
    )
    dp, tensor = ("z", "y"), ("x", "c")
    tokens = P(dp + tensor, None)
    rows = P(dp, tensor)
    columns = P(tensor, dp)
    in_specs = (
        tokens,
        P(dp),
        rows,
        rows,
        rows,
        columns,
        P(dp),
        rows,
        rows,
        columns,
        P(),
        tokens,
    )
    out_specs = (
        tokens,
        tokens,
        P(dp),
        rows,
        rows,
        rows,
        columns,
        P(dp),
        rows,
        rows,
        columns,
    )
    return jax.shard_map(local, mesh=fine, in_specs=in_specs, out_specs=out_specs, check_vma=False)
```

```python
import functools

import jax
import jax.numpy as jnp
from jax import lax
from jax.experimental import pallas as pl
from jax.experimental.pallas import tpu as pltpu
from jax.sharding import PartitionSpec as P

HEAD_SIZE = 64
SEG = 256
MAX_STEPS = 9
LANES = 2 * HEAD_SIZE
KERNEL_VMEM = 32 * 2**20
SMALL_COST = pl.CostEstimate(flops=2**28, bytes_accessed=2**18, transcendentals=0)


attn_scale = 0.015625
branch_scale = 0.22
norm_eps = 1e-05
rope_base = 10000000.0
masked_score = -1e30


def segment_depth(parents):
    seg_total = parents.shape[0]
    seg_ids = jnp.arange(seg_total, dtype=jnp.int32)
    reach = (parents[:, None] == seg_ids[None, :]) | (seg_ids[:, None] == seg_ids[None, :])
    reach = reach.astype(jnp.float32)
    for doubling in range(4):
        reach = jnp.minimum(jnp.dot(reach, reach, preferred_element_type=jnp.float32), 1.0)
    return jnp.sum(reach, axis=1).astype(jnp.int32) - 1


def rope_tables(position, head_dim):
    half_dim = head_dim // 2
    exponent = jnp.arange(half_dim, dtype=jnp.float32) * (2.0 / head_dim)
    inverse = jnp.power(rope_base, -exponent)
    angles = position.astype(jnp.float32)[:, None] * inverse[None, :]
    return (jnp.cos(angles), jnp.sin(angles))


def rotated(value, axis, step):
    size = lax.axis_size(axis)
    return lax.ppermute(value, axis, [(i, (i + step) % size) for i in range(size)])


def relative_pieces(value, axis):
    return [value] + [rotated(value, axis, k) for k in range(1, lax.axis_size(axis))]


def natural_pieces(pieces, axis):
    size = len(pieces)
    place = lax.axis_index(axis)
    return [
        lax.select_n(place, *[pieces[(i - j) % size] for i in range(size)]) for j in range(size)
    ]


def gathered(value, axis):
    size = lax.axis_size(axis)
    copies = jnp.broadcast_to(value[None], (size, *value.shape))
    return lax.all_to_all(copies, axis, 0, 0, tiled=True)


def exchanged(blocks, axis):
    return lax.all_to_all(blocks, axis, 0, 0, tiled=True)


def summed_pieces(pieces, axis):
    sent = [rotated(pieces[k].astype(jnp.bfloat16), axis, -k) for k in range(1, len(pieces))]
    total = pieces[0].astype(jnp.float32)
    for value in sent:
        total = total + value.astype(jnp.float32)
    return total


def summed_blocks(blocks, axis):
    return jnp.sum(exchanged(blocks.astype(jnp.bfloat16), axis).astype(jnp.float32), axis=0)


def column_blocks(value, count):
    return value.reshape(value.shape[0], count, -1).transpose(1, 0, 2)


def joined_columns(blocks):
    return blocks.transpose(1, 0, 2).reshape(blocks.shape[1], -1)


def relative_columns(value):
    size = lax.axis_size("y")
    place = lax.axis_index("y")
    rows = value.shape[0]
    split = value.reshape(rows, lax.axis_size("z"), size, -1)
    flat = [split[:, :, i].reshape(rows, -1) for i in range(size)]
    return jnp.concatenate(
        [
            lax.select_n(place, *[flat[(i - k) % size] for i in range(size)])
            for k in range(size)
        ],
        axis=1,
    )


def natural_columns(value):
    size = lax.axis_size("y")
    rows = value.shape[0]
    split = value.reshape(rows, size, lax.axis_size("z"), -1)
    parts = natural_pieces([split[:, k] for k in range(size)], "y")
    return jnp.stack(parts, axis=2).reshape(rows, -1)


def together(*values):
    return lax.optimization_barrier(values)


def after(value, *others):
    return lax.optimization_barrier((value, *others))[0]


def ancestor_count(parents, seg):
    def climb(step, state):
        current, count = state
        above = parents[current]
        return above, count + jnp.where(above != current, 1, 0)

    return lax.fori_loop(0, MAX_STEPS, climb, (seg, jnp.int32(1)))[1]


def left_lanes(shape):
    return lax.broadcasted_iota(jnp.int32, shape, 1) < HEAD_SIZE


def stacked_heads(pairs, to_left):
    left = left_lanes(pairs[0].shape)
    stack = []
    for pair in pairs:
        swapped = pltpu.roll(pair, HEAD_SIZE, 1)
        for head in (pair, swapped) if to_left else (swapped, pair):
            stack.append(jnp.where(left, head, 0.0) if to_left else jnp.where(left, 0.0, head))
    return jnp.concatenate(stack, axis=0)


def unstacked_heads(stack, from_left):
    left = left_lanes((SEG, 2 * HEAD_SIZE))
    pairs = []
    for first in range(0, stack.shape[0], 2 * SEG):
        even, odd = stack[first : first + SEG], stack[first + SEG : first + 2 * SEG]
        if from_left:
            odd = pltpu.roll(odd, HEAD_SIZE, 1)
        else:
            even = pltpu.roll(even, HEAD_SIZE, 1)
        pairs.append(jnp.where(left, even, odd))
    return pairs


def turned(value, cosine, sine, direction):
    half = HEAD_SIZE // 2
    lane = lax.broadcasted_iota(jnp.int32, value.shape, 1)
    first = lax.rem(lane, HEAD_SIZE) < half
    ahead = pltpu.roll(value, LANES - half, 1)
    behind = pltpu.roll(value, half, 1)
    signed = sine * direction
    return value * cosine + jnp.where(first, -ahead * signed, behind * signed)


def nt_dot(left, right):
    return lax.dot_general(
        left, right, (((1,), (1,)), ((), ())), preferred_element_type=jnp.float32
    )


def nn_dot(left, right):
    return lax.dot_general(
        left, right, (((1,), (0,)), ((), ())), preferred_element_type=jnp.float32
    )


def causal_tile(rows):
    query = lax.rem(lax.broadcasted_iota(jnp.int32, (rows, SEG), 0), SEG)
    return lax.broadcasted_iota(jnp.int32, (rows, SEG), 1) <= query


def lane_blocks(ref):
    return [ref[:, at : at + LANES] for at in range(0, ref.shape[1], LANES)]


def key_tables(cosine, sine):
    left = left_lanes(cosine.shape)
    return jnp.where(left, cosine, 1.0), jnp.where(left, sine, 0.0)


def settle_kernel(*refs):
    count = len(refs) // 2
    for value, out in zip(refs[:count], refs[count:]):
        out[...] = value[...]


def settled(*values):
    return pl.pallas_call(
        settle_kernel,
        out_shape=[jax.ShapeDtypeStruct(v.shape, v.dtype) for v in values],
        compiler_params=pltpu.CompilerParams(vmem_limit_bytes=KERNEL_VMEM),
        cost_estimate=SMALL_COST,
    )(*values)


def project_kernel(parts, keys, rows, *refs):
    weights, (cosine, sine, out) = refs[:parts], refs[parts:]
    depth = weights[0].shape[0]
    product = sum(nn_dot(rows[:, i * depth : (i + 1) * depth], w[...]) for i, w in enumerate(weights))
    cos, sin = cosine[...], sine[...]
    if keys:
        cos, sin = key_tables(cos, sin)
    for at in range(0, product.shape[1], LANES):
        block = turned(product[:, at : at + LANES], cos, sin, 1.0)
        out[:, at : at + LANES] = block.astype(jnp.bfloat16)


def project(rows, weights, cosine, sine, keys=False):
    count, width = rows.shape
    depth, cols = weights[0].shape
    step = 2 * LANES
    table = pl.BlockSpec((count, LANES), lambda j: (0, 0))
    return pl.pallas_call(
        functools.partial(project_kernel, len(weights), keys),
        grid=(cols // step,),
        in_specs=[pl.BlockSpec((count, width), lambda j: (0, 0))]
        + [pl.BlockSpec((depth, step), lambda j: (0, j))] * len(weights)
        + [table, table],
        out_specs=pl.BlockSpec((count, step), lambda j: (0, j)),
        out_shape=jax.ShapeDtypeStruct((count, cols), jnp.bfloat16),
        compiler_params=pltpu.CompilerParams(vmem_limit_bytes=KERNEL_VMEM),
        cost_estimate=SMALL_COST,
    )(rows, *weights, cosine, sine)


def attend_kernel(parents, segs, queries, keys_values, out, stats, out_low, scores):
    seg = segs[pl.program_id(0)]
    count = ancestor_count(parents, seg)
    pairs = [block.astype(jnp.float32) * attn_scale for block in lane_blocks(queries)]
    stack = stacked_heads(pairs, True).astype(jnp.bfloat16)
    rows = stack.shape[0]

    first = jnp.where(causal_tile(rows), nt_dot(stack, keys_values[seg]), masked_score)
    scores[0] = first

    def folded(tile):
        return jnp.maximum(tile[:, :LANES], tile[:, LANES:])

    def measure(step, state):
        current, top = state
        current = parents[current]
        tile = nt_dot(stack, keys_values[current])
        scores[step] = tile
        return current, jnp.maximum(top, folded(tile))

    top = lax.fori_loop(1, count, measure, (seg, folded(first)))[1]
    row_max = jnp.max(top, axis=1, keepdims=True)
    left = left_lanes((SEG, LANES))

    def gather(step, state):
        current, mixed = state
        terms = jnp.exp(scores[step] - row_max).astype(jnp.bfloat16)
        tile = jnp.where(left, jnp.ones((SEG, LANES), jnp.bfloat16), keys_values[current])
        return parents[current], mixed + nn_dot(terms, tile)

    start = (seg, jnp.zeros((rows, LANES), jnp.float32))
    mixed = lax.fori_loop(0, count, gather, start)[1]
    total = mixed[:, :1]
    mixed = mixed / total
    stats[0] = row_max + jnp.log(total)
    for place, pair in enumerate(unstacked_heads(mixed, False)):
        out[:, place * LANES : (place + 1) * LANES] = pair
        out_low[:, place * LANES : (place + 1) * LANES] = pair.astype(jnp.bfloat16)


def attend_back_kernel(
    parents, segs, queries, grads, attended, stats, cosine, sine, keys_values, *refs
):
    earlier, (grad_queries, grad_kv, kv_sum) = refs[:-3], refs[-3:]
    seg = segs[pl.program_id(0)]
    count = ancestor_count(parents, seg)

    @pl.when(pl.program_id(0) == 0)
    def _():
        kv_sum[...] = earlier[0][...] if earlier else jnp.zeros_like(kv_sum)

    query_pairs = [block.astype(jnp.float32) * attn_scale for block in lane_blocks(queries)]
    grad_pairs = [block.astype(jnp.float32) for block in lane_blocks(grads)]
    left = left_lanes((SEG, LANES))
    deltas = []
    for pair, out in zip(grad_pairs, lane_blocks(attended)):
        product = pair * out
        deltas.append(jnp.sum(jnp.where(left, product, 0.0), axis=1, keepdims=True))
        deltas.append(jnp.sum(jnp.where(left, 0.0, product), axis=1, keepdims=True))
    delta = jnp.concatenate(deltas, axis=0)
    query_wide = stacked_heads(query_pairs, True)
    grad_wide = stacked_heads(grad_pairs, False)
    query_stack, grad_stack = query_wide.astype(jnp.bfloat16), grad_wide.astype(jnp.bfloat16)
    query_turned = query_wide.T.astype(jnp.bfloat16)
    grad_turned = grad_wide.T.astype(jnp.bfloat16)
    log_total = stats[0]
    rows = query_stack.shape[0]

    def visit(current, total, diagonal):
        tile_kv = keys_values[current]
        tile = nt_dot(query_stack, tile_kv)
        if diagonal:
            tile = jnp.where(causal_tile(rows), tile, masked_score)
        probs = jnp.exp(tile - log_total)
        grad_probs = nt_dot(grad_stack, tile_kv)
        grad_tile = (probs * (grad_probs - delta)).astype(jnp.bfloat16)
        kv_sum[current] += nn_dot(query_turned, grad_tile) + nn_dot(
            grad_turned, probs.astype(jnp.bfloat16)
        )
        return total + nn_dot(grad_tile, tile_kv)

    total = visit(seg, jnp.zeros((rows, LANES), jnp.float32), True)

    def climb(step, state):
        current, total = state
        current = parents[current]
        return current, visit(current, total, False)

    total = lax.fori_loop(1, count, climb, (seg, total))[1]
    cos, sin = cosine[...], sine[...]
    for place, pair in enumerate(unstacked_heads(total * attn_scale, True)):
        grad_queries[:, place * LANES : (place + 1) * LANES] = turned(
            pair, cos, sin, -1.0
        ).astype(jnp.bfloat16)

    @pl.when(pl.program_id(0) == pl.num_programs(0) - 1)
    def _():
        grad_kv[...] = kv_sum[...].astype(grad_kv.dtype)


def attention_specs(cols, seg_total):
    block = pl.BlockSpec((SEG, cols), lambda s: (s, 0))
    table = pl.BlockSpec((SEG, LANES), lambda s: (s, 0))
    whole = pl.BlockSpec((seg_total, SEG, LANES), lambda s: (0, 0, 0))
    rows = SEG * (cols // HEAD_SIZE)
    stat = pl.BlockSpec((1, rows, 1), lambda s: (s, 0, 0))
    return block, table, whole, rows, stat, pl.BlockSpec(memory_space=pltpu.SMEM)


def attend(parents, segs, queries, keys_values):
    count, cols = queries.shape
    block, table, whole, rows, stat, scalar = attention_specs(cols, keys_values.shape[0])
    steps = count // SEG
    return pl.pallas_call(
        attend_kernel,
        grid=(steps,),
        in_specs=[scalar, scalar, block, whole],
        out_specs=[block, stat, block],
        out_shape=[
            jax.ShapeDtypeStruct((count, cols), jnp.float32),
            jax.ShapeDtypeStruct((steps, rows, 1), jnp.float32),
            jax.ShapeDtypeStruct((count, cols), jnp.bfloat16),
        ],
        scratch_shapes=[pltpu.VMEM((MAX_STEPS + 1, rows, SEG), jnp.float32)],
        compiler_params=pltpu.CompilerParams(vmem_limit_bytes=KERNEL_VMEM),
        cost_estimate=SMALL_COST,
    )(parents, segs, queries, keys_values)


def attend_back(
    parents, segs, queries, grads, attended, stats, cosine, sine, place, keys_values, earlier=None
):
    count, cols = queries.shape
    first = place * (count // SEG)
    seg_total = keys_values.shape[0]
    block, table, whole, rows, stat, scalar = attention_specs(cols, seg_total)
    sums = pl.BlockSpec((seg_total, LANES, SEG), lambda s: (0, 0, 0))
    last = earlier is not None
    sum_type = jnp.bfloat16 if last else jnp.float32
    return pl.pallas_call(
        attend_back_kernel,
        grid=(count // SEG,),
        in_specs=[scalar, scalar, block, block, block, stat]
        + [pl.BlockSpec((SEG, LANES), lambda s: (first + s, 0))] * 2
        + [whole]
        + [sums] * last,
        out_specs=[block, sums],
        out_shape=[
            jax.ShapeDtypeStruct((count, cols), jnp.bfloat16),
            jax.ShapeDtypeStruct((seg_total, LANES, SEG), sum_type),
        ],
        scratch_shapes=[pltpu.VMEM((seg_total, LANES, SEG), jnp.float32)],
        compiler_params=pltpu.CompilerParams(vmem_limit_bytes=56 * 2**20),
        cost_estimate=SMALL_COST,
    )(
        parents, segs, queries, grads, attended, stats, cosine, sine, keys_values,
        *([earlier] if last else []),
    )


def in_turn(per, count, step):
    for i in range(count):
        pl.when(pl.program_id(1) // per == i)(functools.partial(step, i))


def gate_kernel(per, parts, pieces, rows, *refs):
    gates, ups = refs[: parts * pieces], refs[parts * pieces : 2 * parts * pieces]
    activated, gate_slope, up_slope = refs[2 * parts * pieces :]
    depth = gates[0].shape[0]

    def product(weights, i):
        return sum(
            nn_dot(rows[:, k * depth : (k + 1) * depth], weights[k * pieces + i][...])
            for k in range(parts)
        )

    def step(i):
        gate, up = product(gates, i), product(ups, i)
        sigmoid = 1.0 / (1.0 + jnp.exp(-gate))
        silu = gate * sigmoid
        activated[...] = (silu * up).astype(jnp.bfloat16)
        gate_slope[...] = up * sigmoid * (1.0 + gate * (1.0 - sigmoid))
        up_slope[...] = silu

    in_turn(per, pieces, step)


def gate_back_kernel(per, parts, pieces, grads, *refs):
    weights, (gate_slope, up_slope, grad_gate, grad_up) = refs[:-4], refs[-4:]
    blocks, _, depth = weights[0].shape

    def step(i):
        grad = 0.0
        for k in range(parts):
            for z in range(blocks):
                at = (k * blocks + z) * depth
                grad = grad + nt_dot(grads[:, at : at + depth], weights[k * pieces + i][z])
        grad_gate[...] = (grad * gate_slope[...]).astype(jnp.bfloat16)
        grad_up[...] = (grad * up_slope[...]).astype(jnp.bfloat16)

    in_turn(per, pieces, step)


def down_kernel(per, parts, pieces, acts, *refs):
    weights, out = refs[:-1], refs[-1]
    depth = weights[0].shape[1]

    def step(k):
        total = sum(
            nn_dot(acts[:, i * depth : (i + 1) * depth], weights[k * pieces + i][0])
            for i in range(pieces)
        )
        out[...] = total.astype(jnp.bfloat16)

    in_turn(per, parts, step)


def turned_kernel(terms, per, parts, pieces, *refs):
    lefts, weights, out = refs[:terms], refs[terms:-1], refs[-1]
    depth = weights[0].shape[1]

    def step(k):
        total = 0.0
        for term, left in enumerate(lefts):
            for i in range(pieces):
                weight = weights[(term * parts + k) * pieces + i]
                total = total + nt_dot(left[:, i * depth : (i + 1) * depth], weight[...])
        out[...] = total.astype(jnp.bfloat16)

    in_turn(per, parts, step)


def wide_call(kernel, whole, weights, tiled, axis, by_piece, outs):
    parts, pieces = len(weights[0]), len(weights[0][0])
    shape = weights[0][0][0].shape
    groups = pieces if by_piece else parts
    if len(shape) == 3 and axis == 0:
        width, block, per = shape[0] * shape[2], (1, *shape[1:]), shape[0]
    else:
        width = shape[axis]
        per = width // min(width, 256)
        block = tuple(n // per if at == axis else n for at, n in enumerate(shape))
    tile = (min(whole[0].shape[0], 1024), width // per)
    count, cols = whole[0].shape[0], groups * width

    def piece_spec(k, i):
        group = i if by_piece else k

        def place(row, col):
            at = jnp.clip(col - group * per, 0, per - 1)
            return tuple(at if dim == axis else 0 for dim in range(len(shape)))

        return pl.BlockSpec(block, place)

    tile_spec = pl.BlockSpec(tile, lambda row, col: (row, col))
    flat = [v for weight in weights for row in weight for v in row]
    return pl.pallas_call(
        functools.partial(kernel, per, parts, pieces),
        grid=(count // tile[0], groups * per),
        in_specs=[pl.BlockSpec((tile[0], v.shape[1]), lambda row, col: (row, 0)) for v in whole]
        + [piece_spec(k, i) for _ in weights for k in range(parts) for i in range(pieces)]
        + [tile_spec] * len(tiled),
        out_specs=[tile_spec] * len(outs),
        out_shape=[jax.ShapeDtypeStruct((count, cols), t) for t in outs],
        compiler_params=pltpu.CompilerParams(vmem_limit_bytes=KERNEL_VMEM),
        cost_estimate=SMALL_COST,
    )(*whole, *flat, *tiled)


def gate_forward(rows, gates, ups):
    outs = (jnp.bfloat16, jnp.float32, jnp.float32)
    return wide_call(gate_kernel, [rows], [gates, ups], [], 1, True, outs)


def gate_backward(grads, downs, gate_slope, up_slope):
    outs = (jnp.bfloat16, jnp.bfloat16)
    return wide_call(gate_back_kernel, [grads], [downs], [gate_slope, up_slope], 1, True, outs)


def down_forward(acts, downs):
    if downs[0][0].shape[2] % LANES:
        rows = [jnp.concatenate([joined_columns(v) for v in row], axis=0) for row in downs]
        return nn_dot(acts, jnp.concatenate(rows, axis=1)).astype(jnp.bfloat16)
    return wide_call(down_kernel, [acts], [downs], [], 0, False, (jnp.bfloat16,))[0]


def turned_product(lefts, weights):
    kernel = functools.partial(turned_kernel, len(lefts))
    return wide_call(kernel, lefts, weights, [], 0, False, (jnp.bfloat16,))[0]


def o_kernel(parts, place, *refs):
    rows, weights, out = refs[:-1 - parts], refs[-1 - parts : -1], refs[-1]
    blocks = weights[0].shape[0]
    depth = rows[0].shape[1]
    at = lax.rem(pl.program_id(0), blocks)
    for k in range(parts):

        @pl.when(pl.program_id(0) // blocks == k)
        def _(k=k):
            total = 0.0
            for i, piece in enumerate(rows):
                group = lax.rem(place[0] + i, len(rows))
                start = pl.multiple_of(group * depth, depth)
                total = total + nn_dot(piece[...], weights[k][at, pl.ds(start, depth), :])
            out[...] = total.astype(jnp.bfloat16)


def o_forward(pieces, weights, place):
    count, depth = pieces[0].shape
    blocks, _, step = weights[0].shape
    if step % LANES:
        full = jnp.concatenate([joined_columns(v) for v in weights], axis=1)
        return nn_dot(in_groups(pieces), full).astype(jnp.bfloat16)
    whole = pl.BlockSpec(weights[0].shape, lambda j: (0, 0, 0))
    return pl.pallas_call(
        functools.partial(o_kernel, len(weights)),
        grid=(len(weights) * blocks,),
        in_specs=[pl.BlockSpec(memory_space=pltpu.SMEM)]
        + [pl.BlockSpec((count, depth), lambda j: (0, 0))] * len(pieces)
        + [whole] * len(weights),
        out_specs=pl.BlockSpec((count, step), lambda j: (0, j)),
        out_shape=jax.ShapeDtypeStruct((count, len(weights) * blocks * step), jnp.bfloat16),
        compiler_params=pltpu.CompilerParams(vmem_limit_bytes=KERNEL_VMEM),
        cost_estimate=SMALL_COST,
    )(place.astype(jnp.int32).reshape(1), *pieces, *weights)


def o_back_kernel(parts, rows, *refs):
    weights, out = refs[:parts], refs[parts]
    blocks, _, step = weights[0].shape
    total = 0.0
    for k in range(parts):
        for z in range(blocks):
            at = (k * blocks + z) * step
            total = total + nt_dot(rows[:, at : at + step], weights[k][z])
    out[...] = total.astype(jnp.bfloat16)


def o_backward(rows, weights):
    return pl.pallas_call(
        functools.partial(o_back_kernel, len(weights)),
        out_shape=jax.ShapeDtypeStruct((rows.shape[0], weights[0].shape[1]), jnp.bfloat16),
        compiler_params=pltpu.CompilerParams(vmem_limit_bytes=KERNEL_VMEM),
        cost_estimate=SMALL_COST,
    )(rows, *weights)


def split_kernel(*refs):
    values, out = refs[:-1], refs[-1]
    for i, value in enumerate(values):
        out[0, i] = value[...]


def split_columns(values, count):
    rows, cols = values[0].shape
    step = cols // count
    if step % LANES:
        return jnp.stack([column_blocks(v, count) for v in values], axis=1)
    return pl.pallas_call(
        split_kernel,
        grid=(count,),
        in_specs=[pl.BlockSpec((rows, step), lambda j: (0, j))] * len(values),
        out_specs=pl.BlockSpec((1, len(values), rows, step), lambda j: (j, 0, 0, 0)),
        out_shape=jax.ShapeDtypeStruct((count, len(values), rows, step), values[0].dtype),
        compiler_params=pltpu.CompilerParams(vmem_limit_bytes=KERNEL_VMEM),
        cost_estimate=SMALL_COST,
    )(*values)


def finish_kernel(pair, single, first, second, third):
    first[...] = pair[0, 0].astype(jnp.float32)
    second[...] = pair[0, 1].astype(jnp.float32).T
    third[...] = single[0].astype(jnp.float32)


def finished(pair, single):
    count, _, rows, cols = pair.shape
    if cols % LANES or rows % LANES:
        first, second, third = (joined_columns(v) for v in (pair[:, 0], pair[:, 1], single))
        return [v.astype(jnp.float32) for v in (first, second.T, third)]
    side = pl.BlockSpec((rows, cols), lambda z: (0, z))
    return pl.pallas_call(
        finish_kernel,
        grid=(count,),
        in_specs=[
            pl.BlockSpec((1, 2, rows, cols), lambda z: (z, 0, 0, 0)),
            pl.BlockSpec((1, rows, cols), lambda z: (z, 0, 0)),
        ],
        out_specs=[side, pl.BlockSpec((cols, rows), lambda z: (z, 0)), side],
        out_shape=[
            jax.ShapeDtypeStruct((rows, count * cols), jnp.float32),
            jax.ShapeDtypeStruct((count * cols, rows), jnp.float32),
            jax.ShapeDtypeStruct((rows, count * cols), jnp.float32),
        ],
        compiler_params=pltpu.CompilerParams(vmem_limit_bytes=KERNEL_VMEM),
        cost_estimate=SMALL_COST,
    )(pair, single)


def row_norm(value):
    inverse = lax.rsqrt(jnp.mean(value * value, axis=-1, keepdims=True) + norm_eps)
    return value * inverse, inverse


def norm_back(grad, normed, inverse, gain):
    scaled = grad * gain
    return inverse * (scaled - normed * jnp.mean(scaled * normed, axis=-1, keepdims=True))


def silu_parts(gate_pre):
    sigmoid = jax.nn.sigmoid(gate_pre)
    return sigmoid, gate_pre * sigmoid


def halves(value, count):
    part = value.shape[1] // count
    return [value[:, i * part : (i + 1) * part] for i in range(count)]


def crossed(by_x, by_y):
    half = by_x[0].shape[0] // 2
    upper = [[rotated(v[:half], "x", i) for i in range(1, len(by_x))] for v in by_y[1:]]
    lower = [[rotated(v[half:], "y", k) for v in by_x[1:]] for k in range(1, len(by_y))]
    return upper, lower


def quarters(by_x, by_y, upper, lower):
    far = [[jnp.concatenate(v, axis=0) for v in zip(*rows)] for rows in zip(upper, lower)]
    return [by_x] + [[by_y[k], *far[k - 1]] for k in range(1, len(by_y))]


def matmul(left, right):
    return jnp.dot(left, right, preferred_element_type=jnp.float32)


def matmul_turned(left, right):
    return nt_dot(left, right)


def turned_matmul(left, right):
    return lax.dot_general(
        left, right, (((0,), (0,)), ((), ())), preferred_element_type=jnp.float32
    )


def sent_groups(value):
    size = lax.axis_size("y")
    place = lax.axis_index("y")
    width = value.shape[1] // size
    pieces = []
    for k in range(size):
        start = lax.rem(place + k, size) * width
        piece = lax.dynamic_slice_in_dim(value, start, width, 1)
        pieces.append(rotated(piece, "y", k) if k else piece)
    return pieces


def in_groups(pieces):
    size = len(pieces)
    place = lax.axis_index("y")
    return jnp.concatenate(
        [
            lax.select_n(place, *[pieces[(j - i) % size] for i in range(size)])
            for j in range(size)
        ],
        axis=1,
    )


def in_order(pieces):
    return natural_pieces(pieces, "y")


def turned_sum_kernel(blocks, cosine, sine, out):
    total = sum(blocks[i, 0].astype(jnp.float32) for i in range(blocks.shape[0]))
    cos, sin = key_tables(cosine[...], sine[...])
    out[...] = turned(total.T, cos, sin, -1.0).astype(jnp.bfloat16)


def turned_sum(blocks, cosine, sine):
    terms, segs, lanes, seg = blocks.shape
    table = pl.BlockSpec((seg, lanes), lambda s: (s, 0))
    return pl.pallas_call(
        turned_sum_kernel,
        grid=(segs,),
        in_specs=[pl.BlockSpec((terms, 1, lanes, seg), lambda s: (0, s, 0, 0)), table, table],
        out_specs=table,
        out_shape=jax.ShapeDtypeStruct((segs * seg, lanes), jnp.bfloat16),
        compiler_params=pltpu.CompilerParams(vmem_limit_bytes=KERNEL_VMEM),
        cost_estimate=SMALL_COST,
    )(blocks, cosine, sine)


def gathered_core(x_pieces):
    rows = jnp.stack(natural_pieces(x_pieces, "x"))
    rows = jnp.stack(natural_pieces(relative_pieces(rows, "c"), "c"), axis=1)
    return rows.reshape(-1, rows.shape[-1])


def own_first(value, axis):
    size = value.shape[0]
    place = lax.axis_index(axis)
    return [
        lax.dynamic_index_in_dim(value, lax.rem(place - k + size, size), 0, keepdims=False)
        for k in range(size)
    ]


def core_sum(part, rows):
    blocks = part.reshape(lax.axis_size("x"), lax.axis_size("c"), rows, -1)
    return summed_pieces(own_first(blocks.transpose(1, 0, 2, 3), "c"), "c").astype(jnp.bfloat16)


def x_blocks(value):
    return own_first(value, "x")


def tensor_sum(part, rows):
    return summed_pieces(x_blocks(core_sum(part, rows)), "x")


def local(
    tokens,
    norm_gain,
    q_weight,
    key_matrix,
    value_matrix,
    o_weight,
    mlp_gain,
    gate_weight,
    up_weight,
    down_weight,
    parents,
    out_grad,
):
    z_size, y_size, x_size = (lax.axis_size(name) for name in ("z", "y", "x"))
    tensor_size = x_size * lax.axis_size("c")
    low = jnp.bfloat16
    local_rows, width = tokens.shape
    group_rows = local_rows * tensor_size
    kv_cols = key_matrix.shape[1]
    kv_local = kv_cols // HEAD_SIZE
    q_cols = q_weight.shape[1]
    own_width = norm_gain.shape[0]

    own_tokens = relative_columns(tokens)
    own_grad = relative_columns(out_grad).astype(jnp.float32)
    both_gains = jnp.concatenate([norm_gain, mlp_gain])
    both_gains = jnp.pad(both_gains, (0, -both_gains.shape[0] % (2 * kv_cols)))
    key_heads, value_heads = halves(key_matrix, kv_local), halves(value_matrix, kv_local)
    kv_shard = jnp.concatenate(
        [
            jnp.concatenate([v for kv in zip(key_heads, value_heads) for v in kv], axis=1),
            both_gains.reshape(-1, 2 * kv_cols),
        ],
        axis=0,
    )
    kv_copies = jnp.broadcast_to(kv_shard[None], (z_size, *kv_shard.shape))
    kv_copies, q_weight = together(kv_copies, q_weight)
    kv_z = exchanged(kv_copies, "z")
    q_z = lax.all_gather(q_weight, "z", axis=0, tiled=True)
    group_tokens = gathered_core(relative_pieces(own_tokens, "x"))
    kv_z, o_weight = together(kv_z, o_weight)
    o_z = lax.all_gather(o_weight, "z", axis=0)

    depth = segment_depth(parents)
    seg_count = group_rows // SEG
    z_place, y_place = lax.axis_index("z"), lax.axis_index("y")
    sources = [lax.rem(y_place - k + y_size, y_size) for k in range(y_size)]
    segs = jnp.concatenate(
        [
            (z_place * y_size + source) * seg_count + jnp.arange(seg_count, dtype=jnp.int32)
            for source in sources
        ]
    )
    seg_ids = jnp.arange(depth.shape[0], dtype=jnp.int32)
    seg_depth = jnp.sum(jnp.where(segs[:, None] == seg_ids[None, :], depth[None, :], 0), axis=1)
    position = (seg_depth[:, None] * SEG + jnp.arange(SEG, dtype=jnp.int32)[None, :]).reshape(-1)
    cosine_table, sine_table = rope_tables(position, HEAD_SIZE)
    cosine_lanes = jnp.tile(cosine_table, (1, 4))
    sine_lanes = jnp.tile(sine_table, (1, 4))
    ordered = [jnp.concatenate(in_order(jnp.split(v, y_size))) for v in (cosine_lanes, sine_lanes)]
    cosine_lanes, sine_lanes, *ordered = settled(cosine_lanes, sine_lanes, *ordered)

    kv_zy = relative_pieces(kv_z, "y")
    kv_zy, cosine_lanes, sine_lanes, ordered = together(kv_zy, cosine_lanes, sine_lanes, ordered)
    kv_weights = [v[:, :own_width].reshape(-1, 2 * kv_cols) for v in kv_zy]
    gains = [
        v[:, own_width:].reshape(z_size, -1)[:, : 2 * own_width].reshape(z_size, 2, own_width)
        for v in kv_zy
    ]
    gains = jnp.stack(gains).astype(jnp.float32)
    gain_one, gain_two = gains[:, :, 0].reshape(-1), gains[:, :, 1].reshape(-1)
    inputs = own_tokens.astype(jnp.float32)
    normed_one, inv_one = row_norm(inputs)
    group_normed, _ = row_norm(group_tokens.astype(jnp.float32))
    rows_one = (group_normed * gain_one).astype(low)
    rows_one, q_z = together(rows_one, q_z)
    q_weights = relative_pieces(q_z, "y")
    kv_rows = project(rows_one, kv_weights, cosine_lanes, sine_lanes, keys=True)
    kv_swapped = jnp.stack(natural_pieces(sent_groups(kv_rows), "y"))
    all_kv = gathered(kv_swapped, "z").reshape(-1, SEG, LANES)
    wide_blocks = split_columns(after((gate_weight, up_weight), kv_z), z_size)
    q_weights, wide_blocks = together(q_weights, wide_blocks)
    query_rows = project(rows_one, q_weights, cosine_lanes, sine_lanes)
    queries = sent_groups(query_rows)
    all_kv, queries, o_z, wide_blocks = together(all_kv, queries, o_z, wide_blocks)

    wide_z = exchanged(wide_blocks, "z")
    o_weights = relative_pieces(o_z, "y")
    seg_lists = jnp.split(segs, y_size)
    attends, lows = [None] * y_size, [None] * y_size
    for k in range(y_size - 1, 0, -1):
        *attends[k], lows[k] = attend(parents, seg_lists[k], queries[k], all_kv)
    queries[0], attends[1:], lows[1:] = together(queries[0], attends[1:], lows[1:])
    returned = [rotated(v, "y", -k) for k, v in enumerate(lows[1:], 1)]
    *attends[0], lows[0] = attend(parents, seg_lists[0], queries[0], all_kv)
    attn_pieces = [lows[0], *returned]
    attn_pieces, o_weights = together(attn_pieces, o_weights)
    attn_part = o_forward(attn_pieces, o_weights, y_place)
    attn_low = in_groups(attn_pieces)
    attn_core = core_sum(attn_part, local_rows)
    attn_core, wide_z = together(attn_core, wide_z)

    gate_z, up_z = (wide_z[:, i].reshape(z_size * own_width, -1) for i in range(2))
    gate_zy, up_zy = relative_pieces(gate_z, "y"), relative_pieces(up_z, "y")
    gate_zx = relative_pieces(gate_z, "x")
    attn_mine = summed_pieces(x_blocks(attn_core), "x")
    attn_mine, up_z, down_weight = together(attn_mine, up_z, down_weight)

    middle = inputs + branch_scale * attn_mine
    normed_two, inv_two = row_norm(middle)
    hidden_two = (normed_two * gain_two).astype(low)
    rows_two = lax.all_gather(hidden_two, ("z", "c"), axis=0, tiled=True)
    down_z = exchanged(down_weight.reshape(z_size, -1, own_width), "z")
    gate_zx, gate_zy, up_z = together(gate_zx, gate_zy, up_z)
    gate_far = [relative_pieces(v, "y")[1:] for v in gate_zx[1:]]
    up_zx = relative_pieces(up_z, "x")
    grad_mlp = (branch_scale * own_grad).astype(low)
    up_zx, up_zy, grad_mlp, down_z = together(up_zx, up_zy, grad_mlp, down_z)
    grad_mlp_rows = lax.all_gather(grad_mlp, ("z", "c"), axis=0, tiled=True)
    up_crossed = crossed(up_zx, up_zy)
    rows_two, gate_far, up_crossed, down_z = together(rows_two, gate_far, up_crossed, down_z)
    down_zy, down_zx = relative_pieces(down_z, "y"), relative_pieces(down_z, "x")
    gates = [gate_zx] + [[gate_zy[k], *[v[k - 1] for v in gate_far]] for k in range(1, y_size)]
    ups = quarters(up_zx, up_zy, *up_crossed)
    activated, gate_slope, up_slope = gate_forward(rows_two, gates, ups)
    down_zy, down_zx, activated, gate_slope, up_slope = together(
        down_zy, down_zx, activated, gate_slope, up_slope
    )
    down_crossed = together(*crossed(down_zx, down_zy))
    downs = quarters(down_zx, down_zy, *down_crossed)
    mlp_part = down_forward(activated, downs)
    mlp_part, grad_mlp_rows = together(mlp_part, grad_mlp_rows)

    mlp_mine = lax.psum_scatter(mlp_part, ("z", "c"), scatter_dimension=0, tiled=True)
    grad_parts, rows_parts = halves(grad_mlp_rows, y_size), halves(rows_two, y_size)
    acts = halves(activated, x_size)
    down_far = [summed_pieces([turned_matmul(a, b) for a in grad_parts], "y").astype(low) for b in acts[1:]]
    grad_gate_act, grad_up_act = gate_backward(grad_mlp_rows, downs, gate_slope, up_slope)
    grad_gate_act, grad_up_act = together(grad_gate_act, grad_up_act)

    gate_parts, up_parts = halves(grad_gate_act, x_size), halves(grad_up_act, x_size)
    gate_dots = [[turned_matmul(a, b) for a in rows_parts] for b in gate_parts[1:]]
    up_dots = [[turned_matmul(a, b) for b in up_parts] for a in rows_parts[1:]]
    for dots in gate_dots + up_dots:
        dots[1:] = [v.astype(low) for v in dots[1:]]
    grad_gate_act, gate_dots, up_dots = together(grad_gate_act, gate_dots, up_dots)
    gate_far = [summed_pieces(v, "y").astype(low) for v in gate_dots]
    up_far = [summed_pieces(v, "x").astype(low) for v in up_dots]
    input_part = turned_product([grad_gate_act, grad_up_act], [gates, ups])
    input_part, down_far = together(input_part, down_far)

    grad_rows_two = lax.psum_scatter(input_part, ("z", "c"), scatter_dimension=0, tiled=True)
    gate_far, up_far, acts = together(gate_far, up_far, acts)
    down_near = summed_pieces([turned_matmul(a, acts[0]) for a in grad_parts], "y")
    down_far = [rotated(v, "x", -1 - i) for i, v in enumerate(down_far)]
    down_near, down_far, mlp_mine = together(down_near, down_far, mlp_mine)
    grad_down_z = sum([v.astype(jnp.float32) for v in down_far], down_near).astype(low)
    gate_near = summed_pieces([turned_matmul(a, gate_parts[0]) for a in rows_parts], "y")
    gate_far = [rotated(v, "x", -1 - i) for i, v in enumerate(gate_far)]
    up_near = [turned_matmul(rows_parts[0], b) for b in up_parts]
    up_near[1:] = [v.astype(low) for v in up_near[1:]]
    grad_rows_two, mlp_mine, up_far, up_near, grad_down_z = together(
        grad_rows_two, mlp_mine, up_far, up_near, grad_down_z
    )
    grad_rows_two = grad_rows_two.astype(jnp.float32)
    gain_two_part = jnp.sum(grad_rows_two * normed_two, axis=0)
    grad_middle = own_grad + norm_back(grad_rows_two, normed_two, inv_two, gain_two)
    grad_attn = (branch_scale * grad_middle).astype(low)
    attn_x = relative_pieces(grad_attn, "x")
    up_far = [rotated(v, "y", -1 - i) for i, v in enumerate(up_far)]
    grad_gate_z = sum([v.astype(jnp.float32) for v in gate_far], gate_near).astype(low)
    wide_z = jnp.stack([v.reshape(z_size, own_width, -1) for v in (grad_gate_z, grad_down_z)], 1)
    attn_x, wide_z, up_near = together(attn_x, wide_z, up_near)
    grad_attn_rows = gathered_core(attn_x)
    grad_heads = o_backward(grad_attn_rows, o_weights)
    grad_heads, grad_attn_rows, up_near, wide_z = together(
        grad_heads, grad_attn_rows, up_near, wide_z
    )
    wide_z = exchanged(wide_z, "z")

    grad_heads = sent_groups(grad_heads)
    o_dots = [turned_matmul(v, attn_low) for v in halves(grad_attn_rows, y_size)[1:]]
    o_dots = [v.astype(low) for v in o_dots]
    grad_heads, o_dots, up_near, grad_attn_rows = together(
        grad_heads, o_dots, up_near, grad_attn_rows
    )
    o_sent = [rotated(v, "y", -1 - i) for i, v in enumerate(o_dots)]
    up_mine = [rotated(v, "x", -1 - i) for i, v in enumerate(up_near[1:])]
    grad_queries, sums = [None] * y_size, None
    for k in range(y_size - 1, 0, -1):
        grad_queries[k], sums = attend_back(
            parents, seg_lists[k], queries[k], grad_heads[k], *attends[k], cosine_lanes,
            sine_lanes, k, all_kv, sums,
        )
    grad_o_y = turned_matmul(halves(grad_attn_rows, y_size)[0], attn_low)
    grad_o_y = sum([v.astype(jnp.float32) for v in o_sent], grad_o_y).astype(low)
    grad_queries[1:], sums, grad_o_y = together(grad_queries[1:], sums, grad_o_y)
    grad_o = lax.psum_scatter(grad_o_y, "z", scatter_dimension=0, tiled=True)
    returned = [rotated(v, "y", -k) for k, v in enumerate(grad_queries[1:], 1)]
    grad_queries[0], grad_kv = attend_back(
        parents, seg_lists[0], queries[0], grad_heads[0], *attends[0], cosine_lanes, sine_lanes,
        0, all_kv, sums,
    )
    grad_kv, wide_z = together(grad_kv, wide_z)
    grad_queries[0], returned, up_far, up_mine, up_near = after(
        (grad_queries[0], returned, up_far, up_mine, up_near), grad_kv
    )

    def owned_dots(left, right):
        dots = [turned_matmul(v, right) for v in halves(left, y_size)]
        return dots[:1] + [v.astype(low) for v in dots[1:]]

    def sent_back(dots):
        return [rotated(v, "y", -1 - i) for i, v in enumerate(dots[1:])]

    def total(own, sent):
        return sum([v.astype(jnp.float32) for v in sent], own).astype(low)

    kv_mine = exchanged(grad_kv.reshape(z_size, y_size * seg_count, LANES, SEG), "z")
    grad_queries = in_groups([grad_queries[0], *returned])
    query_dots = owned_dots(rows_one, grad_queries)
    query_sent = sent_back(query_dots)
    q_full = jnp.concatenate(q_weights, axis=0)
    query_part = matmul_turned(grad_queries, q_full)
    grad_up_z = total(up_near[0], up_far + up_mine)
    kv_mine, query_part, query_dots, query_sent, grad_up_z, grad_o = together(
        kv_mine, query_part, query_dots, query_sent, grad_up_z, grad_o
    )

    grad_up = exchanged(grad_up_z.reshape(z_size, own_width, -1), "z")
    kv_mine = turned_sum(kv_mine, *ordered).reshape(y_size, group_rows, LANES)
    kv_mine = own_first(kv_mine, "y")
    grad_kv_rows = in_groups(
        [kv_mine[0]] + [rotated(v, "y", -k) for k, v in enumerate(kv_mine[1:], 1)]
    )
    kv_full = jnp.concatenate(kv_weights, axis=0)
    input_one = (query_part + matmul_turned(grad_kv_rows, kv_full)).astype(low)
    input_core = core_sum(input_one, local_rows)
    grad_q_y = total(query_dots[0], query_sent)
    kv_dots = owned_dots(rows_one, grad_kv_rows)
    kv_sent = sent_back(kv_dots)
    input_core, grad_q_y, grad_up, wide_z, grad_o = together(
        input_core, grad_q_y, grad_up, wide_z, grad_o
    )
    grad_q = lax.psum_scatter(grad_q_y, "z", scatter_dimension=0, tiled=True)
    input_x = x_blocks(input_core)
    input_sent = [rotated(v, "x", -1 - i) for i, v in enumerate(input_x[1:])]
    grad_gate, grad_down, grad_up = finished(wide_z, grad_up)
    input_x[0], input_sent, kv_sent, kv_dots, grad_gate, grad_down, grad_up, grad_o = together(
        input_x[0], input_sent, kv_sent, kv_dots, grad_gate, grad_down, grad_up, grad_o
    )
    grad_rows_one = sum([v.astype(jnp.float32) for v in input_sent], input_x[0].astype(jnp.float32))
    kv_blocks = own_first(total(kv_dots[0], kv_sent).reshape(z_size, own_width, -1), "z")
    kv_sent = [rotated(v, "z", -1 - i) for i, v in enumerate(kv_blocks[1:])]
    gain_one_part = jnp.sum(grad_rows_one * normed_one, axis=0)
    grad_inputs = grad_middle + norm_back(grad_rows_one, normed_one, inv_one, gain_one)
    gain_parts = jnp.stack([gain_one_part, gain_two_part], axis=0)
    gain_parts = natural_columns(gain_parts).reshape(2, z_size * y_size, 1, own_width)
    gain_parts = jnp.broadcast_to(
        gain_parts, (2, z_size * y_size, tensor_size, own_width)
    ).reshape(2, -1, own_width).transpose(1, 0, 2)
    gain_parts, grad_inputs, mlp_mine = together(gain_parts, grad_inputs, mlp_mine)
    gain_parts = exchanged(gain_parts, ("z", "y", "x", "c"))
    mixed = natural_columns((middle + branch_scale * mlp_mine.astype(jnp.float32)).astype(low))
    grad_tokens = natural_columns(grad_inputs.astype(low))
    grad_o = after(grad_o, grad_inputs).astype(jnp.float32).T
    gain_parts, kv_sent, kv_blocks, grad_q, grad_o, grad_tokens, mixed = together(
        gain_parts, kv_sent, kv_blocks, grad_q.astype(jnp.float32), grad_o, grad_tokens, mixed
    )
    gain_sums = jnp.sum(gain_parts, axis=0)
    grad_kv_weight = sum([v.astype(jnp.float32) for v in kv_sent], kv_blocks[0].astype(jnp.float32))
    grad_heads = halves(grad_kv_weight, 2 * kv_local)
    return (
        mixed,
        grad_tokens,
        gain_sums[0],
        grad_q,
        jnp.concatenate(grad_heads[::2], axis=1),
        jnp.concatenate(grad_heads[1::2], axis=1),
        grad_o,
        gain_sums[1],
        grad_gate,
        grad_up,
        grad_down,
    )


def solution(mesh):
    dp_size, tensor_size = mesh.shape["dp"], mesh.shape["tensor"]
    fine = jax.sharding.Mesh(
        mesh.devices.reshape(dp_size // 2, 2, tensor_size // 2, 2), ("z", "y", "x", "c")
    )
    dp, tensor = ("z", "y"), ("x", "c")
    tokens = P(dp + tensor, None)
    rows = P(dp, tensor)
    columns = P(tensor, dp)
    in_specs = (
        tokens,
        P(dp),
        rows,
        rows,
        rows,
        columns,
        P(dp),
        rows,
        rows,
        columns,
        P(),
        tokens,
    )
    out_specs = (
        tokens,
        tokens,
        P(dp),
        rows,
        rows,
        rows,
        columns,
        P(dp),
        rows,
        rows,
        columns,
    )
    return jax.shard_map(local, mesh=fine, in_specs=in_specs, out_specs=out_specs, check_vma=False)
```
